32 devices in a mesh: dp: 2 (over x), ctx: 16 (over z, y, core).
Axes of the slice: x: 2, y: 2, z: 4, core: 2. Of those that a mesh axis runs over, the one named last changes fastest.
Arguments:
- tokens: bfloat16 [16384, 1024], P(('dp', 'ctx')), may hold values from -6 to 6
- grad_out: bfloat16 [16384, 1024], P(('dp', 'ctx')), may hold values from -6 to 6
- w_query: bfloat16 [1024, 1024], P(('dp', 'ctx')), may hold values from -0.1875 to 0.1875
- w_key: bfloat16 [1024, 512], P(('dp', 'ctx')), may hold values from -0.1875 to 0.1875
- w_value: bfloat16 [1024, 512], P(('dp', 'ctx')), may hold values from -0.1875 to 0.1875
- w_output: bfloat16 [1024, 1024], P(('dp', 'ctx')), may hold values from -6 to 6
- gain_attn: bfloat16 [1024], P(('dp', 'ctx')), may hold values from 0.5 to 1.5
- gain_ffn: bfloat16 [1024], P(('dp', 'ctx')), may hold values from 0.5 to 1.5
- w_router: bfloat16 [1024, 32], P(('dp', 'ctx')), may hold values from -0.09375 to 0.09375
- w_experts: bfloat16 [3, 1024, 16384], P(None, 'dp', 'ctx'), may hold values from -0.35546875 to 0.35546875
- deal_table: int32 [2, 32], P('dp'), may hold values from 0 to 31, as said below
- routes: int32 [16384, 8], P(('dp', 'ctx')), may hold values from 0 to 31, all different within a row; in each aligned block of 512 rows (0 to 511, 512 to 1023, ...) at most 160 rows name the same one
Outputs:
- mixed: bfloat16 [16384, 1024], P(('dp', 'ctx'))
- grad_tokens: float32 [16384, 1024], P(('dp', 'ctx'))
- grad_query: float32 [1024, 1024], P(('dp', 'ctx'))
- grad_key: float32 [1024, 512], P(('dp', 'ctx'))
- grad_value: float32 [1024, 512], P(('dp', 'ctx'))
- grad_output: float32 [1024, 1024], P(('dp', 'ctx'))
- grad_gain_attn: float32 [1024], P(('dp', 'ctx'))
- grad_gain_ffn: float32 [1024], P(('dp', 'ctx'))
- grad_router: float32 [1024, 32], P(('dp', 'ctx'))
- grad_experts: float32 [3, 1024, 16384], P(None, 'dp', 'ctx')
The draws below stay inside these ranges and needn't reach their ends.
Inputs may be any that keep to these rules, and one draw needn't show every extreme that they name: `deal_table`: entry s of row g is k * 16 + b for block b of sequence k of group g; each row holds every number once, and slots 2 c and 2 c + 1 hold blocks b and 15 - b of one sequence. `routes`: A token names 8 different experts. Among the rows of one device no expert is named by more than 160 rows, a bound that some block reaches.
All inputs are finite; a program needn't handle non-finite values.
Results may differ from the reference program's by a relative error of at most 0.028.
Values may be sent and summed in bfloat16 or wider, within the bound.
No kernel may reach another device: no remote copies, remote signals or barrier semaphores. Data moves between devices by JAX's collectives and lax.ppermute only.
A program may use at most 960 MiB of HBM per device.

```python
import math
from functools import partial
import jax
import jax.numpy as jnp
import numpy as np
from jax import lax

D = 1024
HQ = 16
KVH = 8
HD = 64
E = 32
F = 512
TOPK = 8
BLK = 256
BLOCKS = 16
CAP = 160
TOK_DEV = 512
SLOTS = 32
SEQS = 2
TOKENS = 16384
N_DP = 2


def draw_deal_table(key, part):
    key = jax.random.fold_in(key, 11)
    devices = SLOTS // 2
    pairs_per = BLOCKS // 2
    groups = TOKENS // (SLOTS * BLK)

    def one_group(group_key):
        order_key, seq_key, pair_key, flip_key = jax.random.split(group_key, 4)
        device = jnp.arange(devices, dtype=jnp.int32)
        score = jax.random.permutation(order_key, devices).astype(jnp.int32)
        score = jnp.where(device == 0, -3, score)
        score = jnp.where(device == devices // 2, -2, score)
        score = jnp.where(device == devices - 1, -1, score)
        rank = jnp.argsort(jnp.argsort(score, stable=True), stable=True).astype(jnp.int32)
        seq_order = jax.random.permutation(seq_key, SEQS).astype(jnp.int32)
        pair_table = jax.vmap(lambda k: jax.random.permutation(k, pairs_per))(jax.random.split(pair_key, SEQS)).astype(jnp.int32)
        group_rank = rank // pairs_per
        sequence = seq_order[group_rank]
        pair_index = pair_table[group_rank, rank % pairs_per]
        flipped = jax.random.randint(flip_key, (devices,), 0, 2)
        lower = pair_index
        upper = BLOCKS - 1 - pair_index
        leading = jnp.where(flipped == 1, upper, lower)
        trailing = jnp.where(flipped == 1, lower, upper)
        return (jnp.stack([leading, trailing], axis=1) + sequence[:, None] * BLOCKS).reshape(-1).astype(jnp.int32)
    return jax.vmap(one_group)(jax.random.split(key, groups))


def level_of(stream_key, shape, cuts, low, top_value):
    level, own = 1.0, jax.random.fold_in(stream_key, 6)
    for position, blocks in cuts:
        draws = jnp.exp(jax.random.uniform(jax.random.fold_in(own, position), (blocks,), jnp.float32, low / len(cuts), top_value / len(cuts)))
        level = level * jnp.repeat(draws, shape[position] // blocks).reshape([-1 if axis == position else 1 for axis in range(len(shape))])
    return level


def assign_block(key, own, number, rows, number_of, top, most, slope):
    ranking = jax.random.permutation(key, number_of)
    crowded, ordinary = load_shares(number_of, rows * top, most, slope, True), load_shares(number_of, rows * top, most, slope, False)
    places = jnp.arange(number_of)

    def named(sizes, turn):
        used = int((sizes > 0).sum())
        fixed = max(1, used // 4)
        moved = fixed + (places - fixed + turn * (used - fixed)) % max(1, number_of - fixed)
        return jnp.zeros((number_of,), jnp.int32).at[ranking[jnp.where(places < fixed, places, moved)]].set(jnp.asarray(sizes, jnp.int32))

    sizes = jnp.where(number % 4 == 0, named(crowded, number // 4), named(ordinary, number - number // 4 - 1))
    mixed = jax.random.permutation(jax.random.fold_in(own, 3), number_of)
    giver, sink = mixed[0:number_of // 2 * 2:2], mixed[1:number_of // 2 * 2:2]
    margin = jnp.minimum(sizes[giver] - 1, most - sizes[sink]) // 2
    margin = jnp.where((giver == ranking[0]) | (sink == ranking[0]) | (sizes[sink] == 0), 0, jnp.maximum(margin, 0))
    moved = jax.random.randint(jax.random.fold_in(own, 4), (number_of // 2,), 0, 1 << 20) % (margin + 1)
    sizes = sizes.at[giver].add(-moved).at[sink].add(moved)
    items = jnp.searchsorted(jnp.cumsum(sizes), jnp.arange(rows * top), side="right").astype(jnp.int32)
    listing = items.reshape(top, rows).T
    listing = listing[jax.random.permutation(jax.random.fold_in(own, 1), rows)]
    turn = jax.random.randint(jax.random.fold_in(own, 2), (rows, 1), 0, top)
    return jnp.take_along_axis(listing, (jnp.arange(top)[None, :] + turn) % top, axis=1)


def load_shares(number_of, total, most, lean, full):
    weights = [(1 << 20) // math.isqrt(grade ** lean) + 1 for grade in range(1, number_of + 1)]
    largest = most if full else min(most, max(-(-total // number_of), total * weights[0] // sum(weights)))
    least = 1 if total - largest >= number_of - 1 else 0
    counts, surplus = [largest] + [least] * (number_of - 1), total - largest - least * (number_of - 1)
    while surplus > 0:
        candidates = [i for i in range(1, number_of) if counts[i] < largest] or [i for i in range(1, number_of) if counts[i] < most]
        pool, left = sum([weights[i] for i in candidates]), surplus
        for i in candidates:
            addition = min(most - counts[i], max(1, left * weights[i] // pool), surplus)
            counts[i] = counts[i] + addition
            surplus = surplus - addition
    return np.array(counts)


def centred(rng, dims, scale, reach, pieces=(), held_as=jnp.bfloat16):
    level = level_of(rng, dims, pieces, -0.22, 0.18) if pieces else 1.0
    values = jax.random.normal(rng, dims, jnp.float32) * scale * level
    return jnp.minimum(jnp.maximum(values, -reach), reach).astype(held_as)


def setup_inputs(seed: int = 0) -> dict:
    streams_of = jax.random.split(jax.random.key(seed), 13)
    tokens = centred(streams_of[0], (TOKENS, D), 1.0, 6.0, ((0, 32),))
    grad_out = centred(streams_of[1], (TOKENS, D), 1.0, 6.0, ((0, 32),))
    w_query = centred(streams_of[2], (D, HQ * HD), D ** -0.5, 0.1875, ((0, 32),))
    w_key = centred(streams_of[3], (D, KVH * HD), D ** -0.5, 0.1875, ((0, 32),))
    w_value = centred(streams_of[4], (D, KVH * HD), D ** -0.5, 0.1875, ((0, 32),))
    w_output = centred(streams_of[5], (HQ * HD, D), (max(1, HQ * HD // 1024)) ** -0.5, 6.0, ((0, 32),))
    gain_attn = jnp.clip(1.0 + 0.1 * jax.random.normal(streams_of[6], (D,), jnp.float32), 0.5, 1.5).astype(jnp.bfloat16)
    gain_ffn = jnp.clip(1.0 + 0.1 * jax.random.normal(streams_of[7], (D,), jnp.float32), 0.5, 1.5).astype(jnp.bfloat16)
    w_router = centred(streams_of[8], (D, E), (0.5 / (D ** 0.5)), 0.09375, ((0, 32),))
    w_experts = centred(streams_of[9], (3, D, E * F), (1.9 / (D ** 0.5)), 0.35546875, ((1, 2), (2, 16)))
    deal_table = draw_deal_table(jax.random.fold_in(streams_of[12], 71), 0)
    routes_keys = jax.random.split(jax.random.fold_in(streams_of[11], 1), TOKENS // TOK_DEV)
    routes_turns = jax.random.permutation(jax.random.fold_in(streams_of[11], 3), TOKENS // TOK_DEV)
    routes = jax.vmap(lambda own, number: assign_block(jax.random.fold_in(streams_of[11], 2), own, number, TOK_DEV, E, TOPK, CAP, 1))(routes_keys, routes_turns).reshape((TOKENS, TOPK))
    return {"tokens": tokens, "grad_out": grad_out, "w_query": w_query, "w_key": w_key, "w_value": w_value, "w_output": w_output, "gain_attn": gain_attn, "gain_ffn": gain_ffn, "w_router": w_router, "w_experts": w_experts, "deal_table": deal_table, "routes": routes}


@jax.custom_vjp
def low(v):
    return lax.optimization_barrier(v.astype(jnp.bfloat16)).astype(jnp.float32)

@jax.custom_vjp
def low_back(v):
    return v

def low_keep(v):
    return (low(v), None)

def low_pass(kept, grad):
    return (grad,)

def back_keep(v):
    return (v, None)

def back_low(kept, grad):
    return (low(grad),)
low.defvjp(low_keep, low_pass)
low_back.defvjp(back_keep, back_low)
epsilon = 1e-06
highest = lax.Precision.HIGHEST

def rms_norm(values, gain):
    return values * lax.rsqrt(lax.optimization_barrier(jnp.mean(values * values, axis=-1, keepdims=True)) + epsilon) * gain

def rotary(values, positions):
    half_size = values.shape[-1] // 2
    frequency = 10000.0 ** (-(jnp.arange(half_size).astype(jnp.float32) * 2.0 / values.shape[-1]))
    angles = positions.astype(jnp.float32)[:, None] * frequency[None, :]
    cosine = jnp.cos(angles)[:, None, :]
    sine_part = jnp.sin(angles)[:, None, :]
    first_half = values[..., :half_size]
    second = values[..., half_size:]
    return jnp.concatenate([first_half * cosine - second * sine_part, second * cosine + first_half * sine_part], axis=-1)

def layer_forward(tokens, w_query, w_key, w_value, w_output, gain_attn, gain_ffn, w_router, w_experts, deal_table, routes):
    row_count = tokens.shape[0]
    group_span = SLOTS * BLK
    head_ratio = HQ // KVH
    row_index = jnp.arange(row_count, dtype=jnp.int32)
    block_ids = deal_table[row_index // group_span, row_index % group_span // BLK]
    positions = block_ids % BLOCKS * BLK + row_index % BLK
    normed = low(rms_norm(tokens, gain_attn))
    queries = low(rotary(low_back(jnp.dot(normed, w_query, precision=highest)).reshape(row_count, HQ, HD), positions))
    key_proj = low(rotary(low_back(jnp.dot(normed, w_key, precision=highest)).reshape(row_count, KVH, HD), positions))
    value_proj = low(low_back(jnp.dot(normed, w_value, precision=highest))).reshape(row_count, KVH, HD)
    keys_grouped = key_proj.reshape(N_DP, group_span, KVH, HD)
    values_grouped = value_proj.reshape(N_DP, group_span, KVH, HD)
    ids_grouped = block_ids.reshape(N_DP, group_span)

    def attend(entries):
        query_block, query_ids, number = entries
        group_index = number * TOK_DEV // group_span
        key_rows = keys_grouped[group_index]
        value_rows = values_grouped[group_index]
        key_ids = ids_grouped[group_index]
        grouped = query_block.reshape(TOK_DEV, KVH, head_ratio, HD)
        scores = low_back(jnp.einsum('qgrd,kgd->grqk', grouped, key_rows, precision=highest) * HD ** (-0.5))
        permitted = (key_ids[None, :] <= query_ids[:, None]) & (key_ids[None, :] // BLOCKS == query_ids[:, None] // BLOCKS)
        scores = jnp.where(permitted[None, None], scores, -1e+30)
        weights = jax.nn.softmax(scores, axis=-1)
        mixed_values = jnp.einsum('grqk,kgd->qgrd', low(weights), value_rows, precision=highest)
        return mixed_values.reshape(TOK_DEV, HQ * HD)
    count_blocks = row_count // TOK_DEV
    attended = lax.map(jax.checkpoint(attend), (queries.reshape(count_blocks, TOK_DEV, HQ, HD), block_ids.reshape(count_blocks, TOK_DEV), jnp.arange(count_blocks, dtype=jnp.int32)))
    attended = low(low_back(attended.reshape(row_count, HQ * HD)))
    residual = tokens + low_back(jnp.dot(attended, w_output, precision=highest))
    normed_ffn = low(rms_norm(residual, gain_ffn))
    logits = jnp.dot(normed_ffn, w_router, precision=highest)
    picked = (routes[:, :, None] == jnp.arange(E, dtype=jnp.int32)[None, None, :]).astype(jnp.float32)
    chosen = lax.optimization_barrier(jnp.sum(picked * logits[:, None, :], axis=2))
    gate_weights = jax.nn.softmax(chosen, axis=-1)
    spread = lax.optimization_barrier(jnp.sum(gate_weights[:, :, None] * picked, axis=1))
    stacked = w_experts.reshape(3, D, E, F).transpose(0, 2, 1, 3)

    def expert_block(entries):
        block_rows, block_gates = entries

        def one_expert(running, expert):
            gate_w, up_w, down_w, column = expert
            gate_pre = low_back(jnp.dot(block_rows, gate_w, precision=highest))
            up_pre = low_back(jnp.dot(block_rows, up_w, precision=highest))
            hidden = low(jax.nn.silu(gate_pre) * up_pre)
            output = low_back(jnp.dot(hidden, down_w.T, precision=highest))
            return (running + column[:, None] * output, None)
        running, _ = lax.scan(one_expert, jnp.zeros(block_rows.shape, jnp.float32), (stacked[0], stacked[1], stacked[2], block_gates.T))
        return running
    mixture = lax.map(jax.checkpoint(expert_block), (normed_ffn.reshape(count_blocks, TOK_DEV, D), spread.reshape(count_blocks, TOK_DEV, E)))
    return residual + mixture.reshape(row_count, D)

def reference(tokens, grad_out, w_query, w_key, w_value, w_output, gain_attn, gain_ffn, w_router, w_experts, deal_table, routes):
    floats = [a.astype(jnp.float32) for a in (tokens, w_query, w_key, w_value, w_output, gain_attn, gain_ffn, w_router, w_experts)]
    result, pullback = jax.vjp(partial(layer_forward, deal_table=deal_table, routes=routes), *floats)
    gradients = pullback(grad_out.astype(jnp.float32))
    return (result.astype(jnp.bfloat16), gradients[0], gradients[1], gradients[2], gradients[3], gradients[4], gradients[5], gradients[6], gradients[7], gradients[8])
```

```python
from functools import partial

import jax
import jax.numpy as jnp
from jax import lax
from jax.experimental import pallas as pl
from jax.experimental.pallas import tpu as pltpu
from jax.sharding import PartitionSpec as P

D = 1024
HQ = 16
KVH = 8
HD = 64
E = 32
F = 512
TOPK = 8
BLK = 256
BLOCKS = 16
CAP = 160


epsilon = 1e-06
highest = lax.Precision.HIGHEST
floor_value = -1e30


def rms_norm(values, gain):
    return values * lax.rsqrt(jnp.mean(values * values, axis=-1, keepdims=True) + epsilon) * gain


def rotary(values, positions):
    half_size = values.shape[-1] // 2
    frequency = 10000.0 ** (-(jnp.arange(half_size).astype(jnp.float32) * 2.0 / values.shape[-1]))
    angles = positions.astype(jnp.float32)[:, None] * frequency[None, :]
    cosine = jnp.cos(angles)[:, None, :]
    sine_part = jnp.sin(angles)[:, None, :]
    first_half = values[..., :half_size]
    second = values[..., half_size:]
    return jnp.concatenate(
        [first_half * cosine - second * sine_part, second * cosine + first_half * sine_part],
        axis=-1,
    )


def heads_major(block_rows, groups, head_ratio, head_size):
    count = block_rows.shape[0]
    shaped = block_rows.reshape(count, groups, head_ratio, head_size).transpose(1, 2, 0, 3)
    return shaped.reshape(groups, head_ratio * count, head_size)


def rows_major(blocked, groups, head_ratio, head_size):
    count = blocked.shape[1] // head_ratio
    shaped = blocked.reshape(groups, head_ratio, count, head_size).transpose(2, 0, 1, 3)
    return shaped.reshape(count, groups * head_ratio * head_size)


def stats_major(block_rows, groups, head_ratio):
    count = block_rows.shape[0]
    return (
        block_rows.reshape(count, groups, head_ratio)
        .transpose(1, 2, 0)
        .reshape(groups, head_ratio * count)
    )


def pair_blocks(rows, base, groups, head_ratio, head_size):
    return jnp.stack(
        [
            heads_major(lax.dynamic_slice_in_dim(rows, base + i * BLK, BLK), groups, head_ratio, head_size)
            for i in range(2)
        ]
    )


def pair_order(block_pair, per_seq):
    places = block_pair % per_seq
    lower_slot = (places[0] > places[1]).astype(jnp.int32)
    return (lower_slot, 1 - lower_slot, jnp.minimum(places[0], places[1]), block_pair[0] // per_seq)


def keep_state(carry_state):
    return carry_state


def forward_update(query_block, key_block, value_block, slot_number, score_scale):

    def forward_apply_update(carry_state):
        running_max, running_sum, accumulated = carry_state
        scores = (
            jnp.einsum("gqd,gkd->gqk", query_block, key_block, preferred_element_type=jnp.float32)
            * score_scale
        )
        new_max = jnp.maximum(running_max[slot_number], jnp.max(scores, axis=-1))
        factor = jnp.exp(running_max[slot_number] - new_max)
        weights = jnp.exp(scores - new_max[..., None])
        new_sum = running_sum[slot_number] * factor + jnp.sum(weights, axis=-1)
        product = jnp.einsum(
            "gqk,gkd->gqd",
            weights.astype(jnp.bfloat16),
            value_block,
            preferred_element_type=jnp.float32,
        )
        new_acc = accumulated[slot_number] * factor[..., None] + product
        return (
            running_max.at[slot_number].set(new_max),
            running_sum.at[slot_number].set(new_sum),
            accumulated.at[slot_number].set(new_acc),
        )

    return forward_apply_update


def query_update(
    query_block,
    grad_block,
    log_block,
    delta_block,
    key_block,
    value_block,
    slot_number,
    score_scale,
):

    def query_apply_update(accumulated):
        scores = (
            jnp.einsum("gqd,gkd->gqk", query_block, key_block, preferred_element_type=jnp.float32)
            * score_scale
        )
        probs_full = jnp.exp(scores - log_block[..., None])
        prob_grad = jnp.einsum(
            "gqd,gkd->gqk", grad_block, value_block, preferred_element_type=jnp.float32
        )
        score_grad = (probs_full * (prob_grad - delta_block[..., None])).astype(jnp.bfloat16)
        change = (
            jnp.einsum("gqk,gkd->gqd", score_grad, key_block, preferred_element_type=jnp.float32)
            * score_scale
        )
        return accumulated.at[slot_number].add(change)

    return query_apply_update


def key_update(
    query_block,
    grad_block,
    log_block,
    delta_block,
    key_block,
    value_block,
    slot_number,
    score_scale,
):

    def key_apply_update(carry_state):
        key_accum, value_accum = carry_state
        scores = (
            jnp.einsum("gqd,gkd->gqk", query_block, key_block, preferred_element_type=jnp.float32)
            * score_scale
        )
        probs_full = jnp.exp(scores - log_block[..., None])
        value_change = jnp.einsum(
            "gqk,gqd->gkd",
            probs_full.astype(jnp.bfloat16),
            grad_block,
            preferred_element_type=jnp.float32,
        )
        prob_grad = jnp.einsum(
            "gqd,gkd->gqk", grad_block, value_block, preferred_element_type=jnp.float32
        )
        score_grad = (probs_full * (prob_grad - delta_block[..., None])).astype(jnp.bfloat16)
        key_change = (
            jnp.einsum("gqk,gqd->gkd", score_grad, query_block, preferred_element_type=jnp.float32)
            * score_scale
        )
        return (
            key_accum.at[slot_number].add(key_change),
            value_accum.at[slot_number].add(value_change),
        )

    return key_apply_update


def expert_forward(routed_rows, weights_local):
    gate_pre = jnp.einsum(
        "erd,def->erf", routed_rows, weights_local[0], preferred_element_type=jnp.float32
    )
    up_pre = jnp.einsum(
        "erd,def->erf", routed_rows, weights_local[1], preferred_element_type=jnp.float32
    )
    hidden = (jax.nn.silu(gate_pre) * up_pre).astype(jnp.bfloat16)
    return (gate_pre, up_pre, hidden)


def natural_return(partials, split_count):
    devices = partials.shape[0]
    arrived = lax.all_to_all(partials, "ctx", split_axis=0, concat_axis=0, tiled=True)
    shaped = arrived.reshape(
        devices * partials.shape[1] // split_count,
        split_count,
        partials.shape[2],
        partials.shape[3],
    )
    return jnp.sum(shaped, axis=1)


def send_back(partials, split_count):
    return natural_return(partials, split_count)


def spread_slots(slot_values, devices, local_count, split_count):
    width = slot_values.shape[-1]
    return jnp.broadcast_to(
        slot_values.reshape(E, 1, CAP, width), (E, split_count, CAP, width)
    ).reshape(devices, local_count, CAP, width)


def general_device(
    tokens,
    grad_out,
    w_query,
    w_key,
    w_value,
    w_output,
    gain_attn,
    gain_ffn,
    w_router,
    w_experts,
    deal_table,
    routes,
):
    row_count = tokens.shape[0]
    head_ratio = HQ // KVH
    score_scale = HD ** (-0.5)
    full_query, full_key, full_value, full_output, full_router, full_gain_attn, full_gain_ffn = (
        lax.all_gather(w_query, ("dp", "ctx"), axis=0, tiled=True),
        lax.all_gather(w_key, ("dp", "ctx"), axis=0, tiled=True),
        lax.all_gather(w_value, ("dp", "ctx"), axis=0, tiled=True),
        lax.all_gather(w_output, ("dp", "ctx"), axis=0, tiled=True),
        lax.all_gather(w_router, ("dp", "ctx"), axis=0, tiled=True),
        lax.all_gather(gain_attn, ("dp", "ctx"), axis=0, tiled=True),
        lax.all_gather(gain_ffn, ("dp", "ctx"), axis=0, tiled=True),
    )
    experts_local = lax.all_gather(w_experts, "dp", axis=1, tiled=True)
    columns = experts_local.shape[2]
    unit_width = min(F, columns)
    local_count = columns // unit_width
    split_count = F // unit_width
    devices = lax.axis_size("ctx")
    position = lax.axis_index("ctx")
    group_blocks = deal_table[0]
    per_seq = BLOCKS
    own_blocks = lax.dynamic_slice_in_dim(group_blocks, 2 * position, 2)
    query_low, query_high, low_place, own_seq = pair_order(own_blocks, per_seq)
    offsets = jnp.arange(BLK, dtype=jnp.int32)
    positions = ((own_blocks % per_seq)[:, None] * BLK + offsets[None, :]).reshape(-1)
    inputs = tokens.astype(jnp.float32)
    gain_attn_full = full_gain_attn.astype(jnp.float32)
    gain_ffn_full = full_gain_ffn.astype(jnp.float32)
    normed = rms_norm(inputs, gain_attn_full).astype(jnp.bfloat16)
    query_raw = jnp.dot(normed, full_query, preferred_element_type=jnp.float32).reshape(
        row_count, HQ, HD
    )
    key_raw = jnp.dot(normed, full_key, preferred_element_type=jnp.float32).reshape(
        row_count, KVH, HD
    )
    value_raw = jnp.dot(normed, full_value, preferred_element_type=jnp.float32)
    queries = rotary(query_raw, positions).astype(jnp.bfloat16).reshape(row_count, HQ * HD)
    key_proj = rotary(key_raw, positions).astype(jnp.bfloat16).reshape(row_count, KVH * HD)
    value_proj = value_raw.astype(jnp.bfloat16)
    query_heads = pair_blocks(queries, 0, KVH, head_ratio, HD)
    key_heads = pair_blocks(key_proj, 0, KVH, 1, HD)
    value_heads = pair_blocks(value_proj, 0, KVH, 1, HD)
    score_rows = head_ratio * BLK
    initial = (
        jnp.full((2, KVH, score_rows), floor_value, jnp.float32),
        jnp.zeros((2, KVH, score_rows), jnp.float32),
        jnp.zeros((2, KVH, score_rows, HD), jnp.float32),
    )
    initial = forward_update(
        query_heads[query_low], key_heads[query_low], value_heads[query_low], query_low, score_scale
    )(initial)
    carry_state = initial
    key_rows = lax.all_gather(key_proj, "ctx", axis=0, tiled=True)
    value_rows = lax.all_gather(value_proj, "ctx", axis=0, tiled=True)
    def forward_step(j, carry_state):
        key_pair = pair_blocks(key_rows, j * 2 * BLK, KVH, 1, HD)
        value_pair = pair_blocks(value_rows, j * 2 * BLK, KVH, 1, HD)
        block_pair = lax.dynamic_slice_in_dim(group_blocks, 2 * j, 2)
        key_low, key_high, key_place, key_seq = pair_order(block_pair, per_seq)
        same = key_seq == own_seq
        carry_state = lax.cond(
            same,
            forward_update(
                query_heads[query_high],
                key_pair[key_low],
                value_pair[key_low],
                query_high,
                score_scale,
            ),
            keep_state,
            carry_state,
        )
        below = key_place < low_place
        pick_query = jnp.where(below, query_low, query_high)
        pick_key = jnp.where(below, key_low, key_high)
        carry_state = lax.cond(
            same,
            forward_update(
                query_heads[pick_query],
                key_pair[pick_key],
                value_pair[pick_key],
                pick_query,
                score_scale,
            ),
            keep_state,
            carry_state,
        )
        return carry_state

    carry_state = lax.fori_loop(0, key_rows.shape[0] // (2 * BLK), forward_step, carry_state)
    running_max, running_sum, accumulated = carry_state
    attended_heads = accumulated / running_sum[..., None]
    log_total = running_max + jnp.log(running_sum)
    attended_rows = jnp.concatenate(
        [rows_major(attended_heads[i], KVH, head_ratio, HD) for i in range(2)], axis=0
    )
    attended_low = attended_rows.astype(jnp.bfloat16)
    residual = inputs + jnp.dot(attended_low, full_output, preferred_element_type=jnp.float32)
    normed_ffn = rms_norm(residual, gain_ffn_full).astype(jnp.bfloat16)
    expert_ids = jnp.arange(E, dtype=jnp.int32)
    picked = routes[:, :, None] == expert_ids[None, None, :]
    ffn_float = normed_ffn.astype(jnp.float32)
    router_full = full_router.astype(jnp.float32)
    logits = jnp.dot(ffn_float, router_full, precision=highest)
    chosen = jnp.sum(jnp.where(picked, logits[:, None, :], 0.0), axis=2)
    gate_weights = jax.nn.softmax(chosen, axis=-1)
    member = jnp.sum(picked.astype(jnp.int32), axis=1)
    before = jnp.cumsum(member, axis=0) - member
    slot_numbers = jnp.sum(jnp.where(picked, before[:, None, :], 0), axis=2)
    flat_slot = (routes * CAP + slot_numbers).reshape(-1)
    owner_rows = (
        jnp.zeros((E * CAP,), jnp.int32)
        .at[flat_slot]
        .set(jnp.repeat(jnp.arange(1, row_count + 1, dtype=jnp.int32), TOPK))
    )
    slot_gate = jnp.zeros((E * CAP,), jnp.float32).at[flat_slot].set(gate_weights.reshape(-1))
    padded_rows = jnp.concatenate([jnp.zeros((1, D), jnp.bfloat16), normed_ffn], axis=0)
    slot_rows = padded_rows[owner_rows]
    outgoing = spread_slots(slot_rows, devices, local_count, split_count)
    arrived = lax.all_to_all(outgoing, "ctx", split_axis=0, concat_axis=0, tiled=True)
    routed_rows = arrived.transpose(1, 0, 2, 3).reshape(local_count, devices * outgoing.shape[2], D)
    weights_local = experts_local.reshape(3, D, local_count, unit_width)
    gate_pre, up_pre, hidden = expert_forward(routed_rows, weights_local)
    expert_out = jnp.einsum(
        "erf,def->erd", hidden, weights_local[2], preferred_element_type=jnp.float32
    )
    combined = send_back(
        expert_out.reshape(local_count, devices, outgoing.shape[2], D).transpose(1, 0, 2, 3),
        split_count,
    )
    routed_out = combined.reshape(E * CAP, D)[flat_slot].reshape(row_count, TOPK, D)
    mixed = (residual + jnp.sum(gate_weights[:, :, None] * routed_out, axis=1)).astype(jnp.bfloat16)
    upstream = grad_out.astype(jnp.float32)
    gate_grad = jnp.sum(routed_out * upstream[:, None, :], axis=2)
    chosen_grad = gate_weights * (
        gate_grad - jnp.sum(gate_weights * gate_grad, axis=1, keepdims=True)
    )
    logits_grad = jnp.sum(jnp.where(picked, chosen_grad[:, :, None], 0.0), axis=1)
    padded_grad = jnp.concatenate([jnp.zeros((1, D), jnp.float32), upstream], axis=0)
    slot_grad = (padded_grad[owner_rows] * slot_gate[:, None]).astype(jnp.bfloat16)
    outgoing_grad = spread_slots(slot_grad, devices, local_count, split_count)
    arrived_grad = lax.all_to_all(outgoing_grad, "ctx", split_axis=0, concat_axis=0, tiled=True)
    grad_rows = arrived_grad.transpose(1, 0, 2, 3).reshape(
        local_count, devices * outgoing.shape[2], D
    )
    hidden_grad = jnp.einsum(
        "erd,def->erf", grad_rows, weights_local[2], preferred_element_type=jnp.float32
    )
    sigmoid = jax.nn.sigmoid(gate_pre)
    up_grad = (hidden_grad * gate_pre * sigmoid).astype(jnp.bfloat16)
    gate_pre_grad = (hidden_grad * up_pre * sigmoid * (1.0 + gate_pre * (1.0 - sigmoid))).astype(
        jnp.bfloat16
    )
    weight_grad = jnp.stack(
        [
            jnp.einsum(
                "erd,erf->def", routed_rows, gate_pre_grad, preferred_element_type=jnp.float32
            ),
            jnp.einsum("erd,erf->def", routed_rows, up_grad, preferred_element_type=jnp.float32),
            jnp.einsum("erd,erf->def", grad_rows, hidden, preferred_element_type=jnp.float32),
        ]
    ).reshape(3, D, local_count * unit_width)
    input_grad = jnp.einsum(
        "erf,def->erd", gate_pre_grad, weights_local[0], preferred_element_type=jnp.float32
    )
    input_grad = input_grad + jnp.einsum(
        "erf,def->erd", up_grad, weights_local[1], preferred_element_type=jnp.float32
    )
    returned = send_back(
        input_grad.reshape(local_count, devices, outgoing.shape[2], D).transpose(1, 0, 2, 3),
        split_count,
    )
    ffn_grad = jnp.sum(returned.reshape(E * CAP, D)[flat_slot].reshape(row_count, TOPK, D), axis=1)
    ffn_grad = ffn_grad + jnp.einsum("re,de->rd", logits_grad, router_full, precision=highest)
    router_grad = jnp.einsum("rd,re->de", ffn_float, logits_grad, precision=highest)
    expert_grad = lax.psum_scatter(weight_grad, "dp", scatter_dimension=1, tiled=True)
    _, norm_back_ffn = jax.vjp(rms_norm, residual, gain_ffn_full)
    residual_norm_grad, gain_ffn_grad = norm_back_ffn(ffn_grad)
    residual_grad = upstream + residual_norm_grad
    branch_grad = residual_grad.astype(jnp.bfloat16)
    output_grad = jnp.einsum(
        "rc,rd->cd", attended_low, branch_grad, preferred_element_type=jnp.float32
    )
    attended_grad = jnp.einsum(
        "rd,cd->rc", branch_grad, full_output, preferred_element_type=jnp.float32
    ).astype(jnp.bfloat16)
    delta_rows = jnp.sum(
        (attended_grad.astype(jnp.float32) * attended_rows).reshape(row_count, HQ, HD), axis=-1
    )
    delta_heads = jnp.stack(
        [stats_major(delta_rows[i * BLK : (i + 1) * BLK], KVH, head_ratio) for i in range(2)]
    )
    grad_heads = pair_blocks(attended_grad, 0, KVH, head_ratio, HD)
    all_log, all_delta = (
        lax.all_gather(log_total, "ctx", axis=0, tiled=True),
        lax.all_gather(delta_heads, "ctx", axis=0, tiled=True),
    )
    query_start = query_update(
        query_heads[query_low],
        grad_heads[query_low],
        log_total[query_low],
        delta_heads[query_low],
        key_heads[query_low],
        value_heads[query_low],
        query_low,
        score_scale,
    )(jnp.zeros((2, KVH, score_rows, HD), jnp.float32))
    accumulated_grad = query_start
    key_rows = lax.all_gather(key_proj, "ctx", axis=0, tiled=True)
    value_rows = lax.all_gather(value_proj, "ctx", axis=0, tiled=True)
    def query_step(j, accumulated_grad):
        key_pair = pair_blocks(key_rows, j * 2 * BLK, KVH, 1, HD)
        value_pair = pair_blocks(value_rows, j * 2 * BLK, KVH, 1, HD)
        block_pair = lax.dynamic_slice_in_dim(group_blocks, 2 * j, 2)
        key_low, key_high, key_place, key_seq = pair_order(block_pair, per_seq)
        same = key_seq == own_seq
        first = query_update(
            query_heads[query_high],
            grad_heads[query_high],
            log_total[query_high],
            delta_heads[query_high],
            key_pair[key_low],
            value_pair[key_low],
            query_high,
            score_scale,
        )
        accumulated_grad = lax.cond(same, first, keep_state, accumulated_grad)
        below = key_place < low_place
        pick_query = jnp.where(below, query_low, query_high)
        pick_key = jnp.where(below, key_low, key_high)
        second_update = query_update(
            query_heads[pick_query],
            grad_heads[pick_query],
            log_total[pick_query],
            delta_heads[pick_query],
            key_pair[pick_key],
            value_pair[pick_key],
            pick_query,
            score_scale,
        )
        accumulated_grad = lax.cond(same, second_update, keep_state, accumulated_grad)
        return accumulated_grad

    accumulated_grad = lax.fori_loop(0, key_rows.shape[0] // (2 * BLK), query_step, accumulated_grad)
    zero_keys = jnp.zeros((2, KVH, BLK, HD), jnp.float32)
    key_start = key_update(
        query_heads[query_low],
        grad_heads[query_low],
        log_total[query_low],
        delta_heads[query_low],
        key_heads[query_low],
        value_heads[query_low],
        query_low,
        score_scale,
    )((zero_keys, zero_keys))
    carry_state = key_start
    start_row = jnp.int32(0)
    query_rows = lax.all_gather(queries, "ctx", axis=0, tiled=True)
    grad_piece = lax.all_gather(attended_grad, "ctx", axis=0, tiled=True)
    def key_step(j, carry_state):
        slot_first = start_row // BLK + 2 * j
        query_pair = pair_blocks(query_rows, j * 2 * BLK, KVH, head_ratio, HD)
        grad_pair = pair_blocks(grad_piece, j * 2 * BLK, KVH, head_ratio, HD)
        block_pair = lax.dynamic_slice_in_dim(group_blocks, slot_first, 2)
        log_pair = lax.dynamic_slice_in_dim(all_log, slot_first, 2)
        delta_pair = lax.dynamic_slice_in_dim(all_delta, slot_first, 2)
        remote_low, remote_high, remote_place, remote_seq = pair_order(block_pair, per_seq)
        same = remote_seq == own_seq
        first = key_update(
            query_pair[remote_high],
            grad_pair[remote_high],
            log_pair[remote_high],
            delta_pair[remote_high],
            key_heads[query_low],
            value_heads[query_low],
            query_low,
            score_scale,
        )
        carry_state = lax.cond(same, first, keep_state, carry_state)
        below = low_place < remote_place
        pick_remote = jnp.where(below, remote_low, remote_high)
        pick_own = jnp.where(below, query_low, query_high)
        second_update = key_update(
            query_pair[pick_remote],
            grad_pair[pick_remote],
            log_pair[pick_remote],
            delta_pair[pick_remote],
            key_heads[pick_own],
            value_heads[pick_own],
            pick_own,
            score_scale,
        )
        carry_state = lax.cond(same, second_update, keep_state, carry_state)
        return carry_state

    carry_state = lax.fori_loop(0, query_rows.shape[0] // (2 * BLK), key_step, carry_state)
    key_grad_heads, value_grad_heads = carry_state
    query_grad_rows = jnp.concatenate(
        [rows_major(accumulated_grad[i], KVH, head_ratio, HD) for i in range(2)], axis=0
    )
    key_grad_rows = jnp.concatenate(
        [rows_major(key_grad_heads[i], KVH, 1, HD) for i in range(2)], axis=0
    )
    value_grad_rows = jnp.concatenate(
        [rows_major(value_grad_heads[i], KVH, 1, HD) for i in range(2)], axis=0
    )
    _, query_rot_back = jax.vjp(partial(rotary, positions=positions), query_raw)
    _, key_rot_back = jax.vjp(partial(rotary, positions=positions), key_raw)
    query_proj_grad = (
        query_rot_back(query_grad_rows.reshape(row_count, HQ, HD))[0]
        .reshape(row_count, HQ * HD)
        .astype(jnp.bfloat16)
    )
    key_proj_grad = (
        key_rot_back(key_grad_rows.reshape(row_count, KVH, HD))[0]
        .reshape(row_count, KVH * HD)
        .astype(jnp.bfloat16)
    )
    value_proj_grad = value_grad_rows.astype(jnp.bfloat16)
    query_weight_grad = jnp.einsum(
        "rd,rc->dc", normed, query_proj_grad, preferred_element_type=jnp.float32
    )
    key_weight_grad = jnp.einsum(
        "rd,rc->dc", normed, key_proj_grad, preferred_element_type=jnp.float32
    )
    value_weight_grad = jnp.einsum(
        "rd,rc->dc", normed, value_proj_grad, preferred_element_type=jnp.float32
    )
    normed_grad = jnp.einsum(
        "rc,dc->rd", query_proj_grad, full_query, preferred_element_type=jnp.float32
    )
    normed_grad = normed_grad + jnp.einsum(
        "rc,dc->rd", key_proj_grad, full_key, preferred_element_type=jnp.float32
    )
    normed_grad = normed_grad + jnp.einsum(
        "rc,dc->rd", value_proj_grad, full_value, preferred_element_type=jnp.float32
    )
    _, norm_back_attn = jax.vjp(rms_norm, inputs, gain_attn_full)
    input_norm_grad, gain_attn_grad = norm_back_attn(normed_grad)
    tokens_grad = residual_grad + input_norm_grad
    owned = (
        lax.psum_scatter(query_weight_grad, ("dp", "ctx"), scatter_dimension=0, tiled=True),
        lax.psum_scatter(key_weight_grad, ("dp", "ctx"), scatter_dimension=0, tiled=True),
        lax.psum_scatter(value_weight_grad, ("dp", "ctx"), scatter_dimension=0, tiled=True),
        lax.psum_scatter(output_grad, ("dp", "ctx"), scatter_dimension=0, tiled=True),
        lax.psum_scatter(router_grad, ("dp", "ctx"), scatter_dimension=0, tiled=True),
        lax.psum_scatter(gain_attn_grad, ("dp", "ctx"), scatter_dimension=0, tiled=True),
        lax.psum_scatter(gain_ffn_grad, ("dp", "ctx"), scatter_dimension=0, tiled=True),
    )
    return (
        mixed,
        tokens_grad,
        owned[0],
        owned[1],
        owned[2],
        owned[3],
        owned[5],
        owned[6],
        owned[4],
        expert_grad,
    )


TILE = 512
VMEM_BYTES = 60 * 1024 * 1024
CHANNELS = 3 * HD


def nn(a, b):
    return jnp.dot(a, b, preferred_element_type=jnp.float32)


def nt(a, b):
    return lax.dot_general(a, b, (((1,), (1,)), ((), ())), preferred_element_type=jnp.float32)


def tn(a, b):
    return lax.dot_general(a, b, (((0,), (0,)), ((), ())), preferred_element_type=jnp.float32)


def tt(a, b):
    return lax.dot_general(a, b, (((0,), (1,)), ((), ())), preferred_element_type=jnp.float32)


def attention_forward_kernel(seq, table, packed, *refs):
    out, out_rows, log_sum, q_seq, k_seq, v_seq = refs[-6:]
    if seq > 0:
        out[...] = refs[0][...]
    seq_rows = BLOCKS * BLK
    for g in range(BLOCKS):
        slot = table[seq * BLOCKS + g]
        lanes = pl.ds(pl.multiple_of((slot % 2) * BLK, BLK), BLK)
        here = slice(g * BLK, (g + 1) * BLK)
        source = packed.at[slot // 2]
        q_seq[:, here] = source[0:HD, lanes] * jnp.bfloat16(HD**-0.5)
        k_seq[here, :] = source[HD : 2 * HD, lanes].astype(jnp.float32).T.astype(jnp.bfloat16)
        v_seq[:, here] = source[2 * HD : 3 * HD, lanes]

    def update(q, state, start, size):
        top, total, acc = state
        rows = pl.ds(start, size)
        scores = nn(k_seq[rows, :], q)
        new_top = jnp.maximum(top, jnp.max(scores, axis=0, keepdims=True))
        factor = jnp.exp(top - new_top)
        weights = jnp.exp(scores - new_top)
        total = total * factor + jnp.sum(weights, axis=0, keepdims=True)
        acc = acc * factor + nn(v_seq[:, rows], weights.astype(jnp.bfloat16))
        return new_top, total, acc

    def one_tile(n, carry):
        mine = pl.multiple_of(n * TILE, TILE)
        q = q_seq[:, pl.ds(mine, TILE)]
        state = (
            jnp.full((1, TILE), floor_value, jnp.float32),
            jnp.zeros((1, TILE), jnp.float32),
            jnp.zeros((HD, TILE), jnp.float32),
        )
        state = lax.fori_loop(
            0,
            n,
            lambda k, c: update(q, c, pl.multiple_of(k * TILE, TILE), TILE),
            state,
        )
        state = update(q, state, mine, BLK)
        late = update(q[:, BLK:], tuple(s[:, BLK:] for s in state), mine + BLK, BLK)
        top, total, acc = (
            jnp.concatenate([s[:, :BLK], t], axis=1) for s, t in zip(state, late)
        )
        final = acc / total
        out_rows[:, pl.ds(mine, TILE)] = final
        log_sum[:, pl.ds(mine, TILE)] = top + jnp.log(total)
        return carry

    lax.fori_loop(0, seq_rows // TILE, one_tile, 0)
    for g in range(BLOCKS):
        slot = table[seq * BLOCKS + g]
        lanes = pl.ds(pl.multiple_of((slot % 2) * BLK, BLK), BLK)
        out[slot // 2, :, lanes] = out_rows[:, g * BLK : (g + 1) * BLK].astype(jnp.bfloat16)


def attention_backward_kernel(
    table, packed, d_out, out_rows_0, out_rows_1, log_sum, grads, q_seq, k_cols, v_cols, k_seq, v_seq, d_seq,
    delta, dq, dk, dv
):
    block_count = 2 * packed.shape[0]
    seq_rows = BLOCKS * BLK
    for g in range(block_count):
        slot = table[g]
        lanes = pl.ds(pl.multiple_of((slot % 2) * BLK, BLK), BLK)
        here = slice(g * BLK, (g + 1) * BLK)
        source = packed.at[slot // 2]
        q_seq[:, here] = source[0:HD, lanes] * jnp.bfloat16(HD**-0.5)
        k_block = source[HD : 2 * HD, lanes]
        v_block = source[2 * HD : 3 * HD, lanes]
        k_cols[:, here] = k_block
        k_seq[here, :] = k_block.astype(jnp.float32).T.astype(jnp.bfloat16)
        v_seq[here, :] = v_block.astype(jnp.float32).T.astype(jnp.bfloat16)
        d_block = d_out[slot // 2, :, lanes]
        d_seq[:, here] = d_block
        delta[:, here] = jnp.sum(
            d_block.astype(jnp.float32)
            * (out_rows_0, out_rows_1)[g // BLOCKS][
                :, g % BLOCKS * BLK : (g % BLOCKS + 1) * BLK
            ],
            axis=0,
            keepdims=True,
        )
    dq[...] = jnp.zeros_like(dq)

    def pair(k_start, k_size, q_start, q_size, first):
        keys = pl.ds(k_start, k_size)
        cols = pl.ds(q_start, q_size)
        q = q_seq[:, cols]
        d = d_seq[:, cols]
        probs = jnp.exp(nn(k_seq[keys, :], q) - log_sum[:, cols])
        d_scores = (probs * (nn(v_seq[keys, :], d) - delta[:, cols])).astype(jnp.bfloat16)
        new_v = nt(d, probs.astype(jnp.bfloat16))
        new_k = nt(q, d_scores)
        if first:
            dv[:, keys] = new_v
            dk[:, keys] = new_k
        else:
            dv[:, keys] += new_v
            dk[:, keys] += new_k
        dq[:, cols] += nn(k_cols[:, keys], d_scores)

    def one_tile(n, carry):
        per_seq = seq_rows // TILE
        mine = pl.multiple_of(n * TILE, TILE)
        last = (n // per_seq + 1) * per_seq
        pair(mine, BLK, mine, TILE, True)
        pair(mine + BLK, BLK, mine + BLK, BLK, True)

        def step(t, c):
            pair(mine, TILE, pl.multiple_of(t * TILE, TILE), TILE, False)
            return c

        lax.fori_loop(n + 1, last, step, 0)
        return carry

    lax.fori_loop(0, 2 * seq_rows // TILE, one_tile, 0)
    for g in range(block_count):
        slot = table[g]
        lanes = pl.ds(pl.multiple_of((slot % 2) * BLK, BLK), BLK)
        here = slice(g * BLK, (g + 1) * BLK)
        grads[slot // 2, 0:HD, lanes] = (dq[:, here] * HD**-0.5).astype(jnp.bfloat16)
        grads[slot // 2, HD : 2 * HD, lanes] = dk[:, here].astype(jnp.bfloat16)
        grads[slot // 2, 2 * HD : 3 * HD, lanes] = dv[:, here].astype(jnp.bfloat16)


def work(microseconds):
    return int(microseconds * 1.15e9)


def params():
    return pltpu.CompilerParams(vmem_limit_bytes=VMEM_BYTES)


def attention_forward(seq, table, packed, *kept):
    count, _, row_count = packed.shape
    total = BLOCKS * BLK
    whole = pl.BlockSpec(memory_space=pltpu.VMEM)
    return pl.pallas_call(
        partial(attention_forward_kernel, seq),
        out_shape=(
            jax.ShapeDtypeStruct((count, HD, row_count), jnp.bfloat16),
            jax.ShapeDtypeStruct((HD, total), jnp.float32),
            jax.ShapeDtypeStruct((1, total), jnp.float32),
        ),
        in_specs=[pl.BlockSpec(memory_space=pltpu.SMEM), whole] + [whole] * len(kept),
        out_specs=(whole,) * 3,
        scratch_shapes=[
            pltpu.VMEM((HD, total), jnp.bfloat16),
            pltpu.VMEM((total, HD), jnp.bfloat16),
            pltpu.VMEM((HD, total), jnp.bfloat16),
        ],
        compiler_params=params(),
        cost_estimate=pl.CostEstimate(
            flops=work(27), bytes_accessed=packed.size * 2, transcendentals=total * total // 2
        ),
        name="attention_forward",
    )(table, packed, *kept)


def attention_backward(table, packed, d_out, out_rows_0, out_rows_1, log_sum):
    count, _, row_count = packed.shape
    total = count * row_count
    pairs = total * BLOCKS * BLK // 2
    return pl.pallas_call(
        attention_backward_kernel,
        out_shape=jax.ShapeDtypeStruct(packed.shape, jnp.bfloat16),
        in_specs=[pl.BlockSpec(memory_space=pltpu.SMEM)]
        + [pl.BlockSpec(memory_space=pltpu.VMEM)] * 5,
        out_specs=pl.BlockSpec(memory_space=pltpu.VMEM),
        scratch_shapes=[
            pltpu.VMEM((HD, total), jnp.bfloat16),
            pltpu.VMEM((HD, total), jnp.bfloat16),
            pltpu.VMEM((HD, total), jnp.bfloat16),
            pltpu.VMEM((total, HD), jnp.bfloat16),
            pltpu.VMEM((total, HD), jnp.bfloat16),
            pltpu.VMEM((HD, total), jnp.bfloat16),
            pltpu.VMEM((1, total), jnp.float32),
            pltpu.VMEM((HD, total), jnp.float32),
            pltpu.VMEM((HD, total), jnp.float32),
            pltpu.VMEM((HD, total), jnp.float32),
        ],
        compiler_params=params(),
        cost_estimate=pl.CostEstimate(
            flops=work(61), bytes_accessed=packed.size * 6, transcendentals=pairs
        ),
        name="attention_backward",
    )(table, packed, d_out, out_rows_0, out_rows_1, log_sum)


def slot_match(places, rows):
    numbers = lax.broadcasted_iota(jnp.int32, (rows, places.shape[1]), 0).astype(jnp.float32)
    return numbers == places


def column_match(places, columns):
    numbers = lax.broadcasted_iota(jnp.int32, (places.shape[0], columns), 1).astype(jnp.float32)
    return jnp.where(numbers == places, 1.0, 0.0).astype(jnp.bfloat16)


def grad_kernel(count, order, places, *refs):
    sources, weights = refs[:count], refs[count]
    slot_rows, d_hidden, rows = refs[-3:]
    g = pl.program_id(0)
    for k, source in enumerate(sources):

        @pl.when(g == k)
        def _(source=source):
            rows[...] = source[...]

    for e in range(places.shape[1]):
        pick = jnp.where(slot_match(places[0, e : e + 1, :], CAP), 1.0, 0.0).astype(jnp.bfloat16)
        picked = nn(pick, rows[...]).astype(jnp.bfloat16)
        slot_rows[e] = picked
        d_hidden[e] = nn(picked, weights[0, :, e * F : (e + 1) * F]).astype(jnp.bfloat16)


def grad_step(first, order, places, blocks, weights, kept):
    devices, local, row_count = places.shape
    count = len(blocks)
    kept = () if kept is None else tuple(kept)
    block = pl.BlockSpec((row_count, D), lambda g, order: (0, 0))
    return pl.pallas_call(
        partial(grad_kernel, count),
        grid_spec=pltpu.PrefetchScalarGridSpec(
            num_scalar_prefetch=1,
            grid=(count,),
            in_specs=[
                pl.BlockSpec((1, local, row_count), lambda g, order: (order[g], 0, 0)),
                *([block] * count),
                pl.BlockSpec((1, D, local * F), lambda g, order: (2, 0, 0)),
            ]
            + [pl.BlockSpec(memory_space=pl.ANY)] * len(kept),
            out_specs=(
                pl.BlockSpec((local, CAP, D), lambda g, order: (0, first + g, 0)),
                pl.BlockSpec((local, CAP, F), lambda g, order: (0, first + g, 0)),
            ),
            scratch_shapes=[pltpu.VMEM((row_count, D), jnp.bfloat16)],
        ),
        out_shape=(
            jax.ShapeDtypeStruct((local, devices * CAP, D), jnp.bfloat16),
            jax.ShapeDtypeStruct((local, devices * CAP, F), jnp.bfloat16),
        ),
        input_output_aliases={count + 3 + i: i for i in range(len(kept))},
        compiler_params=params(),
        cost_estimate=pl.CostEstimate(
            flops=work(2 * count + 2), bytes_accessed=count * row_count * D * 4, transcendentals=0
        ),
        name="grad_step",
    )(order, places, *blocks, weights, *kept)


def expert_kernel(count, order, places, columns, gates, *refs):
    sources, (d_hidden, weights) = refs[:count], refs[count : count + 2]
    slot_rows, hidden, d_gate_pre, d_up, d_gate, near, far, rows = refs[-8:]
    g = pl.program_id(0)
    for k, source in enumerate(sources):

        @pl.when(g == k)
        def _(source=source):
            rows[...] = source[...]

    total = None
    for e in range(places.shape[1]):
        here = slice(e * F, (e + 1) * F)
        match = slot_match(places[0, e : e + 1, :], CAP)
        pick = jnp.where(match, 1.0, 0.0)
        picked = nn(pick.astype(jnp.bfloat16), rows[...]).astype(jnp.bfloat16)
        slot_rows[e] = picked
        gate_pre = nn(picked, weights[0, :, here])
        up_pre = nn(picked, weights[1, :, here])
        gate = jnp.sum(jnp.where(match, gates[0, e : e + 1, :], 0.0), axis=1, keepdims=True)
        raw = d_hidden[e].astype(jnp.float32)
        sig = 1.0 / (1.0 + jnp.exp(-gate_pre))
        silu = gate_pre * sig
        value = silu * up_pre
        hidden[e] = (gate * value).astype(jnp.bfloat16)
        scaled = raw * gate
        up_grad = (scaled * silu).astype(jnp.bfloat16)
        pre_grad = (scaled * up_pre * sig * (1.0 + gate_pre * (1.0 - sig))).astype(jnp.bfloat16)
        d_up[e] = up_grad
        d_gate_pre[e] = pre_grad
        slot_gate = jnp.sum(raw * value, axis=1, keepdims=True)
        d_gate[0, e : e + 1, :] = jnp.sum(pick * slot_gate, axis=0, keepdims=True)
        back = (nt(pre_grad, weights[0, :, here]) + nt(up_grad, weights[1, :, here])).astype(
            jnp.bfloat16
        )
        spread = nn(column_match(columns[0, :, e : e + 1], CAP), back)
        total = spread if total is None else total + spread
    result = total.astype(jnp.bfloat16)

    @pl.when(g < count // 2)
    def _():
        near[0] = result

    @pl.when(g >= count // 2)
    def _():
        far[0] = result


def expert_step(first, order, places, columns, gates, blocks, d_hidden, weights, kept):
    devices, local, row_count = places.shape
    count = len(blocks)
    wide_slots = pl.BlockSpec((local, CAP, D), lambda g, order: (0, first + g, 0))
    slots = pl.BlockSpec((local, CAP, F), lambda g, order: (0, first + g, 0))
    block = pl.BlockSpec((row_count, D), lambda g, order: (0, 0))
    kept = () if kept is None else tuple(kept)
    first_kept = 6 + count
    half = count // 2
    return pl.pallas_call(
        partial(expert_kernel, count),
        grid_spec=pltpu.PrefetchScalarGridSpec(
            num_scalar_prefetch=1,
            grid=(count,),
            in_specs=[
                pl.BlockSpec((1, local, row_count), lambda g, order: (order[g], 0, 0)),
                pl.BlockSpec((1, row_count, local), lambda g, order: (order[g], 0, 0)),
                pl.BlockSpec((1, local, row_count), lambda g, order: (order[g], 0, 0)),
                *([block] * count),
                slots,
                pl.BlockSpec((2, D, local * F), lambda g, order: (0, 0, 0)),
            ]
            + [pl.BlockSpec(memory_space=pl.ANY)] * len(kept),
            out_specs=(
                wide_slots,
                slots,
                slots,
                slots,
                pl.BlockSpec((1, local, row_count), lambda g, order: (g, 0, 0)),
                pl.BlockSpec((1, row_count, D), lambda g, order: (jnp.minimum(g, half - 1), 0, 0)),
                pl.BlockSpec((1, row_count, D), lambda g, order: (jnp.maximum(g - half, 0), 0, 0)),
            ),
            scratch_shapes=[pltpu.VMEM((row_count, D), jnp.bfloat16)],
        ),
        out_shape=(
            jax.ShapeDtypeStruct((local, devices * CAP, D), jnp.bfloat16),
            jax.ShapeDtypeStruct((local, devices * CAP, F), jnp.bfloat16),
            jax.ShapeDtypeStruct((local, devices * CAP, F), jnp.bfloat16),
            jax.ShapeDtypeStruct((local, devices * CAP, F), jnp.bfloat16),
            jax.ShapeDtypeStruct((count, local, row_count), jnp.float32),
            jax.ShapeDtypeStruct((half, row_count, D), jnp.bfloat16),
            jax.ShapeDtypeStruct((half, row_count, D), jnp.bfloat16),
        ),
        input_output_aliases={first_kept + i: i for i in range(len(kept))},
        compiler_params=params(),
        cost_estimate=pl.CostEstimate(
            flops=work(5 * count),
            bytes_accessed=count * row_count * D * 6,
            transcendentals=count * local * CAP * F,
        ),
        name="expert_step",
    )(order, places, columns, gates, *blocks, d_hidden, weights, *kept)


def output_kernel(order, columns, hidden, weights, out_rows):
    total = None
    for e in range(columns.shape[2]):
        out = nt(hidden[e], weights[0, :, e * F : (e + 1) * F]).astype(jnp.bfloat16)
        spread = nn(column_match(columns[0, :, e : e + 1], CAP), out)
        total = spread if total is None else total + spread
    out_rows[...] = total.astype(jnp.bfloat16)


def output_pass(order, columns, hidden, weights):
    devices, row_count, local = columns.shape
    return pl.pallas_call(
        output_kernel,
        grid_spec=pltpu.PrefetchScalarGridSpec(
            num_scalar_prefetch=1,
            grid=(devices,),
            in_specs=[
                pl.BlockSpec((1, row_count, local), lambda j, order: (order[j], 0, 0)),
                pl.BlockSpec((local, CAP, F), lambda j, order: (0, j, 0)),
                pl.BlockSpec((1, D, local * F), lambda j, order: (2, 0, 0)),
            ],
            out_specs=pl.BlockSpec((row_count, D), lambda j, order: (order[j], 0)),
        ),
        out_shape=jax.ShapeDtypeStruct((devices * row_count, D), jnp.bfloat16),
        compiler_params=params(),
        cost_estimate=pl.CostEstimate(
            flops=work(26), bytes_accessed=devices * row_count * D * 3,
            transcendentals=0,
        ),
        name="output_pass",
    )(order, columns, hidden, weights)


def weight_grad_kernel(half, slot_rows, slot_grads, d_gate_pre, d_up, hidden, *out):
    out[0][...] = tn(slot_rows[0], d_gate_pre[0]).astype(out[0].dtype)
    out[1][...] = tn(slot_rows[0], d_up[0]).astype(out[1].dtype)
    out[2][...] = tn(slot_grads[0], hidden[0]).astype(out[2].dtype)


def weight_grad(half, slot_rows, slot_grads, d_gate_pre, d_up, hidden, dtype):
    local, count, _ = hidden.shape
    wide_slots = pl.BlockSpec((1, count, D // 2), lambda e, half: (e, 0, half[0]))
    slots = pl.BlockSpec((1, count, F), lambda e, half: (e, 0, 0))
    return pl.pallas_call(
        weight_grad_kernel,
        grid_spec=pltpu.PrefetchScalarGridSpec(
            num_scalar_prefetch=1,
            grid=(local,),
            in_specs=[wide_slots, wide_slots, slots, slots, slots],
            out_specs=(pl.BlockSpec((D // 2, F), lambda e, half: (0, e)),) * 3,
        ),
        out_shape=(jax.ShapeDtypeStruct((D // 2, local * F), dtype),) * 3,
        compiler_params=params(),
        cost_estimate=pl.CostEstimate(
            flops=work(15), bytes_accessed=local * count * D * 8, transcendentals=0
        ),
        name="weight_grad",
    )(half, slot_rows, slot_grads, d_gate_pre, d_up, hidden)


LINE = 4
ROWS = 2
CORES = 2
together = lax.optimization_barrier


def place(z, y, c):
    return (z * ROWS + y) * CORES + c


def move(values, target):
    pairs = []
    for z in range(LINE):
        for y in range(ROWS):
            for c in range(CORES):
                there = target(z, y, c)
                if there is not None and 0 <= there[0] < LINE:
                    pairs.append((place(z, y, c), place(*there)))
    return lax.ppermute(values, "ctx", pairs)


def core_swap(values):
    return move(values, lambda z, y, c: (z, y, 1 - c))


def row_swap(values):
    return move(values, lambda z, y, c: (z, 1 - y, c))


def up_from(values, sources):
    return move(values, lambda z, y, c: (z + 1, y, c) if z in sources else None)


def down_from(values, sources):
    return move(values, lambda z, y, c: (z - 1, y, c) if z in sources else None)


def added(*terms):
    total = terms[0].astype(jnp.float32)
    for term in terms[1:]:
        total = total + term.astype(jnp.float32)
    return total.astype(jnp.bfloat16)


LINE_ORDER = ((0, 1, 2, 3), (1, 2, 3, 0), (2, 1, 0, 3), (3, 2, 1, 0))


def send_on(s, own, up, down):
    sent = []
    if s < LINE:
        sent.append(row_swap(own))
    if s < LINE - 1:
        sent.append(up_from(up, tuple(range(s, LINE - 1))))
        sent.append(down_from(down, tuple(range(1, LINE - s))))
    return sent


def newest(s, ups, downs, z):
    if s < LINE - 1:
        return jnp.where(z >= 2, ups[s], downs[s])
    return jnp.where(
        z == 0, downs[3], jnp.where(z == 1, ups[1], jnp.where(z == 2, downs[1], ups[3]))
    )


def near_order(position):
    z = position // (ROWS * CORES)
    y = position // CORES % ROWS
    c = position % CORES
    line = jnp.asarray(LINE_ORDER, jnp.int32)[z]
    steps = []
    for s in range(LINE + 1):
        for other_core in range(CORES):
            if s < LINE:
                steps.append(place(line[s], y, c ^ other_core))
            if s > 0:
                steps.append(place(line[s - 1], 1 - y, c ^ other_core))
    return jnp.stack(steps).astype(jnp.int32)


def scatter_sum(near, far, z):
    summed = [added(a, core_swap(b)) for a, b in zip(reversed(near), reversed(far))][::-1]
    part_3 = added(summed[3][0], row_swap(summed[4][0]))
    up_3 = up_from(part_3, (0,))
    down_3 = down_from(part_3, (3,))
    across_2 = row_swap(summed[3][1])
    up_3, down_3, across_2 = together((up_3, down_3, across_2))
    part_2 = added(summed[2][0], across_2)
    up_2 = up_from(added(part_2, up_3), (0, 1))
    down_2 = down_from(added(part_2, down_3), (3, 2))
    across_1 = row_swap(summed[2][1])
    up_2, down_2, across_1 = together((up_2, down_2, across_1))
    part_1 = added(summed[1][0], across_1)
    up_1 = up_from(added(jnp.where(z == 2, part_3, part_1), up_2), (0, 1, 2))
    down_1 = down_from(added(jnp.where(z == 1, part_3, part_1), down_2), (1, 2, 3))
    across_0 = row_swap(summed[1][1])
    return [summed[0][0], across_0, up_1, down_1]


def one_of(values, index, axis):
    return lax.dynamic_index_in_dim(values, index, axis, keepdims=False)


def owner_first(values, position):
    c = position % CORES
    total, width = values.shape
    spots = LINE * ROWS
    values = values.reshape(2, spots, CORES, total // (2 * spots * CORES), width)
    return added(one_of(values, c, 2), core_swap(one_of(values, 1 - c, 2)))


def owner_last(values, taken, side):
    groups = [[spot * CORES + core for spot in range(LINE * ROWS)] for core in range(CORES)]
    values = lax.all_to_all(
        added(one_of(values, side, 0), taken),
        "ctx",
        split_axis=0,
        concat_axis=0,
        tiled=True,
        axis_index_groups=groups,
    )
    return jnp.sum(values.astype(jnp.float32), axis=0)


def exchange(values):
    return lax.ppermute(values, "dp", [(0, 1), (1, 0)])


def to_heads(values):
    return lax.all_to_all(values, "ctx", split_axis=0, concat_axis=0, tiled=True)


def turn(values, cosine, sine):
    half = HD // 2
    first, second = values[:, :half, :], values[:, half:, :]
    return jnp.concatenate(
        [first * cosine - second * sine, second * cosine + first * sine], axis=1
    )


def per_device(
    tokens, grad_out, w_query, w_key, w_value, w_output, gain_attn, gain_ffn, w_router, w_experts,
    deal_table, routes
):
    row_count = tokens.shape[0]
    devices = lax.axis_size("ctx")
    position = lax.axis_index("ctx")
    side = lax.axis_index("dp")
    both = ("dp", "ctx")
    shard = w_query.shape[0]
    wide = HQ * HD
    narrow = KVH * HD

    extras = jnp.concatenate(
        [w_router, gain_attn[:, None], gain_ffn[:, None], jnp.zeros((shard, 94), jnp.bfloat16)],
        axis=1,
    )
    packed_weights = lax.all_gather(
        jnp.concatenate([w_query, w_key, w_value, extras, w_output], axis=1),
        both,
        axis=0,
        tiled=True,
    )
    other_experts = exchange(w_experts)
    local = w_experts.shape[2] // F
    line_place = position // (ROWS * CORES)
    order = near_order(position)

    g_ups, g_downs, g_across, g_own = [grad_out], [grad_out], [], [grad_out]
    for s in range(2):
        sent = send_on(s, g_own[s], g_ups[s], g_downs[s])
        if s == 1:
            packed_weights, *sent = together((packed_weights, *sent))
        else:
            sent = together(tuple(sent))
        g_across.append(sent[0])
        g_ups.append(sent[1])
        g_downs.append(sent[2])
        g_own.append(newest(s + 1, g_ups, g_downs, line_place))

    full_qkv = packed_weights[:, : wide + 2 * narrow]
    extra_columns = packed_weights[:, wide + 2 * narrow : wide + 2 * narrow + 128]
    full_output = packed_weights[:, wide + 2 * narrow + 128 :]
    full_router = extra_columns[:, :E]
    gain_attn_full = extra_columns[:, E].astype(jnp.float32)
    gain_ffn_full = extra_columns[:, E + 1].astype(jnp.float32)

    expert_ids = jnp.arange(E, dtype=jnp.int32)
    picked = routes[:, :, None] == expert_ids[None, None, :]
    member = jnp.any(picked, axis=1)
    below = (jnp.arange(row_count)[:, None] > jnp.arange(row_count)[None, :]).astype(jnp.bfloat16)
    before = nn(below, member.astype(jnp.bfloat16))
    places = jnp.where(member, before, -1.0)
    slot_places = to_heads(places.T.reshape(devices, local, row_count))

    group_blocks = deal_table[0]
    own_blocks = lax.dynamic_slice_in_dim(group_blocks, 2 * position, 2)
    offsets = jnp.arange(BLK, dtype=jnp.int32)
    positions = ((own_blocks % BLOCKS)[:, None] * BLK + offsets[None, :]).reshape(-1)
    table = jnp.argsort(group_blocks).astype(jnp.int32)
    frequency = 10000.0 ** (-(jnp.arange(HD // 2).astype(jnp.float32) * 2.0 / HD))
    angles = frequency[:, None] * positions.astype(jnp.float32)[None, :]
    cosine, sine = jnp.cos(angles)[None], jnp.sin(angles)[None]
    inputs = tokens.astype(jnp.float32)
    normed = rms_norm(inputs, gain_attn_full).astype(jnp.bfloat16)
    raw = tt(full_qkv, normed)
    queries = turn(raw[:wide].reshape(HQ, HD, row_count), cosine, sine).astype(jnp.bfloat16)
    keys = turn(raw[wide : wide + narrow].reshape(KVH, HD, row_count), cosine, sine).astype(
        jnp.bfloat16
    )
    values = raw[wide + narrow :].reshape(KVH, HD, row_count).astype(jnp.bfloat16)
    ratio = HQ // KVH
    outgoing = jnp.concatenate(
        [queries, jnp.repeat(keys, ratio, axis=0), jnp.repeat(values, ratio, axis=0)], axis=1
    )
    outgoing, other_experts, slot_places = together((outgoing, other_experts, slot_places))
    packed = to_heads(outgoing)
    slot_columns = slot_places.transpose(0, 2, 1)
    first_half = jnp.where(side == 0, w_experts, other_experts)
    second_half = jnp.where(side == 0, other_experts, w_experts)
    experts = jnp.concatenate([first_half, second_half], axis=1)
    g_kept, g_first = None, 0
    for s in range(2):
        blocks = [g_own[s]] + g_across[s - 1 : s] if s else [g_own[0]]
        blocks += [core_swap(b) for b in blocks]
        count = len(blocks)
        g_kept = grad_step(
            g_first, order[g_first : g_first + count], slot_places, blocks, experts, g_kept
        )
        g_first += count
    packed, *g_kept = together((packed, *g_kept))
    sent = send_on(2, g_own[2], g_ups[2], g_downs[2])
    heads, rows_0, sums_0 = attention_forward(0, table, packed)
    heads, rows_0, sums_0, *sent = together((heads, rows_0, sums_0, *sent))
    g_across.append(sent[0])
    g_ups.append(sent[1])
    g_downs.append(sent[2])
    g_own.append(newest(3, g_ups, g_downs, line_place))
    last_across = row_swap(g_own[3])
    heads, rows_1, sums_1 = attention_forward(1, table, packed, heads)
    heads, rows_1, sums_1, last_across = together((heads, rows_1, sums_1, last_across))
    g_across.append(last_across)
    log_sum = jnp.concatenate([sums_0, sums_1], axis=1)
    attended = to_heads(heads)
    for s in range(2, LINE + 1):
        blocks = g_own[s : s + 1] + [g_across[s - 1]]
        blocks += [core_swap(b) for b in blocks]
        count = len(blocks)
        g_kept = grad_step(
            g_first, order[g_first : g_first + count], slot_places, blocks, experts, g_kept
        )
        g_first += count
    attended, *g_kept = together((attended, *g_kept))
    slot_grads, d_hidden = g_kept
    attended = attended.reshape(wide, row_count)
    residual = inputs + tn(attended, full_output)

    normed_ffn = rms_norm(residual, gain_ffn_full).astype(jnp.bfloat16)
    logits = nn(normed_ffn, full_router)
    masked = jnp.where(member, logits, floor_value)
    powers = jnp.where(member, jnp.exp(masked - jnp.max(masked, axis=1, keepdims=True)), 0.0)
    gates = powers / jnp.sum(powers, axis=1, keepdims=True)
    slot_gates = to_heads(gates.T.reshape(devices, local, row_count))
    near, far, d_gate_parts, kept = [], [], [], None
    own, across = normed_ffn, None
    ups, downs = [normed_ffn], [normed_ffn]
    first = 0
    for s in range(LINE + 1):
        blocks = [b for b in (own, across) if b is not None]
        sent = send_on(s, own, ups[-1], downs[-1])
        blocks += [core_swap(b) for b in blocks]
        count = len(blocks)
        *kept, d_gate_part, near_part, far_part = expert_step(
            first, order[first : first + count], slot_places, slot_columns, slot_gates, blocks,
            d_hidden, experts, kept
        )
        if sent:
            *sent, near_part = together((*sent, near_part))
        first += count
        near.append(near_part)
        far.append(far_part)
        d_gate_parts.append(d_gate_part)
        across = sent[0] if s < LINE else None
        if s < LINE - 1:
            ups.append(sent[1])
            downs.append(sent[2])
        own = newest(s + 1, ups, downs, line_place) if s < LINE - 1 else None
    slot_rows, hidden, d_gate_pre, d_up = kept
    arrived = scatter_sum(near, far, line_place)
    given = weight_grad(
        (1 - side).reshape(1), slot_rows, slot_grads, d_gate_pre, d_up, hidden, jnp.bfloat16
    )
    taken = [exchange(part) for part in given]
    out_rows = output_pass(order, slot_columns, hidden, experts)
    owned_experts = weight_grad(
        side.reshape(1), slot_rows, slot_grads, d_gate_pre, d_up, hidden, jnp.float32
    )
    *arrived, out_rows, taken[0], taken[1], owned_experts = together(
        (*arrived, out_rows, taken[0], taken[1], owned_experts)
    )
    ffn_grad = sum(part.astype(jnp.float32) for part in arrived)
    back = jnp.argsort(order)
    d_gate = to_heads(jnp.concatenate(d_gate_parts, axis=0)[back]).reshape(E, row_count).T
    mixture = lax.psum_scatter(out_rows, "ctx", scatter_dimension=0, tiled=True)

    d_logits = gates * (d_gate - jnp.sum(gates * d_gate, axis=1, keepdims=True))
    ffn_grad = ffn_grad + jnp.einsum(
        "re,de->rd", d_logits, full_router.astype(jnp.float32), precision=highest
    )
    router_grad = jnp.einsum(
        "rd,re->de", normed_ffn.astype(jnp.float32), d_logits, precision=highest
    )
    _, norm_back_ffn = jax.vjp(rms_norm, residual, gain_ffn_full)
    residual_norm_grad, gain_ffn_grad = norm_back_ffn(ffn_grad)
    residual_grad = grad_out.astype(jnp.float32) + residual_norm_grad
    branch_grad = residual_grad.astype(jnp.bfloat16)
    attended_grad = nt(full_output, branch_grad).astype(jnp.bfloat16)
    d_heads = to_heads(attended_grad.reshape(HQ, HD, row_count))
    output_grad = nn(attended, branch_grad)
    first_parts = owner_first(
        jnp.concatenate(
            [
                output_grad.astype(jnp.bfloat16),
                router_grad.astype(jnp.bfloat16),
                gain_ffn_grad[:, None].astype(jnp.bfloat16),
                jnp.zeros((D, 95), jnp.bfloat16),
            ],
            axis=1,
        ),
        position,
    )
    d_heads, first_parts, taken[2] = together((d_heads, first_parts, taken[2]))
    first_taken = exchange(one_of(first_parts, 1 - side, 0))

    d_packed = to_heads(attention_backward(table, packed, d_heads, rows_0, rows_1, log_sum))
    d_packed, first_taken = together((d_packed, first_taken))
    first_owned = owner_last(first_parts, first_taken, side)
    d_packed = d_packed.astype(jnp.float32)
    d_query = turn(d_packed[:, :HD], cosine, -sine).astype(jnp.bfloat16).reshape(wide, row_count)
    pairs = d_packed[:, HD:].reshape(KVH, ratio, 2 * HD, row_count).sum(axis=1)
    d_key = turn(pairs[:, :HD], cosine, -sine).astype(jnp.bfloat16).reshape(narrow, row_count)
    d_value = pairs[:, HD:].astype(jnp.bfloat16).reshape(narrow, row_count)
    d_qkv = jnp.concatenate([d_query, d_key, d_value], axis=0)
    qkv_grad = tt(normed, d_qkv)
    normed_grad = tt(d_qkv, full_qkv)
    _, norm_back_attn = jax.vjp(rms_norm, inputs, gain_attn_full)
    input_norm_grad, gain_attn_grad = norm_back_attn(normed_grad)
    tokens_grad = residual_grad + input_norm_grad
    owned_parts = owner_first(
        jnp.concatenate(
            [
                qkv_grad.astype(jnp.bfloat16),
                gain_attn_grad[:, None].astype(jnp.bfloat16),
                jnp.zeros((D, 127), jnp.bfloat16),
            ],
            axis=1,
        ),
        position,
    )
    owned = owner_last(owned_parts, exchange(one_of(owned_parts, 1 - side, 0)), side)
    mixture, late = together((mixture, d_query))
    mixed = (residual + mixture.astype(jnp.float32)).astype(jnp.bfloat16)
    expert_grad = jnp.stack(
        [mine + part.astype(jnp.float32) for mine, part in zip(owned_experts, taken)]
    )
    return (
        mixed,
        tokens_grad,
        owned[:, :wide],
        owned[:, wide : wide + narrow],
        owned[:, wide + narrow : wide + 2 * narrow],
        first_owned[:, :D],
        owned[:, wide + 2 * narrow],
        first_owned[:, D + E],
        first_owned[:, D : D + E],
        expert_grad,
    )


def solution(mesh):
    in_specs = (
        P(("dp", "ctx"), None),
        P(("dp", "ctx"), None),
        P(("dp", "ctx"), None),
        P(("dp", "ctx"), None),
        P(("dp", "ctx"), None),
        P(("dp", "ctx"), None),
        P(("dp", "ctx")),
        P(("dp", "ctx")),
        P(("dp", "ctx"), None),
        P(None, "dp", "ctx"),
        P("dp", None),
        P(("dp", "ctx"), None),
    )
    out_specs = (
        P(("dp", "ctx"), None),
        P(("dp", "ctx"), None),
        P(("dp", "ctx"), None),
        P(("dp", "ctx"), None),
        P(("dp", "ctx"), None),
        P(("dp", "ctx"), None),
        P(("dp", "ctx")),
        P(("dp", "ctx")),
        P(("dp", "ctx"), None),
        P(None, "dp", "ctx"),
    )
    body = per_device if mesh.shape["ctx"] == HQ else general_device
    return jax.shard_map(
        body, mesh=mesh, in_specs=in_specs, out_specs=out_specs, check_vma=False
    )
```

```python
from functools import partial

import jax
import jax.numpy as jnp
from jax import lax
from jax.experimental import pallas as pl
from jax.experimental.pallas import tpu as pltpu
from jax.sharding import PartitionSpec as P

D = 1024
HQ = 16
KVH = 8
HD = 64
E = 32
F = 512
TOPK = 8
BLK = 256
BLOCKS = 16
CAP = 160


epsilon = 1e-06
highest = lax.Precision.HIGHEST
floor_value = -1e30


def rms_norm(values, gain):
    return values * lax.rsqrt(jnp.mean(values * values, axis=-1, keepdims=True) + epsilon) * gain


def rotary(values, positions):
    half_size = values.shape[-1] // 2
    frequency = 10000.0 ** (-(jnp.arange(half_size).astype(jnp.float32) * 2.0 / values.shape[-1]))
    angles = positions.astype(jnp.float32)[:, None] * frequency[None, :]
    cosine = jnp.cos(angles)[:, None, :]
    sine_part = jnp.sin(angles)[:, None, :]
    first_half = values[..., :half_size]
    second = values[..., half_size:]
    return jnp.concatenate(
        [first_half * cosine - second * sine_part, second * cosine + first_half * sine_part],
        axis=-1,
    )


def heads_major(block_rows, groups, head_ratio, head_size):
    count = block_rows.shape[0]
    shaped = block_rows.reshape(count, groups, head_ratio, head_size).transpose(1, 2, 0, 3)
    return shaped.reshape(groups, head_ratio * count, head_size)


def rows_major(blocked, groups, head_ratio, head_size):
    count = blocked.shape[1] // head_ratio
    shaped = blocked.reshape(groups, head_ratio, count, head_size).transpose(2, 0, 1, 3)
    return shaped.reshape(count, groups * head_ratio * head_size)


def stats_major(block_rows, groups, head_ratio):
    count = block_rows.shape[0]
    return (
        block_rows.reshape(count, groups, head_ratio)
        .transpose(1, 2, 0)
        .reshape(groups, head_ratio * count)
    )


def pair_blocks(rows, base, groups, head_ratio, head_size):
    return jnp.stack(
        [
            heads_major(lax.dynamic_slice_in_dim(rows, base + i * BLK, BLK), groups, head_ratio, head_size)
            for i in range(2)
        ]
    )


def pair_order(block_pair, per_seq):
    places = block_pair % per_seq
    lower_slot = (places[0] > places[1]).astype(jnp.int32)
    return (lower_slot, 1 - lower_slot, jnp.minimum(places[0], places[1]), block_pair[0] // per_seq)


def keep_state(carry_state):
    return carry_state


def forward_update(query_block, key_block, value_block, slot_number, score_scale):

    def forward_apply_update(carry_state):
        running_max, running_sum, accumulated = carry_state
        scores = (
            jnp.einsum("gqd,gkd->gqk", query_block, key_block, preferred_element_type=jnp.float32)
            * score_scale
        )
        new_max = jnp.maximum(running_max[slot_number], jnp.max(scores, axis=-1))
        factor = jnp.exp(running_max[slot_number] - new_max)
        weights = jnp.exp(scores - new_max[..., None])
        new_sum = running_sum[slot_number] * factor + jnp.sum(weights, axis=-1)
        product = jnp.einsum(
            "gqk,gkd->gqd",
            weights.astype(jnp.bfloat16),
            value_block,
            preferred_element_type=jnp.float32,
        )
        new_acc = accumulated[slot_number] * factor[..., None] + product
        return (
            running_max.at[slot_number].set(new_max),
            running_sum.at[slot_number].set(new_sum),
            accumulated.at[slot_number].set(new_acc),
        )

    return forward_apply_update


def query_update(
    query_block,
    grad_block,
    log_block,
    delta_block,
    key_block,
    value_block,
    slot_number,
    score_scale,
):

    def query_apply_update(accumulated):
        scores = (
            jnp.einsum("gqd,gkd->gqk", query_block, key_block, preferred_element_type=jnp.float32)
            * score_scale
        )
        probs_full = jnp.exp(scores - log_block[..., None])
        prob_grad = jnp.einsum(
            "gqd,gkd->gqk", grad_block, value_block, preferred_element_type=jnp.float32
        )
        score_grad = (probs_full * (prob_grad - delta_block[..., None])).astype(jnp.bfloat16)
        change = (
            jnp.einsum("gqk,gkd->gqd", score_grad, key_block, preferred_element_type=jnp.float32)
            * score_scale
        )
        return accumulated.at[slot_number].add(change)

    return query_apply_update


def key_update(
    query_block,
    grad_block,
    log_block,
    delta_block,
    key_block,
    value_block,
    slot_number,
    score_scale,
):

    def key_apply_update(carry_state):
        key_accum, value_accum = carry_state
        scores = (
            jnp.einsum("gqd,gkd->gqk", query_block, key_block, preferred_element_type=jnp.float32)
            * score_scale
        )
        probs_full = jnp.exp(scores - log_block[..., None])
        value_change = jnp.einsum(
            "gqk,gqd->gkd",
            probs_full.astype(jnp.bfloat16),
            grad_block,
            preferred_element_type=jnp.float32,
        )
        prob_grad = jnp.einsum(
            "gqd,gkd->gqk", grad_block, value_block, preferred_element_type=jnp.float32
        )
        score_grad = (probs_full * (prob_grad - delta_block[..., None])).astype(jnp.bfloat16)
        key_change = (
            jnp.einsum("gqk,gqd->gkd", score_grad, query_block, preferred_element_type=jnp.float32)
            * score_scale
        )
        return (
            key_accum.at[slot_number].add(key_change),
            value_accum.at[slot_number].add(value_change),
        )

    return key_apply_update


def expert_forward(routed_rows, weights_local):
    gate_pre = jnp.einsum(
        "erd,def->erf", routed_rows, weights_local[0], preferred_element_type=jnp.float32
    )
    up_pre = jnp.einsum(
        "erd,def->erf", routed_rows, weights_local[1], preferred_element_type=jnp.float32
    )
    hidden = (jax.nn.silu(gate_pre) * up_pre).astype(jnp.bfloat16)
    return (gate_pre, up_pre, hidden)


def natural_return(partials, split_count):
    devices = partials.shape[0]
    arrived = lax.all_to_all(partials, "ctx", split_axis=0, concat_axis=0, tiled=True)
    shaped = arrived.reshape(
        devices * partials.shape[1] // split_count,
        split_count,
        partials.shape[2],
        partials.shape[3],
    )
    return jnp.sum(shaped, axis=1)


def send_back(partials, split_count):
    return natural_return(partials, split_count)


def spread_slots(slot_values, devices, local_count, split_count):
    width = slot_values.shape[-1]
    return jnp.broadcast_to(
        slot_values.reshape(E, 1, CAP, width), (E, split_count, CAP, width)
    ).reshape(devices, local_count, CAP, width)


def general_device(
    tokens,
    grad_out,
    w_query,
    w_key,
    w_value,
    w_output,
    gain_attn,
    gain_ffn,
    w_router,
    w_experts,
    deal_table,
    routes,
):
    row_count = tokens.shape[0]
    head_ratio = HQ // KVH
    score_scale = HD ** (-0.5)
    full_query, full_key, full_value, full_output, full_router, full_gain_attn, full_gain_ffn = (
        lax.all_gather(w_query, ("dp", "ctx"), axis=0, tiled=True),
        lax.all_gather(w_key, ("dp", "ctx"), axis=0, tiled=True),
        lax.all_gather(w_value, ("dp", "ctx"), axis=0, tiled=True),
        lax.all_gather(w_output, ("dp", "ctx"), axis=0, tiled=True),
        lax.all_gather(w_router, ("dp", "ctx"), axis=0, tiled=True),
        lax.all_gather(gain_attn, ("dp", "ctx"), axis=0, tiled=True),
        lax.all_gather(gain_ffn, ("dp", "ctx"), axis=0, tiled=True),
    )
    experts_local = lax.all_gather(w_experts, "dp", axis=1, tiled=True)
    columns = experts_local.shape[2]
    unit_width = min(F, columns)
    local_count = columns // unit_width
    split_count = F // unit_width
    devices = lax.axis_size("ctx")
    position = lax.axis_index("ctx")
    group_blocks = deal_table[0]
    per_seq = BLOCKS
    own_blocks = lax.dynamic_slice_in_dim(group_blocks, 2 * position, 2)
    query_low, query_high, low_place, own_seq = pair_order(own_blocks, per_seq)
    offsets = jnp.arange(BLK, dtype=jnp.int32)
    positions = ((own_blocks % per_seq)[:, None] * BLK + offsets[None, :]).reshape(-1)
    inputs = tokens.astype(jnp.float32)
    gain_attn_full = full_gain_attn.astype(jnp.float32)
    gain_ffn_full = full_gain_ffn.astype(jnp.float32)
    normed = rms_norm(inputs, gain_attn_full).astype(jnp.bfloat16)
    query_raw = jnp.dot(normed, full_query, preferred_element_type=jnp.float32).reshape(
        row_count, HQ, HD
    )
    key_raw = jnp.dot(normed, full_key, preferred_element_type=jnp.float32).reshape(
        row_count, KVH, HD
    )
    value_raw = jnp.dot(normed, full_value, preferred_element_type=jnp.float32)
    queries = rotary(query_raw, positions).astype(jnp.bfloat16).reshape(row_count, HQ * HD)
    key_proj = rotary(key_raw, positions).astype(jnp.bfloat16).reshape(row_count, KVH * HD)
    value_proj = value_raw.astype(jnp.bfloat16)
    query_heads = pair_blocks(queries, 0, KVH, head_ratio, HD)
    key_heads = pair_blocks(key_proj, 0, KVH, 1, HD)
    value_heads = pair_blocks(value_proj, 0, KVH, 1, HD)
    score_rows = head_ratio * BLK
    initial = (
        jnp.full((2, KVH, score_rows), floor_value, jnp.float32),
        jnp.zeros((2, KVH, score_rows), jnp.float32),
        jnp.zeros((2, KVH, score_rows, HD), jnp.float32),
    )
    initial = forward_update(
        query_heads[query_low], key_heads[query_low], value_heads[query_low], query_low, score_scale
    )(initial)
    carry_state = initial
    key_rows = lax.all_gather(key_proj, "ctx", axis=0, tiled=True)
    value_rows = lax.all_gather(value_proj, "ctx", axis=0, tiled=True)
    def forward_step(j, carry_state):
        key_pair = pair_blocks(key_rows, j * 2 * BLK, KVH, 1, HD)
        value_pair = pair_blocks(value_rows, j * 2 * BLK, KVH, 1, HD)
        block_pair = lax.dynamic_slice_in_dim(group_blocks, 2 * j, 2)
        key_low, key_high, key_place, key_seq = pair_order(block_pair, per_seq)
        same = key_seq == own_seq
        carry_state = lax.cond(
            same,
            forward_update(
                query_heads[query_high],
                key_pair[key_low],
                value_pair[key_low],
                query_high,
                score_scale,
            ),
            keep_state,
            carry_state,
        )
        below = key_place < low_place
        pick_query = jnp.where(below, query_low, query_high)
        pick_key = jnp.where(below, key_low, key_high)
        carry_state = lax.cond(
            same,
            forward_update(
                query_heads[pick_query],
                key_pair[pick_key],
                value_pair[pick_key],
                pick_query,
                score_scale,
            ),
            keep_state,
            carry_state,
        )
        return carry_state

    carry_state = lax.fori_loop(0, key_rows.shape[0] // (2 * BLK), forward_step, carry_state)
    running_max, running_sum, accumulated = carry_state
    attended_heads = accumulated / running_sum[..., None]
    log_total = running_max + jnp.log(running_sum)
    attended_rows = jnp.concatenate(
        [rows_major(attended_heads[i], KVH, head_ratio, HD) for i in range(2)], axis=0
    )
    attended_low = attended_rows.astype(jnp.bfloat16)
    residual = inputs + jnp.dot(attended_low, full_output, preferred_element_type=jnp.float32)
    normed_ffn = rms_norm(residual, gain_ffn_full).astype(jnp.bfloat16)
    expert_ids = jnp.arange(E, dtype=jnp.int32)
    picked = routes[:, :, None] == expert_ids[None, None, :]
    ffn_float = normed_ffn.astype(jnp.float32)
    router_full = full_router.astype(jnp.float32)
    logits = jnp.dot(ffn_float, router_full, precision=highest)
    chosen = jnp.sum(jnp.where(picked, logits[:, None, :], 0.0), axis=2)
    gate_weights = jax.nn.softmax(chosen, axis=-1)
    member = jnp.sum(picked.astype(jnp.int32), axis=1)
    before = jnp.cumsum(member, axis=0) - member
    slot_numbers = jnp.sum(jnp.where(picked, before[:, None, :], 0), axis=2)
    flat_slot = (routes * CAP + slot_numbers).reshape(-1)
    owner_rows = (
        jnp.zeros((E * CAP,), jnp.int32)
        .at[flat_slot]
        .set(jnp.repeat(jnp.arange(1, row_count + 1, dtype=jnp.int32), TOPK))
    )
    slot_gate = jnp.zeros((E * CAP,), jnp.float32).at[flat_slot].set(gate_weights.reshape(-1))
    padded_rows = jnp.concatenate([jnp.zeros((1, D), jnp.bfloat16), normed_ffn], axis=0)
    slot_rows = padded_rows[owner_rows]
    outgoing = spread_slots(slot_rows, devices, local_count, split_count)
    arrived = lax.all_to_all(outgoing, "ctx", split_axis=0, concat_axis=0, tiled=True)
    routed_rows = arrived.transpose(1, 0, 2, 3).reshape(local_count, devices * outgoing.shape[2], D)
    weights_local = experts_local.reshape(3, D, local_count, unit_width)
    gate_pre, up_pre, hidden = expert_forward(routed_rows, weights_local)
    expert_out = jnp.einsum(
        "erf,def->erd", hidden, weights_local[2], preferred_element_type=jnp.float32
    )
    combined = send_back(
        expert_out.reshape(local_count, devices, outgoing.shape[2], D).transpose(1, 0, 2, 3),
        split_count,
    )
    routed_out = combined.reshape(E * CAP, D)[flat_slot].reshape(row_count, TOPK, D)
    mixed = (residual + jnp.sum(gate_weights[:, :, None] * routed_out, axis=1)).astype(jnp.bfloat16)
    upstream = grad_out.astype(jnp.float32)
    gate_grad = jnp.sum(routed_out * upstream[:, None, :], axis=2)
    chosen_grad = gate_weights * (
        gate_grad - jnp.sum(gate_weights * gate_grad, axis=1, keepdims=True)
    )
    logits_grad = jnp.sum(jnp.where(picked, chosen_grad[:, :, None], 0.0), axis=1)
    padded_grad = jnp.concatenate([jnp.zeros((1, D), jnp.float32), upstream], axis=0)
    slot_grad = (padded_grad[owner_rows] * slot_gate[:, None]).astype(jnp.bfloat16)
    outgoing_grad = spread_slots(slot_grad, devices, local_count, split_count)
    arrived_grad = lax.all_to_all(outgoing_grad, "ctx", split_axis=0, concat_axis=0, tiled=True)
    grad_rows = arrived_grad.transpose(1, 0, 2, 3).reshape(
        local_count, devices * outgoing.shape[2], D
    )
    hidden_grad = jnp.einsum(
        "erd,def->erf", grad_rows, weights_local[2], preferred_element_type=jnp.float32
    )
    sigmoid = jax.nn.sigmoid(gate_pre)
    up_grad = (hidden_grad * gate_pre * sigmoid).astype(jnp.bfloat16)
    gate_pre_grad = (hidden_grad * up_pre * sigmoid * (1.0 + gate_pre * (1.0 - sigmoid))).astype(
        jnp.bfloat16
    )
    weight_grad = jnp.stack(
        [
            jnp.einsum(
                "erd,erf->def", routed_rows, gate_pre_grad, preferred_element_type=jnp.float32
            ),
            jnp.einsum("erd,erf->def", routed_rows, up_grad, preferred_element_type=jnp.float32),
            jnp.einsum("erd,erf->def", grad_rows, hidden, preferred_element_type=jnp.float32),
        ]
    ).reshape(3, D, local_count * unit_width)
    input_grad = jnp.einsum(
        "erf,def->erd", gate_pre_grad, weights_local[0], preferred_element_type=jnp.float32
    )
    input_grad = input_grad + jnp.einsum(
        "erf,def->erd", up_grad, weights_local[1], preferred_element_type=jnp.float32
    )
    returned = send_back(
        input_grad.reshape(local_count, devices, outgoing.shape[2], D).transpose(1, 0, 2, 3),
        split_count,
    )
    ffn_grad = jnp.sum(returned.reshape(E * CAP, D)[flat_slot].reshape(row_count, TOPK, D), axis=1)
    ffn_grad = ffn_grad + jnp.einsum("re,de->rd", logits_grad, router_full, precision=highest)
    router_grad = jnp.einsum("rd,re->de", ffn_float, logits_grad, precision=highest)
    expert_grad = lax.psum_scatter(weight_grad, "dp", scatter_dimension=1, tiled=True)
    _, norm_back_ffn = jax.vjp(rms_norm, residual, gain_ffn_full)
    residual_norm_grad, gain_ffn_grad = norm_back_ffn(ffn_grad)
    residual_grad = upstream + residual_norm_grad
    branch_grad = residual_grad.astype(jnp.bfloat16)
    output_grad = jnp.einsum(
        "rc,rd->cd", attended_low, branch_grad, preferred_element_type=jnp.float32
    )
    attended_grad = jnp.einsum(
        "rd,cd->rc", branch_grad, full_output, preferred_element_type=jnp.float32
    ).astype(jnp.bfloat16)
    delta_rows = jnp.sum(
        (attended_grad.astype(jnp.float32) * attended_rows).reshape(row_count, HQ, HD), axis=-1
    )
    delta_heads = jnp.stack(
        [stats_major(delta_rows[i * BLK : (i + 1) * BLK], KVH, head_ratio) for i in range(2)]
    )
    grad_heads = pair_blocks(attended_grad, 0, KVH, head_ratio, HD)
    all_log, all_delta = (
        lax.all_gather(log_total, "ctx", axis=0, tiled=True),
        lax.all_gather(delta_heads, "ctx", axis=0, tiled=True),
    )
    query_start = query_update(
        query_heads[query_low],
        grad_heads[query_low],
        log_total[query_low],
        delta_heads[query_low],
        key_heads[query_low],
        value_heads[query_low],
        query_low,
        score_scale,
    )(jnp.zeros((2, KVH, score_rows, HD), jnp.float32))
    accumulated_grad = query_start
    key_rows = lax.all_gather(key_proj, "ctx", axis=0, tiled=True)
    value_rows = lax.all_gather(value_proj, "ctx", axis=0, tiled=True)
    def query_step(j, accumulated_grad):
        key_pair = pair_blocks(key_rows, j * 2 * BLK, KVH, 1, HD)
        value_pair = pair_blocks(value_rows, j * 2 * BLK, KVH, 1, HD)
        block_pair = lax.dynamic_slice_in_dim(group_blocks, 2 * j, 2)
        key_low, key_high, key_place, key_seq = pair_order(block_pair, per_seq)
        same = key_seq == own_seq
        first = query_update(
            query_heads[query_high],
            grad_heads[query_high],
            log_total[query_high],
            delta_heads[query_high],
            key_pair[key_low],
            value_pair[key_low],
            query_high,
            score_scale,
        )
        accumulated_grad = lax.cond(same, first, keep_state, accumulated_grad)
        below = key_place < low_place
        pick_query = jnp.where(below, query_low, query_high)
        pick_key = jnp.where(below, key_low, key_high)
        second_update = query_update(
            query_heads[pick_query],
            grad_heads[pick_query],
            log_total[pick_query],
            delta_heads[pick_query],
            key_pair[pick_key],
            value_pair[pick_key],
            pick_query,
            score_scale,
        )
        accumulated_grad = lax.cond(same, second_update, keep_state, accumulated_grad)
        return accumulated_grad

    accumulated_grad = lax.fori_loop(0, key_rows.shape[0] // (2 * BLK), query_step, accumulated_grad)
    zero_keys = jnp.zeros((2, KVH, BLK, HD), jnp.float32)
    key_start = key_update(
        query_heads[query_low],
        grad_heads[query_low],
        log_total[query_low],
        delta_heads[query_low],
        key_heads[query_low],
        value_heads[query_low],
        query_low,
        score_scale,
    )((zero_keys, zero_keys))
    carry_state = key_start
    start_row = jnp.int32(0)
    query_rows = lax.all_gather(queries, "ctx", axis=0, tiled=True)
    grad_piece = lax.all_gather(attended_grad, "ctx", axis=0, tiled=True)
    def key_step(j, carry_state):
        slot_first = start_row // BLK + 2 * j
        query_pair = pair_blocks(query_rows, j * 2 * BLK, KVH, head_ratio, HD)
        grad_pair = pair_blocks(grad_piece, j * 2 * BLK, KVH, head_ratio, HD)
        block_pair = lax.dynamic_slice_in_dim(group_blocks, slot_first, 2)
        log_pair = lax.dynamic_slice_in_dim(all_log, slot_first, 2)
        delta_pair = lax.dynamic_slice_in_dim(all_delta, slot_first, 2)
        remote_low, remote_high, remote_place, remote_seq = pair_order(block_pair, per_seq)
        same = remote_seq == own_seq
        first = key_update(
            query_pair[remote_high],
            grad_pair[remote_high],
            log_pair[remote_high],
            delta_pair[remote_high],
            key_heads[query_low],
            value_heads[query_low],
            query_low,
            score_scale,
        )
        carry_state = lax.cond(same, first, keep_state, carry_state)
        below = low_place < remote_place
        pick_remote = jnp.where(below, remote_low, remote_high)
        pick_own = jnp.where(below, query_low, query_high)
        second_update = key_update(
            query_pair[pick_remote],
            grad_pair[pick_remote],
            log_pair[pick_remote],
            delta_pair[pick_remote],
            key_heads[pick_own],
            value_heads[pick_own],
            pick_own,
            score_scale,
        )
        carry_state = lax.cond(same, second_update, keep_state, carry_state)
        return carry_state

    carry_state = lax.fori_loop(0, query_rows.shape[0] // (2 * BLK), key_step, carry_state)
    key_grad_heads, value_grad_heads = carry_state
    query_grad_rows = jnp.concatenate(
        [rows_major(accumulated_grad[i], KVH, head_ratio, HD) for i in range(2)], axis=0
    )
    key_grad_rows = jnp.concatenate(
        [rows_major(key_grad_heads[i], KVH, 1, HD) for i in range(2)], axis=0
    )
    value_grad_rows = jnp.concatenate(
        [rows_major(value_grad_heads[i], KVH, 1, HD) for i in range(2)], axis=0
    )
    _, query_rot_back = jax.vjp(partial(rotary, positions=positions), query_raw)
    _, key_rot_back = jax.vjp(partial(rotary, positions=positions), key_raw)
    query_proj_grad = (
        query_rot_back(query_grad_rows.reshape(row_count, HQ, HD))[0]
        .reshape(row_count, HQ * HD)
        .astype(jnp.bfloat16)
    )
    key_proj_grad = (
        key_rot_back(key_grad_rows.reshape(row_count, KVH, HD))[0]
        .reshape(row_count, KVH * HD)
        .astype(jnp.bfloat16)
    )
    value_proj_grad = value_grad_rows.astype(jnp.bfloat16)
    query_weight_grad = jnp.einsum(
        "rd,rc->dc", normed, query_proj_grad, preferred_element_type=jnp.float32
    )
    key_weight_grad = jnp.einsum(
        "rd,rc->dc", normed, key_proj_grad, preferred_element_type=jnp.float32
    )
    value_weight_grad = jnp.einsum(
        "rd,rc->dc", normed, value_proj_grad, preferred_element_type=jnp.float32
    )
    normed_grad = jnp.einsum(
        "rc,dc->rd", query_proj_grad, full_query, preferred_element_type=jnp.float32
    )
    normed_grad = normed_grad + jnp.einsum(
        "rc,dc->rd", key_proj_grad, full_key, preferred_element_type=jnp.float32
    )
    normed_grad = normed_grad + jnp.einsum(
        "rc,dc->rd", value_proj_grad, full_value, preferred_element_type=jnp.float32
    )
    _, norm_back_attn = jax.vjp(rms_norm, inputs, gain_attn_full)
    input_norm_grad, gain_attn_grad = norm_back_attn(normed_grad)
    tokens_grad = residual_grad + input_norm_grad
    owned = (
        lax.psum_scatter(query_weight_grad, ("dp", "ctx"), scatter_dimension=0, tiled=True),
        lax.psum_scatter(key_weight_grad, ("dp", "ctx"), scatter_dimension=0, tiled=True),
        lax.psum_scatter(value_weight_grad, ("dp", "ctx"), scatter_dimension=0, tiled=True),
        lax.psum_scatter(output_grad, ("dp", "ctx"), scatter_dimension=0, tiled=True),
        lax.psum_scatter(router_grad, ("dp", "ctx"), scatter_dimension=0, tiled=True),
        lax.psum_scatter(gain_attn_grad, ("dp", "ctx"), scatter_dimension=0, tiled=True),
        lax.psum_scatter(gain_ffn_grad, ("dp", "ctx"), scatter_dimension=0, tiled=True),
    )
    return (
        mixed,
        tokens_grad,
        owned[0],
        owned[1],
        owned[2],
        owned[3],
        owned[5],
        owned[6],
        owned[4],
        expert_grad,
    )


VMEM_BYTES = 60 * 1024 * 1024


def nn(a, b):
    return jnp.dot(a, b, preferred_element_type=jnp.float32)


def nt(a, b):
    return lax.dot_general(a, b, (((1,), (1,)), ((), ())), preferred_element_type=jnp.float32)


def tn(a, b):
    return lax.dot_general(a, b, (((0,), (0,)), ((), ())), preferred_element_type=jnp.float32)


def tt(a, b):
    return lax.dot_general(a, b, (((0,), (1,)), ((), ())), preferred_element_type=jnp.float32)


def lanes_of(slot):
    return pl.ds(pl.multiple_of((slot % 2) * BLK, BLK), BLK)


def by_core(table, mine, other, work_on):
    core = table[table.shape[0] - 1]

    @pl.when(core == 0)
    def _():
        work_on(mine, other)

    @pl.when(core == 1)
    def _():
        work_on(other, mine)


def attention_forward_kernel(
    table, mine, other, out, out_rows, log_sum, q_seq, k_seq, v_seq
):
    for seq in range(2):

        def load(key_source, value_source):
            for g in range(BLOCKS):
                slot = table[seq * BLOCKS + g]
                lanes = lanes_of(slot)
                here = slice(g * BLK, (g + 1) * BLK)
                q_seq[:, here] = mine[slot // 2, 0:HD, lanes] * jnp.bfloat16(HD**-0.5)
                keys = key_source[slot // 2, HD : 2 * HD, lanes]
                k_seq[here, :] = keys.astype(jnp.float32).T.astype(jnp.bfloat16)
                v_seq[:, here] = value_source[slot // 2, HD : 2 * HD, lanes]

        by_core(table, mine, other, load)
        span = BLOCKS * BLK
        top = jnp.full((1, span), floor_value, jnp.float32)
        total = jnp.zeros((1, span), jnp.float32)
        acc = jnp.zeros((HD, span), jnp.float32)
        for g in range(BLOCKS):
            here = slice(g * BLK, (g + 1) * BLK)
            scores = nn(k_seq[here, :], q_seq[:, g * BLK :])
            new_top = jnp.maximum(top, jnp.max(scores, axis=0, keepdims=True))
            factor = jnp.exp(top - new_top)
            weights = jnp.exp(scores - new_top)
            total = total * factor + jnp.sum(weights, axis=0, keepdims=True)
            acc = acc * factor + nn(v_seq[:, here], weights.astype(jnp.bfloat16))
            final = acc[:, :BLK] / total[:, :BLK]
            place_of = slice(seq * span + g * BLK, seq * span + (g + 1) * BLK)
            out_rows[:, place_of] = final
            log_sum[:, place_of] = new_top[:, :BLK] + jnp.log(total[:, :BLK])
            slot = table[seq * BLOCKS + g]
            out[slot // 2, :, lanes_of(slot)] = final.astype(jnp.bfloat16)
            top, total, acc = new_top[:, BLK:], total[:, BLK:], acc[:, BLK:]


def attention_backward_kernel(
    table, mine, other, d_out, out_rows, log_sum, q_grads, kept, given, q_seq, k_cols, k_seq,
    v_seq, d_seq, delta, dq, dk, dv
):
    span = BLOCKS * BLK
    for seq in range(2):

        def load(key_source, value_source):
            for g in range(BLOCKS):
                slot = table[seq * BLOCKS + g]
                lanes = lanes_of(slot)
                here = slice(g * BLK, (g + 1) * BLK)
                q_seq[:, here] = mine[slot // 2, 0:HD, lanes] * jnp.bfloat16(HD**-0.5)
                keys = key_source[slot // 2, HD : 2 * HD, lanes]
                k_cols[:, here] = keys
                k_seq[here, :] = keys.astype(jnp.float32).T.astype(jnp.bfloat16)
                values = value_source[slot // 2, HD : 2 * HD, lanes]
                v_seq[here, :] = values.astype(jnp.float32).T.astype(jnp.bfloat16)
                d_block = d_out[slot // 2, :, lanes]
                d_seq[:, here] = d_block
                out_block = out_rows[:, seq * span + g * BLK : seq * span + (g + 1) * BLK]
                delta[:, here] = jnp.sum(
                    d_block.astype(jnp.float32) * out_block, axis=0, keepdims=True
                )

        by_core(table, mine, other, load)
        dq[...] = jnp.zeros_like(dq)
        for g in range(BLOCKS):
            keys = slice(g * BLK, (g + 1) * BLK)
            later = slice(g * BLK, span)
            q = q_seq[:, later]
            d = d_seq[:, later]
            sums = log_sum[:, seq * span + g * BLK : (seq + 1) * span]
            probs = jnp.exp(nn(k_seq[keys, :], q) - sums)
            d_scores = (probs * (nn(v_seq[keys, :], d) - delta[:, later])).astype(jnp.bfloat16)
            dv[:, keys] = nt(d, probs.astype(jnp.bfloat16))
            dk[:, keys] = nt(q, d_scores)
            dq[:, later] += nn(k_cols[:, keys], d_scores)

        def store(key_target, value_target):
            for g in range(BLOCKS):
                slot = table[seq * BLOCKS + g]
                lanes = lanes_of(slot)
                here = slice(g * BLK, (g + 1) * BLK)
                q_grads[slot // 2, :, lanes] = (dq[:, here] * HD**-0.5).astype(jnp.bfloat16)
                key_target[slot // 2, :, lanes] = dk[:, here].astype(jnp.bfloat16)
                value_target[slot // 2, :, lanes] = dv[:, here].astype(jnp.bfloat16)

        by_core(table, kept, given, store)


def work(microseconds):
    return int(microseconds * 1.15e9)


def params():
    return pltpu.CompilerParams(vmem_limit_bytes=VMEM_BYTES)


def attention_forward(table, mine, other):
    count, _, row_count = mine.shape
    total = BLOCKS * BLK
    whole = pl.BlockSpec(memory_space=pltpu.VMEM)
    return pl.pallas_call(
        attention_forward_kernel,
        out_shape=(
            jax.ShapeDtypeStruct((count, HD, row_count), jnp.bfloat16),
            jax.ShapeDtypeStruct((HD, 2 * total), jnp.float32),
            jax.ShapeDtypeStruct((1, 2 * total), jnp.float32),
        ),
        in_specs=[pl.BlockSpec(memory_space=pltpu.SMEM), whole, whole],
        out_specs=(whole,) * 3,
        scratch_shapes=[
            pltpu.VMEM((HD, total), jnp.bfloat16),
            pltpu.VMEM((total, HD), jnp.bfloat16),
            pltpu.VMEM((HD, total), jnp.bfloat16),
        ],
        compiler_params=params(),
        cost_estimate=pl.CostEstimate(
            flops=work(36), bytes_accessed=mine.size * 4, transcendentals=total * total // 2
        ),
        name="attention_forward",
    )(table, mine, other)


def attention_backward(table, mine, other, d_out, out_rows, log_sum):
    total = BLOCKS * BLK
    whole = pl.BlockSpec(memory_space=pltpu.VMEM)
    shape = jax.ShapeDtypeStruct(d_out.shape, jnp.bfloat16)
    return pl.pallas_call(
        attention_backward_kernel,
        out_shape=(shape,) * 3,
        in_specs=[pl.BlockSpec(memory_space=pltpu.SMEM)] + [whole] * 5,
        out_specs=(whole,) * 3,
        scratch_shapes=[
            pltpu.VMEM((HD, total), jnp.bfloat16),
            pltpu.VMEM((HD, total), jnp.bfloat16),
            pltpu.VMEM((total, HD), jnp.bfloat16),
            pltpu.VMEM((total, HD), jnp.bfloat16),
            pltpu.VMEM((HD, total), jnp.bfloat16),
            pltpu.VMEM((1, total), jnp.float32),
            pltpu.VMEM((HD, total), jnp.float32),
            pltpu.VMEM((HD, total), jnp.float32),
            pltpu.VMEM((HD, total), jnp.float32),
        ],
        compiler_params=params(),
        cost_estimate=pl.CostEstimate(
            flops=work(58), bytes_accessed=mine.size * 6, transcendentals=total * total // 2
        ),
        name="attention_backward",
    )(table, mine, other, d_out, out_rows, log_sum)


def slot_match(places, rows):
    numbers = lax.broadcasted_iota(jnp.int32, (rows, places.shape[1]), 0).astype(jnp.float32)
    return numbers == places


def column_match(places, columns):
    numbers = lax.broadcasted_iota(jnp.int32, (places.shape[0], columns), 1).astype(jnp.float32)
    return jnp.where(numbers == places, 1.0, 0.0).astype(jnp.bfloat16)


def both_match(places):
    return jnp.concatenate(
        [
            jnp.where(slot_match(places[e : e + 1, :], CAP), 1.0, 0.0)
            for e in range(places.shape[0])
        ],
        axis=0,
    )


def spread_match(places):
    columns = places.T
    count = places.shape[0] * CAP
    numbers = lax.broadcasted_iota(jnp.int32, (columns.shape[0], count), 1)
    found = numbers < 0
    for e in range(places.shape[0]):
        column = columns[:, e : e + 1]
        found = found | (numbers.astype(jnp.float32) == jnp.where(column < 0, -1.0, column + e * CAP))
    return jnp.where(found, 1.0, 0.0).astype(jnp.bfloat16)


def pick_rows(order, places, sources, picked):
    g = pl.program_id(0)
    for k in range(len(sources) // 2):

        @pl.when(g == k)
        def _(k=k):
            for i in range(2):
                pick = both_match(places[order[2 * k + i]]).astype(jnp.bfloat16)
                rows = nn(pick, sources[2 * k + i][...]).astype(jnp.bfloat16)
                for e in range(places.shape[1]):
                    picked[e, i * CAP : (i + 1) * CAP, :] = rows[e * CAP : (e + 1) * CAP]


def grad_kernel(count, order, places, *refs):
    sources, weights = refs[:count], refs[count]
    slot_rows, d_hidden = refs[-2:]
    pick_rows(order, places, sources, slot_rows)
    for e in range(places.shape[1]):
        d_hidden[e] = nn(slot_rows[e], weights[0, :, e * F : (e + 1) * F]).astype(jnp.bfloat16)


def grad_step(first, order, places, blocks, weights, kept):
    devices, local, row_count = places.shape
    count = len(blocks)
    kept = () if kept is None else tuple(kept)
    whole = pl.BlockSpec((devices, local, row_count), lambda g, order: (0, 0, 0))
    block = pl.BlockSpec((row_count, D), lambda g, order: (0, 0))
    return pl.pallas_call(
        partial(grad_kernel, count),
        grid_spec=pltpu.PrefetchScalarGridSpec(
            num_scalar_prefetch=1,
            grid=(count // 2,),
            in_specs=[
                whole,
                *([block] * count),
                pl.BlockSpec((1, D, local * F), lambda g, order: (2, 0, 0)),
            ]
            + [pl.BlockSpec(memory_space=pl.ANY)] * len(kept),
            out_specs=(
                pl.BlockSpec((local, 2 * CAP, D), lambda g, order: (0, first // 2 + g, 0)),
                pl.BlockSpec((local, 2 * CAP, F), lambda g, order: (0, first // 2 + g, 0)),
            ),
        ),
        out_shape=(
            jax.ShapeDtypeStruct((local, devices * CAP, D), jnp.bfloat16),
            jax.ShapeDtypeStruct((local, devices * CAP, F), jnp.bfloat16),
        ),
        input_output_aliases={count + 3 + i: i for i in range(len(kept))},
        compiler_params=params(),
        cost_estimate=pl.CostEstimate(
            flops=work(2 * count + 2), bytes_accessed=count * row_count * D * 4, transcendentals=0
        ),
        name="grad_step",
    )(order, places, *blocks, weights, *kept)


def expert_kernel(count, order, places, gates, *refs):
    sources, (d_hidden, weights) = refs[:count], refs[count : count + 2]
    slot_rows, hidden, d_gate_pre, d_up, d_gate, near, far, back = refs[-8:]
    g = pl.program_id(0)
    local = places.shape[1]
    pick_rows(order, places, sources, slot_rows)
    here = [slice(e * F, (e + 1) * F) for e in range(local)]
    numbers = [order[2 * g], order[2 * g + 1]]
    picks = [both_match(places[j]) for j in numbers]
    slot_gates = []
    for e in range(local):
        gate_pre = nn(slot_rows[e], weights[0, :, here[e]])
        up_pre = nn(slot_rows[e], weights[1, :, here[e]])
        gate = jnp.concatenate(
            [
                jnp.sum(
                    picks[i][e * CAP : (e + 1) * CAP] * gates[numbers[i]][e : e + 1, :],
                    axis=1,
                    keepdims=True,
                )
                for i in range(2)
            ],
            axis=0,
        )
        raw = d_hidden[e].astype(jnp.float32)
        sig = 1.0 / (1.0 + jnp.exp(-gate_pre))
        silu = gate_pre * sig
        value = silu * up_pre
        hidden[e] = (gate * value).astype(jnp.bfloat16)
        scaled = raw * gate
        d_up[e] = (scaled * silu).astype(jnp.bfloat16)
        d_gate_pre[e] = (scaled * up_pre * sig * (1.0 + gate_pre * (1.0 - sig))).astype(
            jnp.bfloat16
        )
        slot_gates.append(jnp.sum(raw * value, axis=1, keepdims=True))
    for e in range(local):
        back[e] = (
            nt(d_gate_pre[e], weights[0, :, here[e]]) + nt(d_up[e], weights[1, :, here[e]])
        ).astype(jnp.bfloat16)
    results = []
    for i in range(2):
        part = slice(i * CAP, (i + 1) * CAP)
        for e in range(local):
            d_gate[i, e : e + 1, :] = jnp.sum(
                picks[i][e * CAP : (e + 1) * CAP] * slot_gates[e][part], axis=0, keepdims=True
            )
        rows = jnp.concatenate([back[e, part] for e in range(local)], axis=0)
        results.append(nn(spread_match(places[numbers[i]]), rows).astype(jnp.bfloat16))
    if count == 2:
        near[0] = results[0]
        far[0] = results[1]
    else:

        @pl.when(g == 0)
        def _():
            near[0] = results[0]
            near[1] = results[1]

        @pl.when(g == 1)
        def _():
            far[0] = results[0]
            far[1] = results[1]


def expert_step(first, order, places, gates, blocks, d_hidden, weights, kept):
    devices, local, row_count = places.shape
    count = len(blocks)
    half = count // 2
    wide_slots = pl.BlockSpec((local, 2 * CAP, D), lambda g, order: (0, first // 2 + g, 0))
    slots = pl.BlockSpec((local, 2 * CAP, F), lambda g, order: (0, first // 2 + g, 0))
    whole = pl.BlockSpec((devices, local, row_count), lambda g, order: (0, 0, 0))
    block = pl.BlockSpec((row_count, D), lambda g, order: (0, 0))
    sums = pl.BlockSpec((half, row_count, D), lambda g, order: (0, 0, 0))
    kept = () if kept is None else tuple(kept)
    first_kept = 5 + count
    return pl.pallas_call(
        partial(expert_kernel, count),
        grid_spec=pltpu.PrefetchScalarGridSpec(
            num_scalar_prefetch=1,
            grid=(half,),
            in_specs=[
                whole,
                whole,
                *([block] * count),
                slots,
                pl.BlockSpec((2, D, local * F), lambda g, order: (0, 0, 0)),
            ]
            + [pl.BlockSpec(memory_space=pl.ANY)] * len(kept),
            out_specs=(
                wide_slots,
                slots,
                slots,
                slots,
                pl.BlockSpec((2, local, row_count), lambda g, order: (g, 0, 0)),
                sums,
                sums,
            ),
            scratch_shapes=[pltpu.VMEM((local, 2 * CAP, D), jnp.bfloat16)],
        ),
        out_shape=(
            jax.ShapeDtypeStruct((local, devices * CAP, D), jnp.bfloat16),
            jax.ShapeDtypeStruct((local, devices * CAP, F), jnp.bfloat16),
            jax.ShapeDtypeStruct((local, devices * CAP, F), jnp.bfloat16),
            jax.ShapeDtypeStruct((local, devices * CAP, F), jnp.bfloat16),
            jax.ShapeDtypeStruct((count, local, row_count), jnp.float32),
            jax.ShapeDtypeStruct((half, row_count, D), jnp.bfloat16),
            jax.ShapeDtypeStruct((half, row_count, D), jnp.bfloat16),
        ),
        input_output_aliases={first_kept + i: i for i in range(len(kept))},
        compiler_params=params(),
        cost_estimate=pl.CostEstimate(
            flops=work(4 * count + 2),
            bytes_accessed=count * row_count * D * 6,
            transcendentals=count * local * CAP * F,
        ),
        name="expert_step",
    )(order, places, gates, *blocks, d_hidden, weights, *kept)


def output_kernel(order, columns, hidden, weights, out_rows):
    total = None
    for e in range(columns.shape[2]):
        out = nt(hidden[e], weights[0, :, e * F : (e + 1) * F]).astype(jnp.bfloat16)
        spread = nn(column_match(columns[0, :, e : e + 1], CAP), out)
        total = spread if total is None else total + spread
    out_rows[...] = total.astype(jnp.bfloat16)


def output_pass(order, columns, hidden, weights):
    devices, row_count, local = columns.shape
    return pl.pallas_call(
        output_kernel,
        grid_spec=pltpu.PrefetchScalarGridSpec(
            num_scalar_prefetch=1,
            grid=(devices,),
            in_specs=[
                pl.BlockSpec((1, row_count, local), lambda j, order: (order[j], 0, 0)),
                pl.BlockSpec((local, CAP, F), lambda j, order: (0, j, 0)),
                pl.BlockSpec((1, D, local * F), lambda j, order: (2, 0, 0)),
            ],
            out_specs=pl.BlockSpec((row_count, D), lambda j, order: (order[j], 0)),
        ),
        out_shape=jax.ShapeDtypeStruct((devices * row_count, D), jnp.bfloat16),
        compiler_params=params(),
        cost_estimate=pl.CostEstimate(
            flops=work(26), bytes_accessed=devices * row_count * D * 3,
            transcendentals=0,
        ),
        name="output_pass",
    )(order, columns, hidden, weights)


def weight_grad_kernel(half, slot_rows, slot_grads, d_gate_pre, d_up, hidden, *out):
    out[0][...] = tn(slot_rows[0], d_gate_pre[0]).astype(out[0].dtype)
    out[1][...] = tn(slot_rows[0], d_up[0]).astype(out[1].dtype)
    out[2][...] = tn(slot_grads[0], hidden[0]).astype(out[2].dtype)


def weight_grad(half, slot_rows, slot_grads, d_gate_pre, d_up, hidden, dtype):
    local, count, _ = hidden.shape
    wide_slots = pl.BlockSpec((1, count, D // 2), lambda e, half: (e, 0, half[0]))
    slots = pl.BlockSpec((1, count, F), lambda e, half: (e, 0, 0))
    return pl.pallas_call(
        weight_grad_kernel,
        grid_spec=pltpu.PrefetchScalarGridSpec(
            num_scalar_prefetch=1,
            grid=(local,),
            in_specs=[wide_slots, wide_slots, slots, slots, slots],
            out_specs=(pl.BlockSpec((D // 2, F), lambda e, half: (0, e)),) * 3,
        ),
        out_shape=(jax.ShapeDtypeStruct((D // 2, local * F), dtype),) * 3,
        compiler_params=params(),
        cost_estimate=pl.CostEstimate(
            flops=work(15), bytes_accessed=local * count * D * 8, transcendentals=0
        ),
        name="weight_grad",
    )(half, slot_rows, slot_grads, d_gate_pre, d_up, hidden)


LINE = 4
ROWS = 2
CORES = 2
together = lax.optimization_barrier


def place(z, y, c):
    return (z * ROWS + y) * CORES + c


def move(values, target):
    pairs = []
    for z in range(LINE):
        for y in range(ROWS):
            for c in range(CORES):
                there = target(z, y, c)
                if there is not None and 0 <= there[0] < LINE:
                    pairs.append((place(z, y, c), place(*there)))
    return lax.ppermute(values, "ctx", pairs)


def core_swap(values):
    return move(values, lambda z, y, c: (z, y, 1 - c))


def row_swap(values):
    return move(values, lambda z, y, c: (z, 1 - y, c))


def up_from(values, sources):
    return move(values, lambda z, y, c: (z + 1, y, c) if z in sources else None)


def down_from(values, sources):
    return move(values, lambda z, y, c: (z - 1, y, c) if z in sources else None)


def added(*terms):
    total = terms[0].astype(jnp.float32)
    for term in terms[1:]:
        total = total + term.astype(jnp.float32)
    return total.astype(jnp.bfloat16)


LINE_ORDER = ((0, 1, 2, 3), (1, 2, 3, 0), (2, 1, 0, 3), (3, 2, 1, 0))


def send_on(s, own, up, down):
    sent = []
    if s < LINE:
        sent.append(row_swap(own))
    if s < LINE - 1:
        sent.append(up_from(up, tuple(range(s, LINE - 1))))
        sent.append(down_from(down, tuple(range(1, LINE - s))))
    return sent


def newest(s, ups, downs, z):
    if s < LINE - 1:
        return jnp.where(z >= 2, ups[s], downs[s])
    return jnp.where(
        z == 0, downs[3], jnp.where(z == 1, ups[1], jnp.where(z == 2, downs[1], ups[3]))
    )


def near_order(position):
    z = position // (ROWS * CORES)
    y = position // CORES % ROWS
    c = position % CORES
    line = jnp.asarray(LINE_ORDER, jnp.int32)[z]
    steps = []
    for s in range(LINE + 1):
        for other_core in range(CORES):
            if s < LINE:
                steps.append(place(line[s], y, c ^ other_core))
            if s > 0:
                steps.append(place(line[s - 1], 1 - y, c ^ other_core))
    return jnp.stack(steps).astype(jnp.int32)


def scatter_sum(summed, z):
    across_3 = row_swap(summed[4][0])
    across_3, give_2, give_1, give_0 = together(
        (across_3, summed[3][1], summed[2][1], summed[1][1])
    )
    part_3 = added(summed[3][0], across_3)
    up_3 = up_from(part_3, (0,))
    down_3 = down_from(part_3, (3,))
    across_2 = row_swap(give_2)
    up_3, down_3, across_2, give_1, give_0 = together((up_3, down_3, across_2, give_1, give_0))
    part_2 = added(summed[2][0], across_2)
    up_2 = up_from(added(part_2, up_3), (0, 1))
    down_2 = down_from(added(part_2, down_3), (3, 2))
    across_1 = row_swap(give_1)
    up_2, down_2, across_1, give_0 = together((up_2, down_2, across_1, give_0))
    part_1 = added(summed[1][0], across_1)
    up_1 = up_from(added(jnp.where(z == 2, part_3, part_1), up_2), (0, 1, 2))
    down_1 = down_from(added(jnp.where(z == 1, part_3, part_1), down_2), (1, 2, 3))
    across_0 = row_swap(give_0)
    return [summed[0][0], across_0, up_1, down_1]


def one_of(values, index, axis):
    return lax.dynamic_index_in_dim(values, index, axis, keepdims=False)


def halves(values, core, axis):
    total = values.shape[axis]
    shape = list(values.shape)
    split = shape[:axis] + [LINE * ROWS * 2, CORES, total // (2 * LINE * ROWS * CORES)]
    values = values.reshape(split + shape[axis + 1 :])
    shape[axis] = total // CORES
    return tuple(
        one_of(values, which, axis + 1).reshape(shape) for which in (core, 1 - core)
    )


def by_side(values):
    spots = LINE * ROWS
    return values.reshape(2, spots, values.shape[0] // (2 * spots), values.shape[1])


def side_sum(values, side):
    return added(one_of(values, side, 0), exchange(one_of(values, 1 - side, 0)))


def owner_last(values):
    groups = [[spot * CORES + core for spot in range(LINE * ROWS)] for core in range(CORES)]
    values = lax.all_to_all(
        values, "ctx", split_axis=0, concat_axis=0, tiled=True, axis_index_groups=groups
    )
    return jnp.sum(values.astype(jnp.float32), axis=0)


def exchange(values):
    return lax.ppermute(values, "dp", [(0, 1), (1, 0)])


def to_heads(values):
    return lax.all_to_all(values, "ctx", split_axis=0, concat_axis=0, tiled=True)


def turn(values, cosine, sine):
    half = HD // 2
    first, second = values[:, :half, :], values[:, half:, :]
    return jnp.concatenate(
        [first * cosine - second * sine, second * cosine + first * sine], axis=1
    )


def per_device(
    tokens, grad_out, w_query, w_key, w_value, w_output, gain_attn, gain_ffn, w_router, w_experts,
    deal_table, routes
):
    row_count = tokens.shape[0]
    devices = lax.axis_size("ctx")
    position = lax.axis_index("ctx")
    side = lax.axis_index("dp")
    both = ("dp", "ctx")
    shard = w_query.shape[0]
    wide = HQ * HD
    narrow = KVH * HD

    extras = jnp.concatenate(
        [w_router, gain_attn[:, None], gain_ffn[:, None], jnp.zeros((shard, 94), jnp.bfloat16)],
        axis=1,
    )
    packed_weights = lax.all_gather(
        jnp.concatenate([w_query, w_key, w_value, extras, w_output], axis=1),
        both,
        axis=0,
        tiled=True,
    )
    other_experts = exchange(w_experts)
    local = w_experts.shape[2] // F
    line_place = position // (ROWS * CORES)
    order = near_order(position)

    g_ups, g_downs, g_across, g_own = [grad_out], [grad_out], [], [grad_out]
    for s in range(3):
        sent = send_on(s, g_own[s], g_ups[s], g_downs[s])
        if s == 1:
            packed_weights, *sent = together((packed_weights, *sent))
        elif s == 0:
            sent = together(tuple(sent))
        else:
            step_2 = sent
        g_across.append(sent[0])
        g_ups.append(sent[1])
        g_downs.append(sent[2])
        g_own.append(newest(s + 1, g_ups, g_downs, line_place))

    full_qkv = packed_weights[:, : wide + 2 * narrow]
    extra_columns = packed_weights[:, wide + 2 * narrow : wide + 2 * narrow + 128]
    full_output = packed_weights[:, wide + 2 * narrow + 128 :]
    full_router = extra_columns[:, :E]
    gain_attn_full = extra_columns[:, E].astype(jnp.float32)
    gain_ffn_full = extra_columns[:, E + 1].astype(jnp.float32)

    expert_ids = jnp.arange(E, dtype=jnp.int32)
    picked = routes[:, :, None] == expert_ids[None, None, :]
    member = jnp.any(picked, axis=1)
    below = (jnp.arange(row_count)[:, None] > jnp.arange(row_count)[None, :]).astype(jnp.bfloat16)
    before = nn(below, member.astype(jnp.bfloat16))
    places = jnp.where(member, before, -1.0)
    slot_places = to_heads(places.T.reshape(devices, local, row_count))

    group_blocks = deal_table[0]
    own_blocks = lax.dynamic_slice_in_dim(group_blocks, 2 * position, 2)
    offsets = jnp.arange(BLK, dtype=jnp.int32)
    positions = ((own_blocks % BLOCKS)[:, None] * BLK + offsets[None, :]).reshape(-1)
    core = position % CORES
    table = jnp.concatenate([jnp.argsort(group_blocks).astype(jnp.int32), core.reshape(1)])
    frequency = 10000.0 ** (-(jnp.arange(HD // 2).astype(jnp.float32) * 2.0 / HD))
    angles = frequency[:, None] * positions.astype(jnp.float32)[None, :]
    cosine, sine = jnp.cos(angles)[None], jnp.sin(angles)[None]
    inputs = tokens.astype(jnp.float32)
    normed = rms_norm(inputs, gain_attn_full).astype(jnp.bfloat16)
    normed_near, normed_far = halves(normed, core, 1)
    raw = tt(full_qkv, normed)
    queries = turn(raw[:wide].reshape(HQ, HD, row_count), cosine, sine).astype(jnp.bfloat16)
    keys = turn(raw[wide : wide + narrow].reshape(KVH, HD, row_count), cosine, sine).astype(
        jnp.bfloat16
    )
    values = raw[wide + narrow :].reshape(KVH, HD, row_count).astype(jnp.bfloat16)
    pairs = jnp.stack([keys, values], axis=1).reshape(HQ, HD, row_count)
    outgoing = jnp.concatenate([queries, pairs], axis=1)
    outgoing, other_experts, slot_places, *step_2 = together(
        (outgoing, other_experts, slot_places, *step_2)
    )
    packed = to_heads(outgoing)
    g_across[2], g_ups[3], g_downs[3] = step_2
    g_own[3] = newest(3, g_ups, g_downs, line_place)
    slot_columns = slot_places.transpose(0, 2, 1)
    first_half = jnp.where(side == 0, w_experts, other_experts)
    second_half = jnp.where(side == 0, other_experts, w_experts)
    experts = jnp.concatenate([first_half, second_half], axis=1)
    g_kept, g_first = None, 0
    for s in range(LINE + 1):
        if s == LINE:
            packed, g_own[3], *g_kept = together((packed, g_own[3], *g_kept))
            other_packed = core_swap(packed)
            g_across.append(row_swap(g_own[3]))
            heads, attended_rows, log_sum = attention_forward(table, packed, other_packed)
            heads, g_across[3] = together((heads, g_across[3]))
            attended = to_heads(heads)
        blocks = g_own[s : s + 1] + (g_across[s - 1 : s] if s else [])
        blocks += [core_swap(b) for b in blocks]
        count = len(blocks)
        g_kept = grad_step(
            g_first, order[g_first : g_first + count], slot_places, blocks, experts, g_kept
        )
        g_first += count
    attended, *g_kept = together((attended, *g_kept))
    attended = attended.reshape(wide, row_count)
    slot_grads, d_hidden = g_kept
    residual = inputs + tn(attended, full_output)

    normed_ffn = rms_norm(residual, gain_ffn_full).astype(jnp.bfloat16)
    logits = nn(normed_ffn, full_router)
    masked = jnp.where(member, logits, floor_value)
    powers = jnp.where(member, jnp.exp(masked - jnp.max(masked, axis=1, keepdims=True)), 0.0)
    gates = powers / jnp.sum(powers, axis=1, keepdims=True)
    slot_gates = to_heads(gates.T.reshape(devices, local, row_count))
    summed, d_gate_parts, kept = [], [], None
    own, across = normed_ffn, None
    ups, downs = [normed_ffn], [normed_ffn]
    first = 0
    for s in range(LINE + 1):
        blocks = [b for b in (own, across) if b is not None]
        sent = send_on(s, own, ups[-1], downs[-1])
        blocks += [core_swap(b) for b in blocks]
        count = len(blocks)
        *kept, d_gate_part, near_part, far_part = expert_step(
            first, order[first : first + count], slot_places, slot_gates, blocks, d_hidden,
            experts, kept
        )
        if sent and summed:
            *sent, near_part, summed[-1] = together((*sent, near_part, summed[-1]))
        elif sent:
            *sent, near_part = together((*sent, near_part))
        first += count
        summed.append(added(near_part, core_swap(far_part)))
        d_gate_parts.append(d_gate_part)
        across = sent[0] if s < LINE else None
        if s < LINE - 1:
            ups.append(sent[1])
            downs.append(sent[2])
        own = newest(s + 1, ups, downs, line_place) if s < LINE - 1 else None
    slot_rows, hidden, d_gate_pre, d_up = kept
    arrived = scatter_sum(summed, line_place)
    given = weight_grad(
        (1 - side).reshape(1), slot_rows, slot_grads, d_gate_pre, d_up, hidden, jnp.bfloat16
    )
    taken = [exchange(part) for part in given]
    out_rows = output_pass(order, slot_columns, hidden, experts)
    owned_experts = weight_grad(
        side.reshape(1), slot_rows, slot_grads, d_gate_pre, d_up, hidden, jnp.float32
    )
    back = jnp.argsort(order)
    d_gate = to_heads(jnp.concatenate(d_gate_parts, axis=0)[back])
    *arrived, out_rows, taken[0], taken[1], owned_experts, d_gate = together(
        (*arrived, out_rows, taken[0], taken[1], owned_experts, d_gate)
    )
    d_gate = d_gate.reshape(E, row_count).T
    ffn_grad = sum(part.astype(jnp.float32) for part in arrived)
    mixture = lax.psum_scatter(out_rows, "ctx", scatter_dimension=0, tiled=True)

    d_logits = gates * (d_gate - jnp.sum(gates * d_gate, axis=1, keepdims=True))
    ffn_grad = ffn_grad + jnp.einsum(
        "re,de->rd", d_logits, full_router.astype(jnp.float32), precision=highest
    )
    router_grad = jnp.einsum(
        "rd,re->de", normed_ffn.astype(jnp.float32), d_logits, precision=highest
    )
    _, norm_back_ffn = jax.vjp(rms_norm, residual, gain_ffn_full)
    residual_norm_grad, gain_ffn_grad = norm_back_ffn(ffn_grad)
    residual_grad = grad_out.astype(jnp.float32) + residual_norm_grad
    branch_grad = residual_grad.astype(jnp.bfloat16)
    attended_grad = nt(full_output, branch_grad).astype(jnp.bfloat16)
    d_heads = to_heads(attended_grad.reshape(HQ, HD, row_count))
    output_grad = jnp.concatenate(
        [
            nn(attended, branch_grad).astype(jnp.bfloat16),
            router_grad.astype(jnp.bfloat16),
            gain_ffn_grad[:, None].astype(jnp.bfloat16),
            jnp.zeros((D, 95), jnp.bfloat16),
        ],
        axis=1,
    )
    first_near, first_far = halves(output_grad, core, 0)
    first_parts = by_side(added(first_near, core_swap(first_far)))
    d_heads, first_parts = together((d_heads, first_parts))
    first_taken = exchange(one_of(first_parts, 1 - side, 0))

    q_grads, kept_grads, given_grads = attention_backward(
        table, packed, other_packed, d_heads, attended_rows, log_sum
    )
    q_grads, first_taken, taken[2] = together((q_grads, first_taken, taken[2]))
    q_back = to_heads(q_grads)
    pair_grads = added(kept_grads, core_swap(given_grads))
    q_back, pair_grads = together((q_back, pair_grads))
    pair_back = to_heads(pair_grads)
    d_query = (
        turn(q_back.astype(jnp.float32), cosine, -sine)
        .astype(jnp.bfloat16)
        .reshape(wide, row_count)
    )
    far_grad = core_swap(tt(normed_far, d_query).astype(jnp.bfloat16))
    near_grad = tt(normed_near, d_query).astype(jnp.bfloat16)
    query_parts = side_sum(by_side(added(near_grad, far_grad)), side)
    query_parts = jnp.concatenate(
        [query_parts, added(one_of(first_parts, side, 0), first_taken)], axis=2
    )
    pair_back, query_parts = together((pair_back, query_parts))
    query_owned = owner_last(query_parts)
    pairs = pair_back.astype(jnp.float32).reshape(KVH, 2, HD, row_count)
    d_pairs = jnp.concatenate(
        [
            turn(pairs[:, 0], cosine, -sine).astype(jnp.bfloat16),
            pairs[:, 1].astype(jnp.bfloat16),
        ],
        axis=0,
    ).reshape(2 * narrow, row_count)
    far_grad = core_swap(tt(normed_far, d_pairs).astype(jnp.bfloat16))
    near_grad = tt(normed_near, d_pairs).astype(jnp.bfloat16)
    normed_grad = tt(d_query, full_qkv[:, :wide]) + tt(d_pairs, full_qkv[:, wide:])
    pair_parts = side_sum(by_side(added(near_grad, far_grad)), side)
    _, norm_back_attn = jax.vjp(rms_norm, inputs, gain_attn_full)
    input_norm_grad, gain_attn_grad = norm_back_attn(normed_grad)
    tokens_grad = residual_grad + input_norm_grad
    gain_near, gain_far = halves(gain_attn_grad[:, None].astype(jnp.bfloat16), core, 0)
    gain_parts = side_sum(by_side(added(gain_near, core_swap(gain_far))), side)
    pair_owned = owner_last(
        jnp.concatenate(
            [pair_parts, gain_parts, jnp.zeros((*gain_parts.shape[:2], 127), jnp.bfloat16)],
            axis=2,
        )
    )
    mixture, late = together((mixture, d_query))
    mixed = (residual + mixture.astype(jnp.float32)).astype(jnp.bfloat16)
    expert_grad = jnp.stack(
        [mine + part.astype(jnp.float32) for mine, part in zip(owned_experts, taken)]
    )
    return (
        mixed,
        tokens_grad,
        query_owned[:, :wide],
        pair_owned[:, :narrow],
        pair_owned[:, narrow : 2 * narrow],
        query_owned[:, wide : wide + D],
        pair_owned[:, 2 * narrow],
        query_owned[:, wide + D + E],
        query_owned[:, wide + D : wide + D + E],
        expert_grad,
    )


def solution(mesh):
    in_specs = (
        P(("dp", "ctx"), None),
        P(("dp", "ctx"), None),
        P(("dp", "ctx"), None),
        P(("dp", "ctx"), None),
        P(("dp", "ctx"), None),
        P(("dp", "ctx"), None),
        P(("dp", "ctx")),
        P(("dp", "ctx")),
        P(("dp", "ctx"), None),
        P(None, "dp", "ctx"),
        P("dp", None),
        P(("dp", "ctx"), None),
    )
    out_specs = (
        P(("dp", "ctx"), None),
        P(("dp", "ctx"), None),
        P(("dp", "ctx"), None),
        P(("dp", "ctx"), None),
        P(("dp", "ctx"), None),
        P(("dp", "ctx"), None),
        P(("dp", "ctx")),
        P(("dp", "ctx")),
        P(("dp", "ctx"), None),
        P(None, "dp", "ctx"),
    )
    body = per_device if mesh.shape["ctx"] == HQ else general_device
    return jax.shard_map(
        body, mesh=mesh, in_specs=in_specs, out_specs=out_specs, check_vma=False
    )
```

```python
from functools import partial

import jax
import jax.numpy as jnp
from jax import lax
from jax.experimental import pallas as pl
from jax.experimental.pallas import tpu as pltpu
from jax.sharding import PartitionSpec as P

D = 1024
HQ = 16
KVH = 8
HD = 64
E = 32
F = 512
TOPK = 8
BLK = 256
BLOCKS = 16
CAP = 160


epsilon = 1e-06
highest = lax.Precision.HIGHEST
floor_value = -1e30


def rms_norm(values, gain):
    return values * lax.rsqrt(jnp.mean(values * values, axis=-1, keepdims=True) + epsilon) * gain


def rotary(values, positions):
    half_size = values.shape[-1] // 2
    frequency = 10000.0 ** (-(jnp.arange(half_size).astype(jnp.float32) * 2.0 / values.shape[-1]))
    angles = positions.astype(jnp.float32)[:, None] * frequency[None, :]
    cosine = jnp.cos(angles)[:, None, :]
    sine_part = jnp.sin(angles)[:, None, :]
    first_half = values[..., :half_size]
    second = values[..., half_size:]
    return jnp.concatenate(
        [first_half * cosine - second * sine_part, second * cosine + first_half * sine_part],
        axis=-1,
    )


def heads_major(block_rows, groups, head_ratio, head_size):
    count = block_rows.shape[0]
    shaped = block_rows.reshape(count, groups, head_ratio, head_size).transpose(1, 2, 0, 3)
    return shaped.reshape(groups, head_ratio * count, head_size)


def rows_major(blocked, groups, head_ratio, head_size):
    count = blocked.shape[1] // head_ratio
    shaped = blocked.reshape(groups, head_ratio, count, head_size).transpose(2, 0, 1, 3)
    return shaped.reshape(count, groups * head_ratio * head_size)


def stats_major(block_rows, groups, head_ratio):
    count = block_rows.shape[0]
    return (
        block_rows.reshape(count, groups, head_ratio)
        .transpose(1, 2, 0)
        .reshape(groups, head_ratio * count)
    )


def pair_blocks(rows, base, groups, head_ratio, head_size):
    return jnp.stack(
        [
            heads_major(lax.dynamic_slice_in_dim(rows, base + i * BLK, BLK), groups, head_ratio, head_size)
            for i in range(2)
        ]
    )


def pair_order(block_pair, per_seq):
    places = block_pair % per_seq
    lower_slot = (places[0] > places[1]).astype(jnp.int32)
    return (lower_slot, 1 - lower_slot, jnp.minimum(places[0], places[1]), block_pair[0] // per_seq)


def keep_state(carry_state):
    return carry_state


def forward_update(query_block, key_block, value_block, slot_number, score_scale):

    def forward_apply_update(carry_state):
        running_max, running_sum, accumulated = carry_state
        scores = (
            jnp.einsum("gqd,gkd->gqk", query_block, key_block, preferred_element_type=jnp.float32)
            * score_scale
        )
        new_max = jnp.maximum(running_max[slot_number], jnp.max(scores, axis=-1))
        factor = jnp.exp(running_max[slot_number] - new_max)
        weights = jnp.exp(scores - new_max[..., None])
        new_sum = running_sum[slot_number] * factor + jnp.sum(weights, axis=-1)
        product = jnp.einsum(
            "gqk,gkd->gqd",
            weights.astype(jnp.bfloat16),
            value_block,
            preferred_element_type=jnp.float32,
        )
        new_acc = accumulated[slot_number] * factor[..., None] + product
        return (
            running_max.at[slot_number].set(new_max),
            running_sum.at[slot_number].set(new_sum),
            accumulated.at[slot_number].set(new_acc),
        )

    return forward_apply_update


def query_update(
    query_block,
    grad_block,
    log_block,
    delta_block,
    key_block,
    value_block,
    slot_number,
    score_scale,
):

    def query_apply_update(accumulated):
        scores = (
            jnp.einsum("gqd,gkd->gqk", query_block, key_block, preferred_element_type=jnp.float32)
            * score_scale
        )
        probs_full = jnp.exp(scores - log_block[..., None])
        prob_grad = jnp.einsum(
            "gqd,gkd->gqk", grad_block, value_block, preferred_element_type=jnp.float32
        )
        score_grad = (probs_full * (prob_grad - delta_block[..., None])).astype(jnp.bfloat16)
        change = (
            jnp.einsum("gqk,gkd->gqd", score_grad, key_block, preferred_element_type=jnp.float32)
            * score_scale
        )
        return accumulated.at[slot_number].add(change)

    return query_apply_update


def key_update(
    query_block,
    grad_block,
    log_block,
    delta_block,
    key_block,
    value_block,
    slot_number,
    score_scale,
):

    def key_apply_update(carry_state):
        key_accum, value_accum = carry_state
        scores = (
            jnp.einsum("gqd,gkd->gqk", query_block, key_block, preferred_element_type=jnp.float32)
            * score_scale
        )
        probs_full = jnp.exp(scores - log_block[..., None])
        value_change = jnp.einsum(
            "gqk,gqd->gkd",
            probs_full.astype(jnp.bfloat16),
            grad_block,
            preferred_element_type=jnp.float32,
        )
        prob_grad = jnp.einsum(
            "gqd,gkd->gqk", grad_block, value_block, preferred_element_type=jnp.float32
        )
        score_grad = (probs_full * (prob_grad - delta_block[..., None])).astype(jnp.bfloat16)
        key_change = (
            jnp.einsum("gqk,gqd->gkd", score_grad, query_block, preferred_element_type=jnp.float32)
            * score_scale
        )
        return (
            key_accum.at[slot_number].add(key_change),
            value_accum.at[slot_number].add(value_change),
        )

    return key_apply_update


def expert_forward(routed_rows, weights_local):
    gate_pre = jnp.einsum(
        "erd,def->erf", routed_rows, weights_local[0], preferred_element_type=jnp.float32
    )
    up_pre = jnp.einsum(
        "erd,def->erf", routed_rows, weights_local[1], preferred_element_type=jnp.float32
    )
    hidden = (jax.nn.silu(gate_pre) * up_pre).astype(jnp.bfloat16)
    return (gate_pre, up_pre, hidden)


def natural_return(partials, split_count):
    devices = partials.shape[0]
    arrived = lax.all_to_all(partials, "ctx", split_axis=0, concat_axis=0, tiled=True)
    shaped = arrived.reshape(
        devices * partials.shape[1] // split_count,
        split_count,
        partials.shape[2],
        partials.shape[3],
    )
    return jnp.sum(shaped, axis=1)


def send_back(partials, split_count):
    return natural_return(partials, split_count)


def spread_slots(slot_values, devices, local_count, split_count):
    width = slot_values.shape[-1]
    return jnp.broadcast_to(
        slot_values.reshape(E, 1, CAP, width), (E, split_count, CAP, width)
    ).reshape(devices, local_count, CAP, width)


def general_device(
    tokens,
    grad_out,
    w_query,
    w_key,
    w_value,
    w_output,
    gain_attn,
    gain_ffn,
    w_router,
    w_experts,
    deal_table,
    routes,
):
    row_count = tokens.shape[0]
    head_ratio = HQ // KVH
    score_scale = HD ** (-0.5)
    full_query, full_key, full_value, full_output, full_router, full_gain_attn, full_gain_ffn = (
        lax.all_gather(w_query, ("dp", "ctx"), axis=0, tiled=True),
        lax.all_gather(w_key, ("dp", "ctx"), axis=0, tiled=True),
        lax.all_gather(w_value, ("dp", "ctx"), axis=0, tiled=True),
        lax.all_gather(w_output, ("dp", "ctx"), axis=0, tiled=True),
        lax.all_gather(w_router, ("dp", "ctx"), axis=0, tiled=True),
        lax.all_gather(gain_attn, ("dp", "ctx"), axis=0, tiled=True),
        lax.all_gather(gain_ffn, ("dp", "ctx"), axis=0, tiled=True),
    )
    experts_local = lax.all_gather(w_experts, "dp", axis=1, tiled=True)
    columns = experts_local.shape[2]
    unit_width = min(F, columns)
    local_count = columns // unit_width
    split_count = F // unit_width
    devices = lax.axis_size("ctx")
    position = lax.axis_index("ctx")
    group_blocks = deal_table[0]
    per_seq = BLOCKS
    own_blocks = lax.dynamic_slice_in_dim(group_blocks, 2 * position, 2)
    query_low, query_high, low_place, own_seq = pair_order(own_blocks, per_seq)
    offsets = jnp.arange(BLK, dtype=jnp.int32)
    positions = ((own_blocks % per_seq)[:, None] * BLK + offsets[None, :]).reshape(-1)
    inputs = tokens.astype(jnp.float32)
    gain_attn_full = full_gain_attn.astype(jnp.float32)
    gain_ffn_full = full_gain_ffn.astype(jnp.float32)
    normed = rms_norm(inputs, gain_attn_full).astype(jnp.bfloat16)
    query_raw = jnp.dot(normed, full_query, preferred_element_type=jnp.float32).reshape(
        row_count, HQ, HD
    )
    key_raw = jnp.dot(normed, full_key, preferred_element_type=jnp.float32).reshape(
        row_count, KVH, HD
    )
    value_raw = jnp.dot(normed, full_value, preferred_element_type=jnp.float32)
    queries = rotary(query_raw, positions).astype(jnp.bfloat16).reshape(row_count, HQ * HD)
    key_proj = rotary(key_raw, positions).astype(jnp.bfloat16).reshape(row_count, KVH * HD)
    value_proj = value_raw.astype(jnp.bfloat16)
    query_heads = pair_blocks(queries, 0, KVH, head_ratio, HD)
    key_heads = pair_blocks(key_proj, 0, KVH, 1, HD)
    value_heads = pair_blocks(value_proj, 0, KVH, 1, HD)
    score_rows = head_ratio * BLK
    initial = (
        jnp.full((2, KVH, score_rows), floor_value, jnp.float32),
        jnp.zeros((2, KVH, score_rows), jnp.float32),
        jnp.zeros((2, KVH, score_rows, HD), jnp.float32),
    )
    initial = forward_update(
        query_heads[query_low], key_heads[query_low], value_heads[query_low], query_low, score_scale
    )(initial)
    carry_state = initial
    key_rows = lax.all_gather(key_proj, "ctx", axis=0, tiled=True)
    value_rows = lax.all_gather(value_proj, "ctx", axis=0, tiled=True)
    def forward_step(j, carry_state):
        key_pair = pair_blocks(key_rows, j * 2 * BLK, KVH, 1, HD)
        value_pair = pair_blocks(value_rows, j * 2 * BLK, KVH, 1, HD)
        block_pair = lax.dynamic_slice_in_dim(group_blocks, 2 * j, 2)
        key_low, key_high, key_place, key_seq = pair_order(block_pair, per_seq)
        same = key_seq == own_seq
        carry_state = lax.cond(
            same,
            forward_update(
                query_heads[query_high],
                key_pair[key_low],
                value_pair[key_low],
                query_high,
                score_scale,
            ),
            keep_state,
            carry_state,
        )
        below = key_place < low_place
        pick_query = jnp.where(below, query_low, query_high)
        pick_key = jnp.where(below, key_low, key_high)
        carry_state = lax.cond(
            same,
            forward_update(
                query_heads[pick_query],
                key_pair[pick_key],
                value_pair[pick_key],
                pick_query,
                score_scale,
            ),
            keep_state,
            carry_state,
        )
        return carry_state

    carry_state = lax.fori_loop(0, key_rows.shape[0] // (2 * BLK), forward_step, carry_state)
    running_max, running_sum, accumulated = carry_state
    attended_heads = accumulated / running_sum[..., None]
    log_total = running_max + jnp.log(running_sum)
    attended_rows = jnp.concatenate(
        [rows_major(attended_heads[i], KVH, head_ratio, HD) for i in range(2)], axis=0
    )
    attended_low = attended_rows.astype(jnp.bfloat16)
    residual = inputs + jnp.dot(attended_low, full_output, preferred_element_type=jnp.float32)
    normed_ffn = rms_norm(residual, gain_ffn_full).astype(jnp.bfloat16)
    expert_ids = jnp.arange(E, dtype=jnp.int32)
    picked = routes[:, :, None] == expert_ids[None, None, :]
    ffn_float = normed_ffn.astype(jnp.float32)
    router_full = full_router.astype(jnp.float32)
    logits = jnp.dot(ffn_float, router_full, precision=highest)
    chosen = jnp.sum(jnp.where(picked, logits[:, None, :], 0.0), axis=2)
    gate_weights = jax.nn.softmax(chosen, axis=-1)
    member = jnp.sum(picked.astype(jnp.int32), axis=1)
    before = jnp.cumsum(member, axis=0) - member
    slot_numbers = jnp.sum(jnp.where(picked, before[:, None, :], 0), axis=2)
    flat_slot = (routes * CAP + slot_numbers).reshape(-1)
    owner_rows = (
        jnp.zeros((E * CAP,), jnp.int32)
        .at[flat_slot]
        .set(jnp.repeat(jnp.arange(1, row_count + 1, dtype=jnp.int32), TOPK))
    )
    slot_gate = jnp.zeros((E * CAP,), jnp.float32).at[flat_slot].set(gate_weights.reshape(-1))
    padded_rows = jnp.concatenate([jnp.zeros((1, D), jnp.bfloat16), normed_ffn], axis=0)
    slot_rows = padded_rows[owner_rows]
    outgoing = spread_slots(slot_rows, devices, local_count, split_count)
    arrived = lax.all_to_all(outgoing, "ctx", split_axis=0, concat_axis=0, tiled=True)
    routed_rows = arrived.transpose(1, 0, 2, 3).reshape(local_count, devices * outgoing.shape[2], D)
    weights_local = experts_local.reshape(3, D, local_count, unit_width)
    gate_pre, up_pre, hidden = expert_forward(routed_rows, weights_local)
    expert_out = jnp.einsum(
        "erf,def->erd", hidden, weights_local[2], preferred_element_type=jnp.float32
    )
    combined = send_back(
        expert_out.reshape(local_count, devices, outgoing.shape[2], D).transpose(1, 0, 2, 3),
        split_count,
    )
    routed_out = combined.reshape(E * CAP, D)[flat_slot].reshape(row_count, TOPK, D)
    mixed = (residual + jnp.sum(gate_weights[:, :, None] * routed_out, axis=1)).astype(jnp.bfloat16)
    upstream = grad_out.astype(jnp.float32)
    gate_grad = jnp.sum(routed_out * upstream[:, None, :], axis=2)
    chosen_grad = gate_weights * (
        gate_grad - jnp.sum(gate_weights * gate_grad, axis=1, keepdims=True)
    )
    logits_grad = jnp.sum(jnp.where(picked, chosen_grad[:, :, None], 0.0), axis=1)
    padded_grad = jnp.concatenate([jnp.zeros((1, D), jnp.float32), upstream], axis=0)
    slot_grad = (padded_grad[owner_rows] * slot_gate[:, None]).astype(jnp.bfloat16)
    outgoing_grad = spread_slots(slot_grad, devices, local_count, split_count)
    arrived_grad = lax.all_to_all(outgoing_grad, "ctx", split_axis=0, concat_axis=0, tiled=True)
    grad_rows = arrived_grad.transpose(1, 0, 2, 3).reshape(
        local_count, devices * outgoing.shape[2], D
    )
    hidden_grad = jnp.einsum(
        "erd,def->erf", grad_rows, weights_local[2], preferred_element_type=jnp.float32
    )
    sigmoid = jax.nn.sigmoid(gate_pre)
    up_grad = (hidden_grad * gate_pre * sigmoid).astype(jnp.bfloat16)
    gate_pre_grad = (hidden_grad * up_pre * sigmoid * (1.0 + gate_pre * (1.0 - sigmoid))).astype(
        jnp.bfloat16
    )
    weight_grad = jnp.stack(
        [
            jnp.einsum(
                "erd,erf->def", routed_rows, gate_pre_grad, preferred_element_type=jnp.float32
            ),
            jnp.einsum("erd,erf->def", routed_rows, up_grad, preferred_element_type=jnp.float32),
            jnp.einsum("erd,erf->def", grad_rows, hidden, preferred_element_type=jnp.float32),
        ]
    ).reshape(3, D, local_count * unit_width)
    input_grad = jnp.einsum(
        "erf,def->erd", gate_pre_grad, weights_local[0], preferred_element_type=jnp.float32
    )
    input_grad = input_grad + jnp.einsum(
        "erf,def->erd", up_grad, weights_local[1], preferred_element_type=jnp.float32
    )
    returned = send_back(
        input_grad.reshape(local_count, devices, outgoing.shape[2], D).transpose(1, 0, 2, 3),
        split_count,
    )
    ffn_grad = jnp.sum(returned.reshape(E * CAP, D)[flat_slot].reshape(row_count, TOPK, D), axis=1)
    ffn_grad = ffn_grad + jnp.einsum("re,de->rd", logits_grad, router_full, precision=highest)
    router_grad = jnp.einsum("rd,re->de", ffn_float, logits_grad, precision=highest)
    expert_grad = lax.psum_scatter(weight_grad, "dp", scatter_dimension=1, tiled=True)
    _, norm_back_ffn = jax.vjp(rms_norm, residual, gain_ffn_full)
    residual_norm_grad, gain_ffn_grad = norm_back_ffn(ffn_grad)
    residual_grad = upstream + residual_norm_grad
    branch_grad = residual_grad.astype(jnp.bfloat16)
    output_grad = jnp.einsum(
        "rc,rd->cd", attended_low, branch_grad, preferred_element_type=jnp.float32
    )
    attended_grad = jnp.einsum(
        "rd,cd->rc", branch_grad, full_output, preferred_element_type=jnp.float32
    ).astype(jnp.bfloat16)
    delta_rows = jnp.sum(
        (attended_grad.astype(jnp.float32) * attended_rows).reshape(row_count, HQ, HD), axis=-1
    )
    delta_heads = jnp.stack(
        [stats_major(delta_rows[i * BLK : (i + 1) * BLK], KVH, head_ratio) for i in range(2)]
    )
    grad_heads = pair_blocks(attended_grad, 0, KVH, head_ratio, HD)
    all_log, all_delta = (
        lax.all_gather(log_total, "ctx", axis=0, tiled=True),
        lax.all_gather(delta_heads, "ctx", axis=0, tiled=True),
    )
    query_start = query_update(
        query_heads[query_low],
        grad_heads[query_low],
        log_total[query_low],
        delta_heads[query_low],
        key_heads[query_low],
        value_heads[query_low],
        query_low,
        score_scale,
    )(jnp.zeros((2, KVH, score_rows, HD), jnp.float32))
    accumulated_grad = query_start
    key_rows = lax.all_gather(key_proj, "ctx", axis=0, tiled=True)
    value_rows = lax.all_gather(value_proj, "ctx", axis=0, tiled=True)
    def query_step(j, accumulated_grad):
        key_pair = pair_blocks(key_rows, j * 2 * BLK, KVH, 1, HD)
        value_pair = pair_blocks(value_rows, j * 2 * BLK, KVH, 1, HD)
        block_pair = lax.dynamic_slice_in_dim(group_blocks, 2 * j, 2)
        key_low, key_high, key_place, key_seq = pair_order(block_pair, per_seq)
        same = key_seq == own_seq
        first = query_update(
            query_heads[query_high],
            grad_heads[query_high],
            log_total[query_high],
            delta_heads[query_high],
            key_pair[key_low],
            value_pair[key_low],
            query_high,
            score_scale,
        )
        accumulated_grad = lax.cond(same, first, keep_state, accumulated_grad)
        below = key_place < low_place
        pick_query = jnp.where(below, query_low, query_high)
        pick_key = jnp.where(below, key_low, key_high)
        second_update = query_update(
            query_heads[pick_query],
            grad_heads[pick_query],
            log_total[pick_query],
            delta_heads[pick_query],
            key_pair[pick_key],
            value_pair[pick_key],
            pick_query,
            score_scale,
        )
        accumulated_grad = lax.cond(same, second_update, keep_state, accumulated_grad)
        return accumulated_grad

    accumulated_grad = lax.fori_loop(0, key_rows.shape[0] // (2 * BLK), query_step, accumulated_grad)
    zero_keys = jnp.zeros((2, KVH, BLK, HD), jnp.float32)
    key_start = key_update(
        query_heads[query_low],
        grad_heads[query_low],
        log_total[query_low],
        delta_heads[query_low],
        key_heads[query_low],
        value_heads[query_low],
        query_low,
        score_scale,
    )((zero_keys, zero_keys))
    carry_state = key_start
    start_row = jnp.int32(0)
    query_rows = lax.all_gather(queries, "ctx", axis=0, tiled=True)
    grad_piece = lax.all_gather(attended_grad, "ctx", axis=0, tiled=True)
    def key_step(j, carry_state):
        slot_first = start_row // BLK + 2 * j
        query_pair = pair_blocks(query_rows, j * 2 * BLK, KVH, head_ratio, HD)
        grad_pair = pair_blocks(grad_piece, j * 2 * BLK, KVH, head_ratio, HD)
        block_pair = lax.dynamic_slice_in_dim(group_blocks, slot_first, 2)
        log_pair = lax.dynamic_slice_in_dim(all_log, slot_first, 2)
        delta_pair = lax.dynamic_slice_in_dim(all_delta, slot_first, 2)
        remote_low, remote_high, remote_place, remote_seq = pair_order(block_pair, per_seq)
        same = remote_seq == own_seq
        first = key_update(
            query_pair[remote_high],
            grad_pair[remote_high],
            log_pair[remote_high],
            delta_pair[remote_high],
            key_heads[query_low],
            value_heads[query_low],
            query_low,
            score_scale,
        )
        carry_state = lax.cond(same, first, keep_state, carry_state)
        below = low_place < remote_place
        pick_remote = jnp.where(below, remote_low, remote_high)
        pick_own = jnp.where(below, query_low, query_high)
        second_update = key_update(
            query_pair[pick_remote],
            grad_pair[pick_remote],
            log_pair[pick_remote],
            delta_pair[pick_remote],
            key_heads[pick_own],
            value_heads[pick_own],
            pick_own,
            score_scale,
        )
        carry_state = lax.cond(same, second_update, keep_state, carry_state)
        return carry_state

    carry_state = lax.fori_loop(0, query_rows.shape[0] // (2 * BLK), key_step, carry_state)
    key_grad_heads, value_grad_heads = carry_state
    query_grad_rows = jnp.concatenate(
        [rows_major(accumulated_grad[i], KVH, head_ratio, HD) for i in range(2)], axis=0
    )
    key_grad_rows = jnp.concatenate(
        [rows_major(key_grad_heads[i], KVH, 1, HD) for i in range(2)], axis=0
    )
    value_grad_rows = jnp.concatenate(
        [rows_major(value_grad_heads[i], KVH, 1, HD) for i in range(2)], axis=0
    )
    _, query_rot_back = jax.vjp(partial(rotary, positions=positions), query_raw)
    _, key_rot_back = jax.vjp(partial(rotary, positions=positions), key_raw)
    query_proj_grad = (
        query_rot_back(query_grad_rows.reshape(row_count, HQ, HD))[0]
        .reshape(row_count, HQ * HD)
        .astype(jnp.bfloat16)
    )
    key_proj_grad = (
        key_rot_back(key_grad_rows.reshape(row_count, KVH, HD))[0]
        .reshape(row_count, KVH * HD)
        .astype(jnp.bfloat16)
    )
    value_proj_grad = value_grad_rows.astype(jnp.bfloat16)
    query_weight_grad = jnp.einsum(
        "rd,rc->dc", normed, query_proj_grad, preferred_element_type=jnp.float32
    )
    key_weight_grad = jnp.einsum(
        "rd,rc->dc", normed, key_proj_grad, preferred_element_type=jnp.float32
    )
    value_weight_grad = jnp.einsum(
        "rd,rc->dc", normed, value_proj_grad, preferred_element_type=jnp.float32
    )
    normed_grad = jnp.einsum(
        "rc,dc->rd", query_proj_grad, full_query, preferred_element_type=jnp.float32
    )
    normed_grad = normed_grad + jnp.einsum(
        "rc,dc->rd", key_proj_grad, full_key, preferred_element_type=jnp.float32
    )
    normed_grad = normed_grad + jnp.einsum(
        "rc,dc->rd", value_proj_grad, full_value, preferred_element_type=jnp.float32
    )
    _, norm_back_attn = jax.vjp(rms_norm, inputs, gain_attn_full)
    input_norm_grad, gain_attn_grad = norm_back_attn(normed_grad)
    tokens_grad = residual_grad + input_norm_grad
    owned = (
        lax.psum_scatter(query_weight_grad, ("dp", "ctx"), scatter_dimension=0, tiled=True),
        lax.psum_scatter(key_weight_grad, ("dp", "ctx"), scatter_dimension=0, tiled=True),
        lax.psum_scatter(value_weight_grad, ("dp", "ctx"), scatter_dimension=0, tiled=True),
        lax.psum_scatter(output_grad, ("dp", "ctx"), scatter_dimension=0, tiled=True),
        lax.psum_scatter(router_grad, ("dp", "ctx"), scatter_dimension=0, tiled=True),
        lax.psum_scatter(gain_attn_grad, ("dp", "ctx"), scatter_dimension=0, tiled=True),
        lax.psum_scatter(gain_ffn_grad, ("dp", "ctx"), scatter_dimension=0, tiled=True),
    )
    return (
        mixed,
        tokens_grad,
        owned[0],
        owned[1],
        owned[2],
        owned[3],
        owned[5],
        owned[6],
        owned[4],
        expert_grad,
    )


VMEM_BYTES = 60 * 1024 * 1024


def nn(a, b):
    return jnp.dot(a, b, preferred_element_type=jnp.float32)


def nt(a, b):
    return lax.dot_general(a, b, (((1,), (1,)), ((), ())), preferred_element_type=jnp.float32)


def tn(a, b):
    return lax.dot_general(a, b, (((0,), (0,)), ((), ())), preferred_element_type=jnp.float32)


def tt(a, b):
    return lax.dot_general(a, b, (((0,), (1,)), ((), ())), preferred_element_type=jnp.float32)


def lanes_of(slot):
    return pl.ds(pl.multiple_of((slot % 2) * BLK, BLK), BLK)


def by_core(table, mine, other, work_on):
    core = table[table.shape[0] - 1]

    @pl.when(core == 0)
    def _():
        work_on(mine, other)

    @pl.when(core == 1)
    def _():
        work_on(other, mine)


def attention_forward_kernel(
    table, mine, other, out, out_rows, log_sum, q_seq, k_seq, v_seq
):
    for seq in range(2):

        def load(key_source, value_source):
            for g in range(BLOCKS):
                slot = table[seq * BLOCKS + g]
                lanes = lanes_of(slot)
                here = slice(g * BLK, (g + 1) * BLK)
                q_seq[:, here] = mine[slot // 2, 0:HD, lanes] * jnp.bfloat16(HD**-0.5)
                keys = key_source[slot // 2, HD : 2 * HD, lanes]
                k_seq[here, :] = keys.astype(jnp.float32).T.astype(jnp.bfloat16)
                v_seq[:, here] = value_source[slot // 2, HD : 2 * HD, lanes]

        by_core(table, mine, other, load)
        span = BLOCKS * BLK
        top = jnp.full((1, span), floor_value, jnp.float32)
        total = jnp.zeros((1, span), jnp.float32)
        acc = jnp.zeros((HD, span), jnp.float32)
        for g in range(BLOCKS):
            here = slice(g * BLK, (g + 1) * BLK)
            scores = nn(k_seq[here, :], q_seq[:, g * BLK :])
            new_top = jnp.maximum(top, jnp.max(scores, axis=0, keepdims=True))
            factor = jnp.exp(top - new_top)
            weights = jnp.exp(scores - new_top)
            total = total * factor + jnp.sum(weights, axis=0, keepdims=True)
            acc = acc * factor + nn(v_seq[:, here], weights.astype(jnp.bfloat16))
            final = acc[:, :BLK] / total[:, :BLK]
            place_of = slice(seq * span + g * BLK, seq * span + (g + 1) * BLK)
            out_rows[:, place_of] = final
            log_sum[:, place_of] = new_top[:, :BLK] + jnp.log(total[:, :BLK])
            slot = table[seq * BLOCKS + g]
            out[slot // 2, :, lanes_of(slot)] = final.astype(jnp.bfloat16)
            top, total, acc = new_top[:, BLK:], total[:, BLK:], acc[:, BLK:]


def attention_backward_kernel(
    table, mine, other, d_out, out_rows, log_sum, q_grads, kept, given, q_seq, k_cols, k_seq,
    v_seq, d_seq, delta, dq, dk, dv
):
    span = BLOCKS * BLK
    for seq in range(2):

        def load(key_source, value_source):
            for g in range(BLOCKS):
                slot = table[seq * BLOCKS + g]
                lanes = lanes_of(slot)
                here = slice(g * BLK, (g + 1) * BLK)
                q_seq[:, here] = mine[slot // 2, 0:HD, lanes] * jnp.bfloat16(HD**-0.5)
                keys = key_source[slot // 2, HD : 2 * HD, lanes]
                k_cols[:, here] = keys
                k_seq[here, :] = keys.astype(jnp.float32).T.astype(jnp.bfloat16)
                values = value_source[slot // 2, HD : 2 * HD, lanes]
                v_seq[here, :] = values.astype(jnp.float32).T.astype(jnp.bfloat16)
                d_block = d_out[slot // 2, :, lanes]
                d_seq[:, here] = d_block
                out_block = out_rows[:, seq * span + g * BLK : seq * span + (g + 1) * BLK]
                delta[:, here] = jnp.sum(
                    d_block.astype(jnp.float32) * out_block, axis=0, keepdims=True
                )

        by_core(table, mine, other, load)
        dq[...] = jnp.zeros_like(dq)
        for g in range(BLOCKS):
            keys = slice(g * BLK, (g + 1) * BLK)
            later = slice(g * BLK, span)
            q = q_seq[:, later]
            d = d_seq[:, later]
            sums = log_sum[:, seq * span + g * BLK : (seq + 1) * span]
            probs = jnp.exp(nn(k_seq[keys, :], q) - sums)
            d_scores = (probs * (nn(v_seq[keys, :], d) - delta[:, later])).astype(jnp.bfloat16)
            dv[:, keys] = nt(d, probs.astype(jnp.bfloat16))
            dk[:, keys] = nt(q, d_scores)
            dq[:, later] += nn(k_cols[:, keys], d_scores)

        def store(key_target, value_target):
            for g in range(BLOCKS):
                slot = table[seq * BLOCKS + g]
                lanes = lanes_of(slot)
                here = slice(g * BLK, (g + 1) * BLK)
                q_grads[slot // 2, :, lanes] = (dq[:, here] * HD**-0.5).astype(jnp.bfloat16)
                key_target[slot // 2, :, lanes] = dk[:, here].astype(jnp.bfloat16)
                value_target[slot // 2, :, lanes] = dv[:, here].astype(jnp.bfloat16)

        by_core(table, kept, given, store)


def work(microseconds):
    return int(microseconds * 1.15e9)


def params():
    return pltpu.CompilerParams(vmem_limit_bytes=VMEM_BYTES)


def attention_forward(table, mine, other):
    count, _, row_count = mine.shape
    total = BLOCKS * BLK
    whole = pl.BlockSpec(memory_space=pltpu.VMEM)
    return pl.pallas_call(
        attention_forward_kernel,
        out_shape=(
            jax.ShapeDtypeStruct((count, HD, row_count), jnp.bfloat16),
            jax.ShapeDtypeStruct((HD, 2 * total), jnp.float32),
            jax.ShapeDtypeStruct((1, 2 * total), jnp.float32),
        ),
        in_specs=[pl.BlockSpec(memory_space=pltpu.SMEM), whole, whole],
        out_specs=(whole,) * 3,
        scratch_shapes=[
            pltpu.VMEM((HD, total), jnp.bfloat16),
            pltpu.VMEM((total, HD), jnp.bfloat16),
            pltpu.VMEM((HD, total), jnp.bfloat16),
        ],
        compiler_params=params(),
        cost_estimate=pl.CostEstimate(
            flops=work(36), bytes_accessed=mine.size * 4, transcendentals=total * total // 2
        ),
        name="attention_forward",
    )(table, mine, other)


def attention_backward(table, mine, other, d_out, out_rows, log_sum):
    total = BLOCKS * BLK
    whole = pl.BlockSpec(memory_space=pltpu.VMEM)
    shape = jax.ShapeDtypeStruct(d_out.shape, jnp.bfloat16)
    return pl.pallas_call(
        attention_backward_kernel,
        out_shape=(shape,) * 3,
        in_specs=[pl.BlockSpec(memory_space=pltpu.SMEM)] + [whole] * 5,
        out_specs=(whole,) * 3,
        scratch_shapes=[
            pltpu.VMEM((HD, total), jnp.bfloat16),
            pltpu.VMEM((HD, total), jnp.bfloat16),
            pltpu.VMEM((total, HD), jnp.bfloat16),
            pltpu.VMEM((total, HD), jnp.bfloat16),
            pltpu.VMEM((HD, total), jnp.bfloat16),
            pltpu.VMEM((1, total), jnp.float32),
            pltpu.VMEM((HD, total), jnp.float32),
            pltpu.VMEM((HD, total), jnp.float32),
            pltpu.VMEM((HD, total), jnp.float32),
        ],
        compiler_params=params(),
        cost_estimate=pl.CostEstimate(
            flops=work(58), bytes_accessed=mine.size * 6, transcendentals=total * total // 2
        ),
        name="attention_backward",
    )(table, mine, other, d_out, out_rows, log_sum)


def slot_match(places, rows):
    numbers = lax.broadcasted_iota(jnp.int32, (rows, places.shape[1]), 0).astype(jnp.float32)
    return numbers == places


def column_match(places, columns):
    numbers = lax.broadcasted_iota(jnp.int32, (places.shape[0], columns), 1).astype(jnp.float32)
    return jnp.where(numbers == places, 1.0, 0.0).astype(jnp.bfloat16)


def both_match(places):
    return jnp.concatenate(
        [
            jnp.where(slot_match(places[e : e + 1, :], CAP), 1.0, 0.0)
            for e in range(places.shape[0])
        ],
        axis=0,
    )


def spread_match(places):
    columns = places.T
    count = places.shape[0] * CAP
    numbers = lax.broadcasted_iota(jnp.int32, (columns.shape[0], count), 1)
    found = numbers < 0
    for e in range(places.shape[0]):
        column = columns[:, e : e + 1]
        found = found | (numbers.astype(jnp.float32) == jnp.where(column < 0, -1.0, column + e * CAP))
    return jnp.where(found, 1.0, 0.0).astype(jnp.bfloat16)


def pick_rows(order, places, sources, picked):
    g = pl.program_id(0)
    for k in range(len(sources) // 2):

        @pl.when(g == k)
        def _(k=k):
            for i in range(2):
                pick = both_match(places[order[2 * k + i]]).astype(jnp.bfloat16)
                rows = nn(pick, sources[2 * k + i][...]).astype(jnp.bfloat16)
                for e in range(places.shape[1]):
                    picked[e, i * CAP : (i + 1) * CAP, :] = rows[e * CAP : (e + 1) * CAP]


def grad_kernel(count, order, places, *refs):
    sources, weights = refs[:count], refs[count]
    slot_rows, d_hidden = refs[-2:]
    pick_rows(order, places, sources, slot_rows)
    for e in range(places.shape[1]):
        d_hidden[e] = nn(slot_rows[e], weights[0, :, e * F : (e + 1) * F]).astype(jnp.bfloat16)


def grad_step(first, order, places, blocks, weights, kept):
    devices, local, row_count = places.shape
    count = len(blocks)
    kept = () if kept is None else tuple(kept)
    whole = pl.BlockSpec((devices, local, row_count), lambda g, order: (0, 0, 0))
    block = pl.BlockSpec((row_count, D), lambda g, order: (0, 0))
    return pl.pallas_call(
        partial(grad_kernel, count),
        grid_spec=pltpu.PrefetchScalarGridSpec(
            num_scalar_prefetch=1,
            grid=(count // 2,),
            in_specs=[
                whole,
                *([block] * count),
                pl.BlockSpec((1, D, local * F), lambda g, order: (2, 0, 0)),
            ]
            + [pl.BlockSpec(memory_space=pl.ANY)] * len(kept),
            out_specs=(
                pl.BlockSpec((local, 2 * CAP, D), lambda g, order: (0, first // 2 + g, 0)),
                pl.BlockSpec((local, 2 * CAP, F), lambda g, order: (0, first // 2 + g, 0)),
            ),
        ),
        out_shape=(
            jax.ShapeDtypeStruct((local, devices * CAP, D), jnp.bfloat16),
            jax.ShapeDtypeStruct((local, devices * CAP, F), jnp.bfloat16),
        ),
        input_output_aliases={count + 3 + i: i for i in range(len(kept))},
        compiler_params=params(),
        cost_estimate=pl.CostEstimate(
            flops=work(2 * count + 2), bytes_accessed=count * row_count * D * 4, transcendentals=0
        ),
        name="grad_step",
    )(order, places, *blocks, weights, *kept)


def expert_kernel(count, order, places, gates, *refs):
    sources, (d_hidden, weights) = refs[:count], refs[count : count + 2]
    slot_rows, hidden, d_gate_pre, d_up, d_gate, near, far, back = refs[-8:]
    g = pl.program_id(0)
    local = places.shape[1]
    pick_rows(order, places, sources, slot_rows)
    here = [slice(e * F, (e + 1) * F) for e in range(local)]
    numbers = [order[2 * g], order[2 * g + 1]]
    picks = [both_match(places[j]) for j in numbers]
    slot_gates = []
    for e in range(local):
        gate_pre = nn(slot_rows[e], weights[0, :, here[e]])
        up_pre = nn(slot_rows[e], weights[1, :, here[e]])
        gate = jnp.concatenate(
            [
                jnp.sum(
                    picks[i][e * CAP : (e + 1) * CAP] * gates[numbers[i]][e : e + 1, :],
                    axis=1,
                    keepdims=True,
                )
                for i in range(2)
            ],
            axis=0,
        )
        raw = d_hidden[e].astype(jnp.float32)
        sig = 1.0 / (1.0 + jnp.exp(-gate_pre))
        silu = gate_pre * sig
        value = silu * up_pre
        hidden[e] = (gate * value).astype(jnp.bfloat16)
        scaled = raw * gate
        d_up[e] = (scaled * silu).astype(jnp.bfloat16)
        d_gate_pre[e] = (scaled * up_pre * sig * (1.0 + gate_pre * (1.0 - sig))).astype(
            jnp.bfloat16
        )
        slot_gates.append(jnp.sum(raw * value, axis=1, keepdims=True))
    for e in range(local):
        back[e] = (
            nt(d_gate_pre[e], weights[0, :, here[e]]) + nt(d_up[e], weights[1, :, here[e]])
        ).astype(jnp.bfloat16)
    results = []
    for i in range(2):
        part = slice(i * CAP, (i + 1) * CAP)
        for e in range(local):
            d_gate[i, e : e + 1, :] = jnp.sum(
                picks[i][e * CAP : (e + 1) * CAP] * slot_gates[e][part], axis=0, keepdims=True
            )
        rows = jnp.concatenate([back[e, part] for e in range(local)], axis=0)
        results.append(nn(spread_match(places[numbers[i]]), rows).astype(jnp.bfloat16))
    if count == 2:
        near[0] = results[0]
        far[0] = results[1]
    else:

        @pl.when(g == 0)
        def _():
            near[0] = results[0]
            near[1] = results[1]

        @pl.when(g == 1)
        def _():
            far[0] = results[0]
            far[1] = results[1]


def expert_step(first, order, places, gates, blocks, d_hidden, weights, kept):
    devices, local, row_count = places.shape
    count = len(blocks)
    half = count // 2
    wide_slots = pl.BlockSpec((local, 2 * CAP, D), lambda g, order: (0, first // 2 + g, 0))
    slots = pl.BlockSpec((local, 2 * CAP, F), lambda g, order: (0, first // 2 + g, 0))
    whole = pl.BlockSpec((devices, local, row_count), lambda g, order: (0, 0, 0))
    block = pl.BlockSpec((row_count, D), lambda g, order: (0, 0))
    sums = pl.BlockSpec((half, row_count, D), lambda g, order: (0, 0, 0))
    kept = () if kept is None else tuple(kept)
    first_kept = 5 + count
    return pl.pallas_call(
        partial(expert_kernel, count),
        grid_spec=pltpu.PrefetchScalarGridSpec(
            num_scalar_prefetch=1,
            grid=(half,),
            in_specs=[
                whole,
                whole,
                *([block] * count),
                slots,
                pl.BlockSpec((2, D, local * F), lambda g, order: (0, 0, 0)),
            ]
            + [pl.BlockSpec(memory_space=pl.ANY)] * len(kept),
            out_specs=(
                wide_slots,
                slots,
                slots,
                slots,
                pl.BlockSpec((2, local, row_count), lambda g, order: (g, 0, 0)),
                sums,
                sums,
            ),
            scratch_shapes=[pltpu.VMEM((local, 2 * CAP, D), jnp.bfloat16)],
        ),
        out_shape=(
            jax.ShapeDtypeStruct((local, devices * CAP, D), jnp.bfloat16),
            jax.ShapeDtypeStruct((local, devices * CAP, F), jnp.bfloat16),
            jax.ShapeDtypeStruct((local, devices * CAP, F), jnp.bfloat16),
            jax.ShapeDtypeStruct((local, devices * CAP, F), jnp.bfloat16),
            jax.ShapeDtypeStruct((count, local, row_count), jnp.float32),
            jax.ShapeDtypeStruct((half, row_count, D), jnp.bfloat16),
            jax.ShapeDtypeStruct((half, row_count, D), jnp.bfloat16),
        ),
        input_output_aliases={first_kept + i: i for i in range(len(kept))},
        compiler_params=params(),
        cost_estimate=pl.CostEstimate(
            flops=work(4 * count + 2),
            bytes_accessed=count * row_count * D * 6,
            transcendentals=count * local * CAP * F,
        ),
        name="expert_step",
    )(order, places, gates, *blocks, d_hidden, weights, *kept)


def output_kernel(order, columns, hidden, weights, first_half, second_half):
    total = None
    for e in range(columns.shape[2]):
        out = nt(hidden[e], weights[0, :, e * F : (e + 1) * F]).astype(jnp.bfloat16)
        spread = nn(column_match(columns[0, :, e : e + 1], CAP), out)
        total = spread if total is None else total + spread
    first_half[...] = total[:, : D // 2].astype(jnp.bfloat16)
    second_half[...] = total[:, D // 2 :].astype(jnp.bfloat16)


def output_pass(order, columns, hidden, weights):
    devices, row_count, local = columns.shape
    return pl.pallas_call(
        output_kernel,
        grid_spec=pltpu.PrefetchScalarGridSpec(
            num_scalar_prefetch=1,
            grid=(devices,),
            in_specs=[
                pl.BlockSpec((1, row_count, local), lambda j, order: (order[j], 0, 0)),
                pl.BlockSpec((local, CAP, F), lambda j, order: (0, j, 0)),
                pl.BlockSpec((1, D, local * F), lambda j, order: (2, 0, 0)),
            ],
            out_specs=(pl.BlockSpec((row_count, D // 2), lambda j, order: (order[j], 0)),) * 2,
        ),
        out_shape=(jax.ShapeDtypeStruct((devices * row_count, D // 2), jnp.bfloat16),) * 2,
        compiler_params=params(),
        cost_estimate=pl.CostEstimate(
            flops=work(26), bytes_accessed=devices * row_count * D * 3,
            transcendentals=0,
        ),
        name="output_pass",
    )(order, columns, hidden, weights)


def weight_grad_kernel(half, slot_rows, slot_grads, d_gate_pre, d_up, hidden, *out):
    out[0][...] = tn(slot_rows[0], d_gate_pre[0]).astype(out[0].dtype)
    out[1][...] = tn(slot_rows[0], d_up[0]).astype(out[1].dtype)
    out[2][...] = tn(slot_grads[0], hidden[0]).astype(out[2].dtype)


def weight_grad(half, slot_rows, slot_grads, d_gate_pre, d_up, hidden, dtype):
    local, count, _ = hidden.shape
    wide_slots = pl.BlockSpec((1, count, D // 2), lambda e, half: (e, 0, half[0]))
    slots = pl.BlockSpec((1, count, F), lambda e, half: (e, 0, 0))
    return pl.pallas_call(
        weight_grad_kernel,
        grid_spec=pltpu.PrefetchScalarGridSpec(
            num_scalar_prefetch=1,
            grid=(local,),
            in_specs=[wide_slots, wide_slots, slots, slots, slots],
            out_specs=(pl.BlockSpec((D // 2, F), lambda e, half: (0, e)),) * 3,
        ),
        out_shape=(jax.ShapeDtypeStruct((D // 2, local * F), dtype),) * 3,
        compiler_params=params(),
        cost_estimate=pl.CostEstimate(
            flops=work(15), bytes_accessed=local * count * D * 8, transcendentals=0
        ),
        name="weight_grad",
    )(half, slot_rows, slot_grads, d_gate_pre, d_up, hidden)


LINE = 4
ROWS = 2
CORES = 2
together = lax.optimization_barrier


def place(z, y, c):
    return (z * ROWS + y) * CORES + c


def move(values, target):
    pairs = []
    for z in range(LINE):
        for y in range(ROWS):
            for c in range(CORES):
                there = target(z, y, c)
                if there is not None and 0 <= there[0] < LINE:
                    pairs.append((place(z, y, c), place(*there)))
    return lax.ppermute(values, "ctx", pairs)


def core_swap(values):
    return move(values, lambda z, y, c: (z, y, 1 - c))


def row_swap(values):
    return move(values, lambda z, y, c: (z, 1 - y, c))


def up_from(values, sources):
    return move(values, lambda z, y, c: (z + 1, y, c) if z in sources else None)


def down_from(values, sources):
    return move(values, lambda z, y, c: (z - 1, y, c) if z in sources else None)


def added(*terms):
    total = terms[0].astype(jnp.float32)
    for term in terms[1:]:
        total = total + term.astype(jnp.float32)
    return total.astype(jnp.bfloat16)


LINE_ORDER = ((0, 1, 2, 3), (1, 2, 3, 0), (2, 1, 0, 3), (3, 2, 1, 0))


def send_on(s, own, up, down):
    sent = []
    if s < LINE:
        sent.append(row_swap(own))
    if s < LINE - 1:
        sent.append(up_from(up, tuple(range(s, LINE - 1))))
        sent.append(down_from(down, tuple(range(1, LINE - s))))
    return sent


def newest(s, ups, downs, z):
    if s < LINE - 1:
        return jnp.where(z >= 2, ups[s], downs[s])
    return jnp.where(
        z == 0, downs[3], jnp.where(z == 1, ups[1], jnp.where(z == 2, downs[1], ups[3]))
    )


def near_order(position):
    z = position // (ROWS * CORES)
    y = position // CORES % ROWS
    c = position % CORES
    line = jnp.asarray(LINE_ORDER, jnp.int32)[z]
    steps = []
    for s in range(LINE + 1):
        for other_core in range(CORES):
            if s < LINE:
                steps.append(place(line[s], y, c ^ other_core))
            if s > 0:
                steps.append(place(line[s - 1], 1 - y, c ^ other_core))
    return jnp.stack(steps).astype(jnp.int32)


def scatter_sum(summed, z, later, beside):
    across_3 = row_swap(summed[4][0])
    across_3, give_2, give_1, give_0, *later = together(
        (across_3, summed[3][1], summed[2][1], summed[1][1], *later)
    )
    part_3 = added(summed[3][0], across_3)
    up_3 = up_from(part_3, (0,))
    down_3 = down_from(part_3, (3,))
    across_2 = row_swap(give_2)
    up_3, down_3, across_2, give_1, give_0, beside = together(
        (up_3, down_3, across_2, give_1, give_0, beside)
    )
    part_2 = added(summed[2][0], across_2)
    up_2 = up_from(added(part_2, up_3), (0, 1))
    down_2 = down_from(added(part_2, down_3), (3, 2))
    across_1 = row_swap(give_1)
    up_2, down_2, across_1, give_0 = together((up_2, down_2, across_1, give_0))
    part_1 = added(summed[1][0], across_1)
    up_1 = up_from(added(jnp.where(z == 2, part_3, part_1), up_2), (0, 1, 2))
    down_1 = down_from(added(jnp.where(z == 1, part_3, part_1), down_2), (1, 2, 3))
    across_0 = row_swap(give_0)
    return [summed[0][0], across_0, up_1, down_1], later, beside


def one_of(values, index, axis):
    return lax.dynamic_index_in_dim(values, index, axis, keepdims=False)


def halves(values, core, axis):
    total = values.shape[axis]
    shape = list(values.shape)
    split = shape[:axis] + [LINE * ROWS * 2, CORES, total // (2 * LINE * ROWS * CORES)]
    values = values.reshape(split + shape[axis + 1 :])
    shape[axis] = total // CORES
    return tuple(
        one_of(values, which, axis + 1).reshape(shape) for which in (core, 1 - core)
    )


def by_side(values):
    spots = LINE * ROWS
    return values.reshape(2, spots, values.shape[0] // (2 * spots), values.shape[1])


def side_sum(values, side):
    return added(one_of(values, side, 0), exchange(one_of(values, 1 - side, 0)))


def owner_last(values):
    groups = [[spot * CORES + core for spot in range(LINE * ROWS)] for core in range(CORES)]
    values = lax.all_to_all(
        values, "ctx", split_axis=0, concat_axis=0, tiled=True, axis_index_groups=groups
    )
    return jnp.sum(values.astype(jnp.float32), axis=0)


def exchange(values):
    return lax.ppermute(values, "dp", [(0, 1), (1, 0)])


def to_heads(values):
    return lax.all_to_all(values, "ctx", split_axis=0, concat_axis=0, tiled=True)


def turn(values, cosine, sine):
    half = HD // 2
    first, second = values[:, :half, :], values[:, half:, :]
    return jnp.concatenate(
        [first * cosine - second * sine, second * cosine + first * sine], axis=1
    )


def per_device(
    tokens, grad_out, w_query, w_key, w_value, w_output, gain_attn, gain_ffn, w_router, w_experts,
    deal_table, routes
):
    row_count = tokens.shape[0]
    devices = lax.axis_size("ctx")
    position = lax.axis_index("ctx")
    side = lax.axis_index("dp")
    both = ("dp", "ctx")
    shard = w_query.shape[0]
    wide = HQ * HD
    narrow = KVH * HD

    extras = jnp.concatenate(
        [w_router, gain_attn[:, None], gain_ffn[:, None], jnp.zeros((shard, 94), jnp.bfloat16)],
        axis=1,
    )
    packed_weights = lax.all_gather(
        jnp.concatenate([w_query, w_key, w_value, extras], axis=1), both, axis=0, tiled=True
    )
    other_experts = exchange(w_experts)
    local = w_experts.shape[2] // F
    line_place = position // (ROWS * CORES)
    order = near_order(position)

    g_ups, g_downs, g_across, g_own = [grad_out], [grad_out], [], [grad_out]
    for s in range(3):
        sent = send_on(s, g_own[s], g_ups[s], g_downs[s])
        if s == 1:
            packed_weights, *sent = together((packed_weights, *sent))
        elif s == 0:
            sent = together(tuple(sent))
        else:
            step_2 = sent
        g_across.append(sent[0])
        g_ups.append(sent[1])
        g_downs.append(sent[2])
        g_own.append(newest(s + 1, g_ups, g_downs, line_place))

    full_qkv = packed_weights[:, : wide + 2 * narrow]
    extra_columns = packed_weights[:, wide + 2 * narrow :]
    full_router = extra_columns[:, :E]
    gain_attn_full = extra_columns[:, E].astype(jnp.float32)
    gain_ffn_full = extra_columns[:, E + 1].astype(jnp.float32)

    expert_ids = jnp.arange(E, dtype=jnp.int32)
    picked = routes[:, :, None] == expert_ids[None, None, :]
    member = jnp.any(picked, axis=1)
    below = (jnp.arange(row_count)[:, None] > jnp.arange(row_count)[None, :]).astype(jnp.bfloat16)
    before = nn(below, member.astype(jnp.bfloat16))
    places = jnp.where(member, before, -1.0)
    slot_places = to_heads(places.T.reshape(devices, local, row_count))

    group_blocks = deal_table[0]
    own_blocks = lax.dynamic_slice_in_dim(group_blocks, 2 * position, 2)
    offsets = jnp.arange(BLK, dtype=jnp.int32)
    positions = ((own_blocks % BLOCKS)[:, None] * BLK + offsets[None, :]).reshape(-1)
    core = position % CORES
    table = jnp.concatenate([jnp.argsort(group_blocks).astype(jnp.int32), core.reshape(1)])
    frequency = 10000.0 ** (-(jnp.arange(HD // 2).astype(jnp.float32) * 2.0 / HD))
    angles = frequency[:, None] * positions.astype(jnp.float32)[None, :]
    cosine, sine = jnp.cos(angles)[None], jnp.sin(angles)[None]
    inputs = tokens.astype(jnp.float32)
    normed = rms_norm(inputs, gain_attn_full).astype(jnp.bfloat16)
    normed_near, normed_far = halves(normed, core, 1)
    raw = tt(full_qkv, normed)
    queries = turn(raw[:wide].reshape(HQ, HD, row_count), cosine, sine).astype(jnp.bfloat16)
    keys = turn(raw[wide : wide + narrow].reshape(KVH, HD, row_count), cosine, sine).astype(
        jnp.bfloat16
    )
    values = raw[wide + narrow :].reshape(KVH, HD, row_count).astype(jnp.bfloat16)
    pairs = jnp.stack([keys, values], axis=1).reshape(HQ, HD, row_count)
    outgoing = jnp.concatenate([queries, pairs], axis=1)
    outgoing, other_experts, slot_places, w_output, *step_2 = together(
        (outgoing, other_experts, slot_places, w_output, *step_2)
    )
    full_output = lax.all_gather(w_output, both, axis=0, tiled=True)
    packed = to_heads(outgoing)
    g_across[2], g_ups[3], g_downs[3] = step_2
    g_own[3] = newest(3, g_ups, g_downs, line_place)
    slot_columns = slot_places.transpose(0, 2, 1)
    first_half = jnp.where(side == 0, w_experts, other_experts)
    second_half = jnp.where(side == 0, other_experts, w_experts)
    experts = jnp.concatenate([first_half, second_half], axis=1)
    g_kept, g_first = None, 0
    for s in range(LINE + 1):
        if s == LINE:
            packed, g_own[3], *g_kept = together((packed, g_own[3], *g_kept))
            other_packed = core_swap(packed)
            g_across.append(row_swap(g_own[3]))
            heads, attended_rows, log_sum = attention_forward(table, packed, other_packed)
            heads, g_across[3] = together((heads, g_across[3]))
            attended = to_heads(heads)
        blocks = g_own[s : s + 1] + (g_across[s - 1 : s] if s else [])
        blocks += [core_swap(b) for b in blocks]
        count = len(blocks)
        g_kept = grad_step(
            g_first, order[g_first : g_first + count], slot_places, blocks, experts, g_kept
        )
        g_first += count
    attended, *g_kept = together((attended, *g_kept))
    attended = attended.reshape(wide, row_count)
    slot_grads, d_hidden = g_kept
    residual = inputs + tn(attended, full_output)

    normed_ffn = rms_norm(residual, gain_ffn_full).astype(jnp.bfloat16)
    logits = nn(normed_ffn, full_router)
    masked = jnp.where(member, logits, floor_value)
    powers = jnp.where(member, jnp.exp(masked - jnp.max(masked, axis=1, keepdims=True)), 0.0)
    gates = powers / jnp.sum(powers, axis=1, keepdims=True)
    swapped = core_swap(normed_ffn)
    gates_out, swapped = together((gates.T.reshape(devices, local, row_count), swapped))
    slot_gates = to_heads(gates_out)
    summed, d_gate_parts, kept = [], [], None
    own, across = normed_ffn, None
    ups, downs = [normed_ffn], [normed_ffn]
    first = 0
    for s in range(LINE + 1):
        blocks = [b for b in (own, across) if b is not None]
        sent = send_on(s, own, ups[-1], downs[-1])
        blocks += [core_swap(b) for b in blocks] if s else [swapped]
        count = len(blocks)
        *kept, d_gate_part, near_part, far_part = expert_step(
            first, order[first : first + count], slot_places, slot_gates, blocks, d_hidden,
            experts, kept
        )
        if sent and summed:
            *sent, near_part, summed[-1] = together((*sent, near_part, summed[-1]))
        elif sent:
            *sent, near_part = together((*sent, near_part))
        first += count
        summed.append(added(near_part, core_swap(far_part)))
        d_gate_parts.append(d_gate_part)
        across = sent[0] if s < LINE else None
        if s < LINE - 1:
            ups.append(sent[1])
            downs.append(sent[2])
        own = newest(s + 1, ups, downs, line_place) if s < LINE - 1 else None
    slot_rows, hidden, d_gate_pre, d_up = kept
    out_rows, late_rows = output_pass(order, slot_columns, hidden, experts)
    arrived, d_gate_parts, out_rows = scatter_sum(summed, line_place, d_gate_parts, out_rows)
    mixture = lax.psum_scatter(out_rows, "ctx", scatter_dimension=0, tiled=True)
    given = weight_grad(
        (1 - side).reshape(1), slot_rows, slot_grads, d_gate_pre, d_up, hidden, jnp.bfloat16
    )
    taken = [exchange(part) for part in given]
    owned_experts = weight_grad(
        side.reshape(1), slot_rows, slot_grads, d_gate_pre, d_up, hidden, jnp.float32
    )
    back = jnp.argsort(order)
    d_gate = to_heads(jnp.concatenate(d_gate_parts, axis=0)[back])
    *arrived, taken[0], taken[1], owned_experts, d_gate = together(
        (*arrived, taken[0], taken[1], owned_experts, d_gate)
    )
    d_gate = d_gate.reshape(E, row_count).T
    ffn_grad = sum(part.astype(jnp.float32) for part in arrived)

    d_logits = gates * (d_gate - jnp.sum(gates * d_gate, axis=1, keepdims=True))
    ffn_grad = ffn_grad + jnp.einsum(
        "re,de->rd", d_logits, full_router.astype(jnp.float32), precision=highest
    )
    router_grad = jnp.einsum(
        "rd,re->de", normed_ffn.astype(jnp.float32), d_logits, precision=highest
    )
    _, norm_back_ffn = jax.vjp(rms_norm, residual, gain_ffn_full)
    residual_norm_grad, gain_ffn_grad = norm_back_ffn(ffn_grad)
    residual_grad = grad_out.astype(jnp.float32) + residual_norm_grad
    branch_grad = residual_grad.astype(jnp.bfloat16)
    attended_grad = nt(full_output, branch_grad).astype(jnp.bfloat16)
    d_heads = to_heads(attended_grad.reshape(HQ, HD, row_count))
    output_grad = jnp.concatenate(
        [
            nn(attended, branch_grad).astype(jnp.bfloat16),
            router_grad.astype(jnp.bfloat16),
            gain_ffn_grad[:, None].astype(jnp.bfloat16),
            jnp.zeros((D, 95), jnp.bfloat16),
        ],
        axis=1,
    )
    first_near, first_far = halves(output_grad, core, 0)
    first_parts = by_side(added(first_near, core_swap(first_far)))
    d_heads, first_parts, late_rows = together((d_heads, first_parts, late_rows))
    late_mixture = lax.psum_scatter(late_rows, "ctx", scatter_dimension=0, tiled=True)
    first_taken = exchange(one_of(first_parts, 1 - side, 0))

    q_grads, kept_grads, given_grads = attention_backward(
        table, packed, other_packed, d_heads, attended_rows, log_sum
    )
    q_grads, first_taken, taken[2] = together((q_grads, first_taken, taken[2]))
    q_back = to_heads(q_grads)
    pair_grads = added(kept_grads, core_swap(given_grads))
    q_back, pair_grads = together((q_back, pair_grads))
    pair_back = to_heads(pair_grads)
    d_query = (
        turn(q_back.astype(jnp.float32), cosine, -sine)
        .astype(jnp.bfloat16)
        .reshape(wide, row_count)
    )
    far_grad = core_swap(tt(normed_far, d_query).astype(jnp.bfloat16))
    near_grad = tt(normed_near, d_query).astype(jnp.bfloat16)
    query_parts = side_sum(by_side(added(near_grad, far_grad)), side)
    query_parts = jnp.concatenate(
        [query_parts, added(one_of(first_parts, side, 0), first_taken)], axis=2
    )
    pair_back, query_parts = together((pair_back, query_parts))
    query_owned = owner_last(query_parts)
    pairs = pair_back.astype(jnp.float32).reshape(KVH, 2, HD, row_count)
    d_pairs = jnp.concatenate(
        [
            turn(pairs[:, 0], cosine, -sine).astype(jnp.bfloat16),
            pairs[:, 1].astype(jnp.bfloat16),
        ],
        axis=0,
    ).reshape(2 * narrow, row_count)
    far_grad = core_swap(tt(normed_far, d_pairs).astype(jnp.bfloat16))
    near_grad = tt(normed_near, d_pairs).astype(jnp.bfloat16)
    normed_grad = tt(d_query, full_qkv[:, :wide]) + tt(d_pairs, full_qkv[:, wide:])
    _, norm_back_attn = jax.vjp(rms_norm, inputs, gain_attn_full)
    input_norm_grad, gain_attn_grad = norm_back_attn(normed_grad)
    gain_near, gain_far = halves(gain_attn_grad[:, None].astype(jnp.bfloat16), core, 0)
    pair_parts = by_side(added(near_grad, far_grad))
    given_pairs = exchange(one_of(pair_parts, 1 - side, 0))
    gain_parts = by_side(added(gain_near, core_swap(gain_far)))
    given_gain = exchange(one_of(gain_parts, 1 - side, 0))
    tokens_grad = residual_grad + input_norm_grad
    given_pairs, given_gain, tokens_grad = together((given_pairs, given_gain, tokens_grad))
    gain_parts = added(one_of(gain_parts, side, 0), given_gain)
    pair_owned = owner_last(
        jnp.concatenate(
            [
                added(one_of(pair_parts, side, 0), given_pairs),
                gain_parts,
                jnp.zeros((*gain_parts.shape[:2], 127), jnp.bfloat16),
            ],
            axis=2,
        )
    )
    mixture = jnp.concatenate([mixture, late_mixture], axis=1)
    mixed = (residual + mixture.astype(jnp.float32)).astype(jnp.bfloat16)
    expert_grad = jnp.stack(
        [mine + part.astype(jnp.float32) for mine, part in zip(owned_experts, taken)]
    )
    return (
        mixed,
        tokens_grad,
        query_owned[:, :wide],
        pair_owned[:, :narrow],
        pair_owned[:, narrow : 2 * narrow],
        query_owned[:, wide : wide + D],
        pair_owned[:, 2 * narrow],
        query_owned[:, wide + D + E],
        query_owned[:, wide + D : wide + D + E],
        expert_grad,
    )


def solution(mesh):
    in_specs = (
        P(("dp", "ctx"), None),
        P(("dp", "ctx"), None),
        P(("dp", "ctx"), None),
        P(("dp", "ctx"), None),
        P(("dp", "ctx"), None),
        P(("dp", "ctx"), None),
        P(("dp", "ctx")),
        P(("dp", "ctx")),
        P(("dp", "ctx"), None),
        P(None, "dp", "ctx"),
        P("dp", None),
        P(("dp", "ctx"), None),
    )
    out_specs = (
        P(("dp", "ctx"), None),
        P(("dp", "ctx"), None),
        P(("dp", "ctx"), None),
        P(("dp", "ctx"), None),
        P(("dp", "ctx"), None),
        P(("dp", "ctx"), None),
        P(("dp", "ctx")),
        P(("dp", "ctx")),
        P(("dp", "ctx"), None),
        P(None, "dp", "ctx"),
    )
    body = per_device if mesh.shape["ctx"] == HQ else general_device
    return jax.shard_map(
        body, mesh=mesh, in_specs=in_specs, out_specs=out_specs, check_vma=False
    )
```

```python
from functools import partial

import jax
import jax.numpy as jnp
from jax import lax
from jax.experimental import pallas as pl
from jax.experimental.pallas import tpu as pltpu
from jax.sharding import PartitionSpec as P

D = 1024
HQ = 16
KVH = 8
HD = 64
E = 32
F = 512
TOPK = 8
BLK = 256
BLOCKS = 16
CAP = 160


epsilon = 1e-06
highest = lax.Precision.HIGHEST
floor_value = -1e30


def rms_norm(values, gain):
    return values * lax.rsqrt(jnp.mean(values * values, axis=-1, keepdims=True) + epsilon) * gain


def rotary(values, positions):
    half_size = values.shape[-1] // 2
    frequency = 10000.0 ** (-(jnp.arange(half_size).astype(jnp.float32) * 2.0 / values.shape[-1]))
    angles = positions.astype(jnp.float32)[:, None] * frequency[None, :]
    cosine = jnp.cos(angles)[:, None, :]
    sine_part = jnp.sin(angles)[:, None, :]
    first_half = values[..., :half_size]
    second = values[..., half_size:]
    return jnp.concatenate(
        [first_half * cosine - second * sine_part, second * cosine + first_half * sine_part],
        axis=-1,
    )


def heads_major(block_rows, groups, head_ratio, head_size):
    count = block_rows.shape[0]
    shaped = block_rows.reshape(count, groups, head_ratio, head_size).transpose(1, 2, 0, 3)
    return shaped.reshape(groups, head_ratio * count, head_size)


def rows_major(blocked, groups, head_ratio, head_size):
    count = blocked.shape[1] // head_ratio
    shaped = blocked.reshape(groups, head_ratio, count, head_size).transpose(2, 0, 1, 3)
    return shaped.reshape(count, groups * head_ratio * head_size)


def stats_major(block_rows, groups, head_ratio):
    count = block_rows.shape[0]
    return (
        block_rows.reshape(count, groups, head_ratio)
        .transpose(1, 2, 0)
        .reshape(groups, head_ratio * count)
    )


def pair_blocks(rows, base, groups, head_ratio, head_size):
    return jnp.stack(
        [
            heads_major(lax.dynamic_slice_in_dim(rows, base + i * BLK, BLK), groups, head_ratio, head_size)
            for i in range(2)
        ]
    )


def pair_order(block_pair, per_seq):
    places = block_pair % per_seq
    lower_slot = (places[0] > places[1]).astype(jnp.int32)
    return (lower_slot, 1 - lower_slot, jnp.minimum(places[0], places[1]), block_pair[0] // per_seq)


def keep_state(carry_state):
    return carry_state


def forward_update(query_block, key_block, value_block, slot_number, score_scale):

    def forward_apply_update(carry_state):
        running_max, running_sum, accumulated = carry_state
        scores = (
            jnp.einsum("gqd,gkd->gqk", query_block, key_block, preferred_element_type=jnp.float32)
            * score_scale
        )
        new_max = jnp.maximum(running_max[slot_number], jnp.max(scores, axis=-1))
        factor = jnp.exp(running_max[slot_number] - new_max)
        weights = jnp.exp(scores - new_max[..., None])
        new_sum = running_sum[slot_number] * factor + jnp.sum(weights, axis=-1)
        product = jnp.einsum(
            "gqk,gkd->gqd",
            weights.astype(jnp.bfloat16),
            value_block,
            preferred_element_type=jnp.float32,
        )
        new_acc = accumulated[slot_number] * factor[..., None] + product
        return (
            running_max.at[slot_number].set(new_max),
            running_sum.at[slot_number].set(new_sum),
            accumulated.at[slot_number].set(new_acc),
        )

    return forward_apply_update


def query_update(
    query_block,
    grad_block,
    log_block,
    delta_block,
    key_block,
    value_block,
    slot_number,
    score_scale,
):

    def query_apply_update(accumulated):
        scores = (
            jnp.einsum("gqd,gkd->gqk", query_block, key_block, preferred_element_type=jnp.float32)
            * score_scale
        )
        probs_full = jnp.exp(scores - log_block[..., None])
        prob_grad = jnp.einsum(
            "gqd,gkd->gqk", grad_block, value_block, preferred_element_type=jnp.float32
        )
        score_grad = (probs_full * (prob_grad - delta_block[..., None])).astype(jnp.bfloat16)
        change = (
            jnp.einsum("gqk,gkd->gqd", score_grad, key_block, preferred_element_type=jnp.float32)
            * score_scale
        )
        return accumulated.at[slot_number].add(change)

    return query_apply_update


def key_update(
    query_block,
    grad_block,
    log_block,
    delta_block,
    key_block,
    value_block,
    slot_number,
    score_scale,
):

    def key_apply_update(carry_state):
        key_accum, value_accum = carry_state
        scores = (
            jnp.einsum("gqd,gkd->gqk", query_block, key_block, preferred_element_type=jnp.float32)
            * score_scale
        )
        probs_full = jnp.exp(scores - log_block[..., None])
        value_change = jnp.einsum(
            "gqk,gqd->gkd",
            probs_full.astype(jnp.bfloat16),
            grad_block,
            preferred_element_type=jnp.float32,
        )
        prob_grad = jnp.einsum(
            "gqd,gkd->gqk", grad_block, value_block, preferred_element_type=jnp.float32
        )
        score_grad = (probs_full * (prob_grad - delta_block[..., None])).astype(jnp.bfloat16)
        key_change = (
            jnp.einsum("gqk,gqd->gkd", score_grad, query_block, preferred_element_type=jnp.float32)
            * score_scale
        )
        return (
            key_accum.at[slot_number].add(key_change),
            value_accum.at[slot_number].add(value_change),
        )

    return key_apply_update


def expert_forward(routed_rows, weights_local):
    gate_pre = jnp.einsum(
        "erd,def->erf", routed_rows, weights_local[0], preferred_element_type=jnp.float32
    )
    up_pre = jnp.einsum(
        "erd,def->erf", routed_rows, weights_local[1], preferred_element_type=jnp.float32
    )
    hidden = (jax.nn.silu(gate_pre) * up_pre).astype(jnp.bfloat16)
    return (gate_pre, up_pre, hidden)


def natural_return(partials, split_count):
    devices = partials.shape[0]
    arrived = lax.all_to_all(partials, "ctx", split_axis=0, concat_axis=0, tiled=True)
    shaped = arrived.reshape(
        devices * partials.shape[1] // split_count,
        split_count,
        partials.shape[2],
        partials.shape[3],
    )
    return jnp.sum(shaped, axis=1)


def send_back(partials, split_count):
    return natural_return(partials, split_count)


def spread_slots(slot_values, devices, local_count, split_count):
    width = slot_values.shape[-1]
    return jnp.broadcast_to(
        slot_values.reshape(E, 1, CAP, width), (E, split_count, CAP, width)
    ).reshape(devices, local_count, CAP, width)


def general_device(
    tokens,
    grad_out,
    w_query,
    w_key,
    w_value,
    w_output,
    gain_attn,
    gain_ffn,
    w_router,
    w_experts,
    deal_table,
    routes,
):
    row_count = tokens.shape[0]
    head_ratio = HQ // KVH
    score_scale = HD ** (-0.5)
    full_query, full_key, full_value, full_output, full_router, full_gain_attn, full_gain_ffn = (
        lax.all_gather(w_query, ("dp", "ctx"), axis=0, tiled=True),
        lax.all_gather(w_key, ("dp", "ctx"), axis=0, tiled=True),
        lax.all_gather(w_value, ("dp", "ctx"), axis=0, tiled=True),
        lax.all_gather(w_output, ("dp", "ctx"), axis=0, tiled=True),
        lax.all_gather(w_router, ("dp", "ctx"), axis=0, tiled=True),
        lax.all_gather(gain_attn, ("dp", "ctx"), axis=0, tiled=True),
        lax.all_gather(gain_ffn, ("dp", "ctx"), axis=0, tiled=True),
    )
    experts_local = lax.all_gather(w_experts, "dp", axis=1, tiled=True)
    columns = experts_local.shape[2]
    unit_width = min(F, columns)
    local_count = columns // unit_width
    split_count = F // unit_width
    devices = lax.axis_size("ctx")
    position = lax.axis_index("ctx")
    group_blocks = deal_table[0]
    per_seq = BLOCKS
    own_blocks = lax.dynamic_slice_in_dim(group_blocks, 2 * position, 2)
    query_low, query_high, low_place, own_seq = pair_order(own_blocks, per_seq)
    offsets = jnp.arange(BLK, dtype=jnp.int32)
    positions = ((own_blocks % per_seq)[:, None] * BLK + offsets[None, :]).reshape(-1)
    inputs = tokens.astype(jnp.float32)
    gain_attn_full = full_gain_attn.astype(jnp.float32)
    gain_ffn_full = full_gain_ffn.astype(jnp.float32)
    normed = rms_norm(inputs, gain_attn_full).astype(jnp.bfloat16)
    query_raw = jnp.dot(normed, full_query, preferred_element_type=jnp.float32).reshape(
        row_count, HQ, HD
    )
    key_raw = jnp.dot(normed, full_key, preferred_element_type=jnp.float32).reshape(
        row_count, KVH, HD
    )
    value_raw = jnp.dot(normed, full_value, preferred_element_type=jnp.float32)
    queries = rotary(query_raw, positions).astype(jnp.bfloat16).reshape(row_count, HQ * HD)
    key_proj = rotary(key_raw, positions).astype(jnp.bfloat16).reshape(row_count, KVH * HD)
    value_proj = value_raw.astype(jnp.bfloat16)
    query_heads = pair_blocks(queries, 0, KVH, head_ratio, HD)
    key_heads = pair_blocks(key_proj, 0, KVH, 1, HD)
    value_heads = pair_blocks(value_proj, 0, KVH, 1, HD)
    score_rows = head_ratio * BLK
    initial = (
        jnp.full((2, KVH, score_rows), floor_value, jnp.float32),
        jnp.zeros((2, KVH, score_rows), jnp.float32),
        jnp.zeros((2, KVH, score_rows, HD), jnp.float32),
    )
    initial = forward_update(
        query_heads[query_low], key_heads[query_low], value_heads[query_low], query_low, score_scale
    )(initial)
    carry_state = initial
    key_rows = lax.all_gather(key_proj, "ctx", axis=0, tiled=True)
    value_rows = lax.all_gather(value_proj, "ctx", axis=0, tiled=True)
    def forward_step(j, carry_state):
        key_pair = pair_blocks(key_rows, j * 2 * BLK, KVH, 1, HD)
        value_pair = pair_blocks(value_rows, j * 2 * BLK, KVH, 1, HD)
        block_pair = lax.dynamic_slice_in_dim(group_blocks, 2 * j, 2)
        key_low, key_high, key_place, key_seq = pair_order(block_pair, per_seq)
        same = key_seq == own_seq
        carry_state = lax.cond(
            same,
            forward_update(
                query_heads[query_high],
                key_pair[key_low],
                value_pair[key_low],
                query_high,
                score_scale,
            ),
            keep_state,
            carry_state,
        )
        below = key_place < low_place
        pick_query = jnp.where(below, query_low, query_high)
        pick_key = jnp.where(below, key_low, key_high)
        carry_state = lax.cond(
            same,
            forward_update(
                query_heads[pick_query],
                key_pair[pick_key],
                value_pair[pick_key],
                pick_query,
                score_scale,
            ),
            keep_state,
            carry_state,
        )
        return carry_state

    carry_state = lax.fori_loop(0, key_rows.shape[0] // (2 * BLK), forward_step, carry_state)
    running_max, running_sum, accumulated = carry_state
    attended_heads = accumulated / running_sum[..., None]
    log_total = running_max + jnp.log(running_sum)
    attended_rows = jnp.concatenate(
        [rows_major(attended_heads[i], KVH, head_ratio, HD) for i in range(2)], axis=0
    )
    attended_low = attended_rows.astype(jnp.bfloat16)
    residual = inputs + jnp.dot(attended_low, full_output, preferred_element_type=jnp.float32)
    normed_ffn = rms_norm(residual, gain_ffn_full).astype(jnp.bfloat16)
    expert_ids = jnp.arange(E, dtype=jnp.int32)
    picked = routes[:, :, None] == expert_ids[None, None, :]
    ffn_float = normed_ffn.astype(jnp.float32)
    router_full = full_router.astype(jnp.float32)
    logits = jnp.dot(ffn_float, router_full, precision=highest)
    chosen = jnp.sum(jnp.where(picked, logits[:, None, :], 0.0), axis=2)
    gate_weights = jax.nn.softmax(chosen, axis=-1)
    member = jnp.sum(picked.astype(jnp.int32), axis=1)
    before = jnp.cumsum(member, axis=0) - member
    slot_numbers = jnp.sum(jnp.where(picked, before[:, None, :], 0), axis=2)
    flat_slot = (routes * CAP + slot_numbers).reshape(-1)
    owner_rows = (
        jnp.zeros((E * CAP,), jnp.int32)
        .at[flat_slot]
        .set(jnp.repeat(jnp.arange(1, row_count + 1, dtype=jnp.int32), TOPK))
    )
    slot_gate = jnp.zeros((E * CAP,), jnp.float32).at[flat_slot].set(gate_weights.reshape(-1))
    padded_rows = jnp.concatenate([jnp.zeros((1, D), jnp.bfloat16), normed_ffn], axis=0)
    slot_rows = padded_rows[owner_rows]
    outgoing = spread_slots(slot_rows, devices, local_count, split_count)
    arrived = lax.all_to_all(outgoing, "ctx", split_axis=0, concat_axis=0, tiled=True)
    routed_rows = arrived.transpose(1, 0, 2, 3).reshape(local_count, devices * outgoing.shape[2], D)
    weights_local = experts_local.reshape(3, D, local_count, unit_width)
    gate_pre, up_pre, hidden = expert_forward(routed_rows, weights_local)
    expert_out = jnp.einsum(
        "erf,def->erd", hidden, weights_local[2], preferred_element_type=jnp.float32
    )
    combined = send_back(
        expert_out.reshape(local_count, devices, outgoing.shape[2], D).transpose(1, 0, 2, 3),
        split_count,
    )
    routed_out = combined.reshape(E * CAP, D)[flat_slot].reshape(row_count, TOPK, D)
    mixed = (residual + jnp.sum(gate_weights[:, :, None] * routed_out, axis=1)).astype(jnp.bfloat16)
    upstream = grad_out.astype(jnp.float32)
    gate_grad = jnp.sum(routed_out * upstream[:, None, :], axis=2)
    chosen_grad = gate_weights * (
        gate_grad - jnp.sum(gate_weights * gate_grad, axis=1, keepdims=True)
    )
    logits_grad = jnp.sum(jnp.where(picked, chosen_grad[:, :, None], 0.0), axis=1)
    padded_grad = jnp.concatenate([jnp.zeros((1, D), jnp.float32), upstream], axis=0)
    slot_grad = (padded_grad[owner_rows] * slot_gate[:, None]).astype(jnp.bfloat16)
    outgoing_grad = spread_slots(slot_grad, devices, local_count, split_count)
    arrived_grad = lax.all_to_all(outgoing_grad, "ctx", split_axis=0, concat_axis=0, tiled=True)
    grad_rows = arrived_grad.transpose(1, 0, 2, 3).reshape(
        local_count, devices * outgoing.shape[2], D
    )
    hidden_grad = jnp.einsum(
        "erd,def->erf", grad_rows, weights_local[2], preferred_element_type=jnp.float32
    )
    sigmoid = jax.nn.sigmoid(gate_pre)
    up_grad = (hidden_grad * gate_pre * sigmoid).astype(jnp.bfloat16)
    gate_pre_grad = (hidden_grad * up_pre * sigmoid * (1.0 + gate_pre * (1.0 - sigmoid))).astype(
        jnp.bfloat16
    )
    weight_grad = jnp.stack(
        [
            jnp.einsum(
                "erd,erf->def", routed_rows, gate_pre_grad, preferred_element_type=jnp.float32
            ),
            jnp.einsum("erd,erf->def", routed_rows, up_grad, preferred_element_type=jnp.float32),
            jnp.einsum("erd,erf->def", grad_rows, hidden, preferred_element_type=jnp.float32),
        ]
    ).reshape(3, D, local_count * unit_width)
    input_grad = jnp.einsum(
        "erf,def->erd", gate_pre_grad, weights_local[0], preferred_element_type=jnp.float32
    )
    input_grad = input_grad + jnp.einsum(
        "erf,def->erd", up_grad, weights_local[1], preferred_element_type=jnp.float32
    )
    returned = send_back(
        input_grad.reshape(local_count, devices, outgoing.shape[2], D).transpose(1, 0, 2, 3),
        split_count,
    )
    ffn_grad = jnp.sum(returned.reshape(E * CAP, D)[flat_slot].reshape(row_count, TOPK, D), axis=1)
    ffn_grad = ffn_grad + jnp.einsum("re,de->rd", logits_grad, router_full, precision=highest)
    router_grad = jnp.einsum("rd,re->de", ffn_float, logits_grad, precision=highest)
    expert_grad = lax.psum_scatter(weight_grad, "dp", scatter_dimension=1, tiled=True)
    _, norm_back_ffn = jax.vjp(rms_norm, residual, gain_ffn_full)
    residual_norm_grad, gain_ffn_grad = norm_back_ffn(ffn_grad)
    residual_grad = upstream + residual_norm_grad
    branch_grad = residual_grad.astype(jnp.bfloat16)
    output_grad = jnp.einsum(
        "rc,rd->cd", attended_low, branch_grad, preferred_element_type=jnp.float32
    )
    attended_grad = jnp.einsum(
        "rd,cd->rc", branch_grad, full_output, preferred_element_type=jnp.float32
    ).astype(jnp.bfloat16)
    delta_rows = jnp.sum(
        (attended_grad.astype(jnp.float32) * attended_rows).reshape(row_count, HQ, HD), axis=-1
    )
    delta_heads = jnp.stack(
        [stats_major(delta_rows[i * BLK : (i + 1) * BLK], KVH, head_ratio) for i in range(2)]
    )
    grad_heads = pair_blocks(attended_grad, 0, KVH, head_ratio, HD)
    all_log, all_delta = (
        lax.all_gather(log_total, "ctx", axis=0, tiled=True),
        lax.all_gather(delta_heads, "ctx", axis=0, tiled=True),
    )
    query_start = query_update(
        query_heads[query_low],
        grad_heads[query_low],
        log_total[query_low],
        delta_heads[query_low],
        key_heads[query_low],
        value_heads[query_low],
        query_low,
        score_scale,
    )(jnp.zeros((2, KVH, score_rows, HD), jnp.float32))
    accumulated_grad = query_start
    key_rows = lax.all_gather(key_proj, "ctx", axis=0, tiled=True)
    value_rows = lax.all_gather(value_proj, "ctx", axis=0, tiled=True)
    def query_step(j, accumulated_grad):
        key_pair = pair_blocks(key_rows, j * 2 * BLK, KVH, 1, HD)
        value_pair = pair_blocks(value_rows, j * 2 * BLK, KVH, 1, HD)
        block_pair = lax.dynamic_slice_in_dim(group_blocks, 2 * j, 2)
        key_low, key_high, key_place, key_seq = pair_order(block_pair, per_seq)
        same = key_seq == own_seq
        first = query_update(
            query_heads[query_high],
            grad_heads[query_high],
            log_total[query_high],
            delta_heads[query_high],
            key_pair[key_low],
            value_pair[key_low],
            query_high,
            score_scale,
        )
        accumulated_grad = lax.cond(same, first, keep_state, accumulated_grad)
        below = key_place < low_place
        pick_query = jnp.where(below, query_low, query_high)
        pick_key = jnp.where(below, key_low, key_high)
        second_update = query_update(
            query_heads[pick_query],
            grad_heads[pick_query],
            log_total[pick_query],
            delta_heads[pick_query],
            key_pair[pick_key],
            value_pair[pick_key],
            pick_query,
            score_scale,
        )
        accumulated_grad = lax.cond(same, second_update, keep_state, accumulated_grad)
        return accumulated_grad

    accumulated_grad = lax.fori_loop(0, key_rows.shape[0] // (2 * BLK), query_step, accumulated_grad)
    zero_keys = jnp.zeros((2, KVH, BLK, HD), jnp.float32)
    key_start = key_update(
        query_heads[query_low],
        grad_heads[query_low],
        log_total[query_low],
        delta_heads[query_low],
        key_heads[query_low],
        value_heads[query_low],
        query_low,
        score_scale,
    )((zero_keys, zero_keys))
    carry_state = key_start
    start_row = jnp.int32(0)
    query_rows = lax.all_gather(queries, "ctx", axis=0, tiled=True)
    grad_piece = lax.all_gather(attended_grad, "ctx", axis=0, tiled=True)
    def key_step(j, carry_state):
        slot_first = start_row // BLK + 2 * j
        query_pair = pair_blocks(query_rows, j * 2 * BLK, KVH, head_ratio, HD)
        grad_pair = pair_blocks(grad_piece, j * 2 * BLK, KVH, head_ratio, HD)
        block_pair = lax.dynamic_slice_in_dim(group_blocks, slot_first, 2)
        log_pair = lax.dynamic_slice_in_dim(all_log, slot_first, 2)
        delta_pair = lax.dynamic_slice_in_dim(all_delta, slot_first, 2)
        remote_low, remote_high, remote_place, remote_seq = pair_order(block_pair, per_seq)
        same = remote_seq == own_seq
        first = key_update(
            query_pair[remote_high],
            grad_pair[remote_high],
            log_pair[remote_high],
            delta_pair[remote_high],
            key_heads[query_low],
            value_heads[query_low],
            query_low,
            score_scale,
        )
        carry_state = lax.cond(same, first, keep_state, carry_state)
        below = low_place < remote_place
        pick_remote = jnp.where(below, remote_low, remote_high)
        pick_own = jnp.where(below, query_low, query_high)
        second_update = key_update(
            query_pair[pick_remote],
            grad_pair[pick_remote],
            log_pair[pick_remote],
            delta_pair[pick_remote],
            key_heads[pick_own],
            value_heads[pick_own],
            pick_own,
            score_scale,
        )
        carry_state = lax.cond(same, second_update, keep_state, carry_state)
        return carry_state

    carry_state = lax.fori_loop(0, query_rows.shape[0] // (2 * BLK), key_step, carry_state)
    key_grad_heads, value_grad_heads = carry_state
    query_grad_rows = jnp.concatenate(
        [rows_major(accumulated_grad[i], KVH, head_ratio, HD) for i in range(2)], axis=0
    )
    key_grad_rows = jnp.concatenate(
        [rows_major(key_grad_heads[i], KVH, 1, HD) for i in range(2)], axis=0
    )
    value_grad_rows = jnp.concatenate(
        [rows_major(value_grad_heads[i], KVH, 1, HD) for i in range(2)], axis=0
    )
    _, query_rot_back = jax.vjp(partial(rotary, positions=positions), query_raw)
    _, key_rot_back = jax.vjp(partial(rotary, positions=positions), key_raw)
    query_proj_grad = (
        query_rot_back(query_grad_rows.reshape(row_count, HQ, HD))[0]
        .reshape(row_count, HQ * HD)
        .astype(jnp.bfloat16)
    )
    key_proj_grad = (
        key_rot_back(key_grad_rows.reshape(row_count, KVH, HD))[0]
        .reshape(row_count, KVH * HD)
        .astype(jnp.bfloat16)
    )
    value_proj_grad = value_grad_rows.astype(jnp.bfloat16)
    query_weight_grad = jnp.einsum(
        "rd,rc->dc", normed, query_proj_grad, preferred_element_type=jnp.float32
    )
    key_weight_grad = jnp.einsum(
        "rd,rc->dc", normed, key_proj_grad, preferred_element_type=jnp.float32
    )
    value_weight_grad = jnp.einsum(
        "rd,rc->dc", normed, value_proj_grad, preferred_element_type=jnp.float32
    )
    normed_grad = jnp.einsum(
        "rc,dc->rd", query_proj_grad, full_query, preferred_element_type=jnp.float32
    )
    normed_grad = normed_grad + jnp.einsum(
        "rc,dc->rd", key_proj_grad, full_key, preferred_element_type=jnp.float32
    )
    normed_grad = normed_grad + jnp.einsum(
        "rc,dc->rd", value_proj_grad, full_value, preferred_element_type=jnp.float32
    )
    _, norm_back_attn = jax.vjp(rms_norm, inputs, gain_attn_full)
    input_norm_grad, gain_attn_grad = norm_back_attn(normed_grad)
    tokens_grad = residual_grad + input_norm_grad
    owned = (
        lax.psum_scatter(query_weight_grad, ("dp", "ctx"), scatter_dimension=0, tiled=True),
        lax.psum_scatter(key_weight_grad, ("dp", "ctx"), scatter_dimension=0, tiled=True),
        lax.psum_scatter(value_weight_grad, ("dp", "ctx"), scatter_dimension=0, tiled=True),
        lax.psum_scatter(output_grad, ("dp", "ctx"), scatter_dimension=0, tiled=True),
        lax.psum_scatter(router_grad, ("dp", "ctx"), scatter_dimension=0, tiled=True),
        lax.psum_scatter(gain_attn_grad, ("dp", "ctx"), scatter_dimension=0, tiled=True),
        lax.psum_scatter(gain_ffn_grad, ("dp", "ctx"), scatter_dimension=0, tiled=True),
    )
    return (
        mixed,
        tokens_grad,
        owned[0],
        owned[1],
        owned[2],
        owned[3],
        owned[5],
        owned[6],
        owned[4],
        expert_grad,
    )


VMEM_BYTES = 60 * 1024 * 1024


def nn(a, b):
    return jnp.dot(a, b, preferred_element_type=jnp.float32)


def nt(a, b):
    return lax.dot_general(a, b, (((1,), (1,)), ((), ())), preferred_element_type=jnp.float32)


def tn(a, b):
    return lax.dot_general(a, b, (((0,), (0,)), ((), ())), preferred_element_type=jnp.float32)


def tt(a, b):
    return lax.dot_general(a, b, (((0,), (1,)), ((), ())), preferred_element_type=jnp.float32)


def lanes_of(slot):
    return pl.ds(pl.multiple_of((slot % 2) * BLK, BLK), BLK)


def by_core(table, mine, other, work_on):
    core = table[table.shape[0] - 1]

    @pl.when(core == 0)
    def _():
        work_on(mine, other)

    @pl.when(core == 1)
    def _():
        work_on(other, mine)


def attention_forward_kernel(
    table, mine, other, out, out_rows, log_sum, q_seq, k_seq, v_seq
):
    for seq in range(2):

        def load(key_source, value_source):
            for g in range(BLOCKS):
                slot = table[seq * BLOCKS + g]
                lanes = lanes_of(slot)
                here = slice(g * BLK, (g + 1) * BLK)
                q_seq[:, here] = mine[slot // 2, 0:HD, lanes] * jnp.bfloat16(HD**-0.5)
                keys = key_source[slot // 2, HD : 2 * HD, lanes]
                k_seq[here, :] = keys.astype(jnp.float32).T.astype(jnp.bfloat16)
                v_seq[:, here] = value_source[slot // 2, HD : 2 * HD, lanes]

        by_core(table, mine, other, load)
        span = BLOCKS * BLK
        top = jnp.full((1, span), floor_value, jnp.float32)
        total = jnp.zeros((1, span), jnp.float32)
        acc = jnp.zeros((HD, span), jnp.float32)
        for g in range(BLOCKS):
            here = slice(g * BLK, (g + 1) * BLK)
            scores = nn(k_seq[here, :], q_seq[:, g * BLK :])
            new_top = jnp.maximum(top, jnp.max(scores, axis=0, keepdims=True))
            factor = jnp.exp(top - new_top)
            weights = jnp.exp(scores - new_top)
            total = total * factor + jnp.sum(weights, axis=0, keepdims=True)
            acc = acc * factor + nn(v_seq[:, here], weights.astype(jnp.bfloat16))
            final = acc[:, :BLK] / total[:, :BLK]
            place_of = slice(seq * span + g * BLK, seq * span + (g + 1) * BLK)
            out_rows[:, place_of] = final
            log_sum[:, place_of] = new_top[:, :BLK] + jnp.log(total[:, :BLK])
            slot = table[seq * BLOCKS + g]
            out[slot // 2, :, lanes_of(slot)] = final.astype(jnp.bfloat16)
            top, total, acc = new_top[:, BLK:], total[:, BLK:], acc[:, BLK:]


def attention_backward_kernel(
    table, mine, other, d_out, out_rows, log_sum, q_grads, kept, given, q_seq, k_cols, k_seq,
    v_seq, d_seq, delta, dq, dk, dv
):
    span = BLOCKS * BLK
    for seq in range(2):

        def load(key_source, value_source):
            for g in range(BLOCKS):
                slot = table[seq * BLOCKS + g]
                lanes = lanes_of(slot)
                here = slice(g * BLK, (g + 1) * BLK)
                q_seq[:, here] = mine[slot // 2, 0:HD, lanes] * jnp.bfloat16(HD**-0.5)
                keys = key_source[slot // 2, HD : 2 * HD, lanes]
                k_cols[:, here] = keys
                k_seq[here, :] = keys.astype(jnp.float32).T.astype(jnp.bfloat16)
                values = value_source[slot // 2, HD : 2 * HD, lanes]
                v_seq[here, :] = values.astype(jnp.float32).T.astype(jnp.bfloat16)
                d_block = d_out[slot // 2, :, lanes]
                d_seq[:, here] = d_block
                out_block = out_rows[:, seq * span + g * BLK : seq * span + (g + 1) * BLK]
                delta[:, here] = jnp.sum(
                    d_block.astype(jnp.float32) * out_block, axis=0, keepdims=True
                )

        by_core(table, mine, other, load)
        dq[...] = jnp.zeros_like(dq)
        for g in range(BLOCKS):
            keys = slice(g * BLK, (g + 1) * BLK)
            later = slice(g * BLK, span)
            q = q_seq[:, later]
            d = d_seq[:, later]
            sums = log_sum[:, seq * span + g * BLK : (seq + 1) * span]
            probs = jnp.exp(nn(k_seq[keys, :], q) - sums)
            d_scores = (probs * (nn(v_seq[keys, :], d) - delta[:, later])).astype(jnp.bfloat16)
            dv[:, keys] = nt(d, probs.astype(jnp.bfloat16))
            dk[:, keys] = nt(q, d_scores)
            dq[:, later] += nn(k_cols[:, keys], d_scores)

        def store(key_target, value_target):
            for g in range(BLOCKS):
                slot = table[seq * BLOCKS + g]
                lanes = lanes_of(slot)
                here = slice(g * BLK, (g + 1) * BLK)
                q_grads[slot // 2, :, lanes] = (dq[:, here] * HD**-0.5).astype(jnp.bfloat16)
                key_target[slot // 2, :, lanes] = dk[:, here].astype(jnp.bfloat16)
                value_target[slot // 2, :, lanes] = dv[:, here].astype(jnp.bfloat16)

        by_core(table, kept, given, store)


def work(microseconds):
    return int(microseconds * 1.15e9)


def params():
    return pltpu.CompilerParams(vmem_limit_bytes=VMEM_BYTES)


def attention_forward(table, mine, other):
    count, _, row_count = mine.shape
    total = BLOCKS * BLK
    whole = pl.BlockSpec(memory_space=pltpu.VMEM)
    return pl.pallas_call(
        attention_forward_kernel,
        out_shape=(
            jax.ShapeDtypeStruct((count, HD, row_count), jnp.bfloat16),
            jax.ShapeDtypeStruct((HD, 2 * total), jnp.float32),
            jax.ShapeDtypeStruct((1, 2 * total), jnp.float32),
        ),
        in_specs=[pl.BlockSpec(memory_space=pltpu.SMEM), whole, whole],
        out_specs=(whole,) * 3,
        scratch_shapes=[
            pltpu.VMEM((HD, total), jnp.bfloat16),
            pltpu.VMEM((total, HD), jnp.bfloat16),
            pltpu.VMEM((HD, total), jnp.bfloat16),
        ],
        compiler_params=params(),
        cost_estimate=pl.CostEstimate(
            flops=work(36), bytes_accessed=mine.size * 4, transcendentals=total * total // 2
        ),
        name="attention_forward",
    )(table, mine, other)


def attention_backward(table, mine, other, d_out, out_rows, log_sum):
    total = BLOCKS * BLK
    whole = pl.BlockSpec(memory_space=pltpu.VMEM)
    shape = jax.ShapeDtypeStruct(d_out.shape, jnp.bfloat16)
    return pl.pallas_call(
        attention_backward_kernel,
        out_shape=(shape,) * 3,
        in_specs=[pl.BlockSpec(memory_space=pltpu.SMEM)] + [whole] * 5,
        out_specs=(whole,) * 3,
        scratch_shapes=[
            pltpu.VMEM((HD, total), jnp.bfloat16),
            pltpu.VMEM((HD, total), jnp.bfloat16),
            pltpu.VMEM((total, HD), jnp.bfloat16),
            pltpu.VMEM((total, HD), jnp.bfloat16),
            pltpu.VMEM((HD, total), jnp.bfloat16),
            pltpu.VMEM((1, total), jnp.float32),
            pltpu.VMEM((HD, total), jnp.float32),
            pltpu.VMEM((HD, total), jnp.float32),
            pltpu.VMEM((HD, total), jnp.float32),
        ],
        compiler_params=params(),
        cost_estimate=pl.CostEstimate(
            flops=work(58), bytes_accessed=mine.size * 6, transcendentals=total * total // 2
        ),
        name="attention_backward",
    )(table, mine, other, d_out, out_rows, log_sum)


def slot_match(places, rows):
    numbers = lax.broadcasted_iota(jnp.int32, (rows, places.shape[1]), 0).astype(jnp.float32)
    return numbers == places


def both_match(places):
    return jnp.concatenate(
        [
            jnp.where(slot_match(places[e : e + 1, :], CAP), 1.0, 0.0)
            for e in range(places.shape[0])
        ],
        axis=0,
    )


def spread_match(places):
    columns = places.T
    count = places.shape[0] * CAP
    numbers = lax.broadcasted_iota(jnp.int32, (columns.shape[0], count), 1)
    found = numbers < 0
    for e in range(places.shape[0]):
        column = columns[:, e : e + 1]
        found = found | (numbers.astype(jnp.float32) == jnp.where(column < 0, -1.0, column + e * CAP))
    return jnp.where(found, 1.0, 0.0).astype(jnp.bfloat16)


def pick_rows(order, places, sources, picked):
    g = pl.program_id(0)
    for k in range(len(sources) // 2):

        @pl.when(g == k)
        def _(k=k):
            for i in range(2):
                pick = both_match(places[order[2 * k + i]]).astype(jnp.bfloat16)
                rows = nn(pick, sources[2 * k + i][...]).astype(jnp.bfloat16)
                for e in range(places.shape[1]):
                    picked[e, i * CAP : (i + 1) * CAP, :] = rows[e * CAP : (e + 1) * CAP]


def grad_kernel(count, order, places, *refs):
    sources, weights = refs[:count], refs[count]
    slot_rows, d_hidden = refs[-2:]
    pick_rows(order, places, sources, slot_rows)
    for e in range(places.shape[1]):
        d_hidden[e] = nn(slot_rows[e], weights[0, :, e * F : (e + 1) * F]).astype(jnp.bfloat16)


def grad_step(first, order, places, blocks, weights, kept):
    devices, local, row_count = places.shape
    count = len(blocks)
    kept = () if kept is None else tuple(kept)
    whole = pl.BlockSpec((devices, local, row_count), lambda g, order: (0, 0, 0))
    block = pl.BlockSpec((row_count, D), lambda g, order: (0, 0))
    return pl.pallas_call(
        partial(grad_kernel, count),
        grid_spec=pltpu.PrefetchScalarGridSpec(
            num_scalar_prefetch=1,
            grid=(count // 2,),
            in_specs=[
                whole,
                *([block] * count),
                pl.BlockSpec((1, D, local * F), lambda g, order: (2, 0, 0)),
            ]
            + [pl.BlockSpec(memory_space=pl.ANY)] * len(kept),
            out_specs=(
                pl.BlockSpec((local, 2 * CAP, D), lambda g, order: (0, first // 2 + g, 0)),
                pl.BlockSpec((local, 2 * CAP, F), lambda g, order: (0, first // 2 + g, 0)),
            ),
        ),
        out_shape=(
            jax.ShapeDtypeStruct((local, devices * CAP, D), jnp.bfloat16),
            jax.ShapeDtypeStruct((local, devices * CAP, F), jnp.bfloat16),
        ),
        input_output_aliases={count + 3 + i: i for i in range(len(kept))},
        compiler_params=params(),
        cost_estimate=pl.CostEstimate(
            flops=work(2 * count + 2), bytes_accessed=count * row_count * D * 4, transcendentals=0
        ),
        name="grad_step",
    )(order, places, *blocks, weights, *kept)


def expert_kernel(count, order, places, gates, *refs):
    sources, (d_hidden, weights) = refs[:count], refs[count : count + 2]
    slot_rows, hidden, d_gate_pre, d_up, d_gate, near, far, back = refs[-8:]
    g = pl.program_id(0)
    local = places.shape[1]
    pick_rows(order, places, sources, slot_rows)
    here = [slice(e * F, (e + 1) * F) for e in range(local)]
    numbers = [order[2 * g], order[2 * g + 1]]
    picks = [both_match(places[j]) for j in numbers]
    slot_gates = []
    for e in range(local):
        gate_pre = nn(slot_rows[e], weights[0, :, here[e]])
        up_pre = nn(slot_rows[e], weights[1, :, here[e]])
        gate = jnp.concatenate(
            [
                jnp.sum(
                    picks[i][e * CAP : (e + 1) * CAP] * gates[numbers[i]][e : e + 1, :],
                    axis=1,
                    keepdims=True,
                )
                for i in range(2)
            ],
            axis=0,
        )
        raw = d_hidden[e].astype(jnp.float32)
        sig = 1.0 / (1.0 + jnp.exp(-gate_pre))
        silu = gate_pre * sig
        value = silu * up_pre
        hidden[e] = (gate * value).astype(jnp.bfloat16)
        scaled = raw * gate
        d_up[e] = (scaled * silu).astype(jnp.bfloat16)
        d_gate_pre[e] = (scaled * up_pre * sig * (1.0 + gate_pre * (1.0 - sig))).astype(
            jnp.bfloat16
        )
        slot_gates.append(jnp.sum(raw * value, axis=1, keepdims=True))
    for e in range(local):
        back[e] = (
            nt(d_gate_pre[e], weights[0, :, here[e]]) + nt(d_up[e], weights[1, :, here[e]])
        ).astype(jnp.bfloat16)
    results = []
    for i in range(2):
        part = slice(i * CAP, (i + 1) * CAP)
        for e in range(local):
            d_gate[i, e : e + 1, :] = jnp.sum(
                picks[i][e * CAP : (e + 1) * CAP] * slot_gates[e][part], axis=0, keepdims=True
            )
        rows = jnp.concatenate([back[e, part] for e in range(local)], axis=0)
        results.append(nn(spread_match(places[numbers[i]]), rows).astype(jnp.bfloat16))
    if count == 2:
        near[0] = results[0]
        far[0] = results[1]
    else:

        @pl.when(g == 0)
        def _():
            near[0] = results[0]
            near[1] = results[1]

        @pl.when(g == 1)
        def _():
            far[0] = results[0]
            far[1] = results[1]


def expert_step(first, order, places, gates, blocks, d_hidden, weights, kept):
    devices, local, row_count = places.shape
    count = len(blocks)
    half = count // 2
    wide_slots = pl.BlockSpec((local, 2 * CAP, D), lambda g, order: (0, first // 2 + g, 0))
    slots = pl.BlockSpec((local, 2 * CAP, F), lambda g, order: (0, first // 2 + g, 0))
    whole = pl.BlockSpec((devices, local, row_count), lambda g, order: (0, 0, 0))
    block = pl.BlockSpec((row_count, D), lambda g, order: (0, 0))
    sums = pl.BlockSpec((half, row_count, D), lambda g, order: (0, 0, 0))
    kept = () if kept is None else tuple(kept)
    first_kept = 5 + count
    return pl.pallas_call(
        partial(expert_kernel, count),
        grid_spec=pltpu.PrefetchScalarGridSpec(
            num_scalar_prefetch=1,
            grid=(half,),
            in_specs=[
                whole,
                whole,
                *([block] * count),
                slots,
                pl.BlockSpec((2, D, local * F), lambda g, order: (0, 0, 0)),
            ]
            + [pl.BlockSpec(memory_space=pl.ANY)] * len(kept),
            out_specs=(
                wide_slots,
                slots,
                slots,
                slots,
                pl.BlockSpec((2, local, row_count), lambda g, order: (g, 0, 0)),
                sums,
                sums,
            ),
            scratch_shapes=[pltpu.VMEM((local, 2 * CAP, D), jnp.bfloat16)],
        ),
        out_shape=(
            jax.ShapeDtypeStruct((local, devices * CAP, D), jnp.bfloat16),
            jax.ShapeDtypeStruct((local, devices * CAP, F), jnp.bfloat16),
            jax.ShapeDtypeStruct((local, devices * CAP, F), jnp.bfloat16),
            jax.ShapeDtypeStruct((local, devices * CAP, F), jnp.bfloat16),
            jax.ShapeDtypeStruct((count, local, row_count), jnp.float32),
            jax.ShapeDtypeStruct((half, row_count, D), jnp.bfloat16),
            jax.ShapeDtypeStruct((half, row_count, D), jnp.bfloat16),
        ),
        input_output_aliases={first_kept + i: i for i in range(len(kept))},
        compiler_params=params(),
        cost_estimate=pl.CostEstimate(
            flops=work(4 * count + 2),
            bytes_accessed=count * row_count * D * 6,
            transcendentals=count * local * CAP * F,
        ),
        name="expert_step",
    )(order, places, gates, *blocks, d_hidden, weights, *kept)


def output_kernel(order, places, hidden, weights, first_half, second_half):
    rows = jnp.concatenate(
        [
            nt(hidden[e], weights[0, :, e * F : (e + 1) * F]).astype(jnp.bfloat16)
            for e in range(places.shape[1])
        ],
        axis=0,
    )
    total = nn(spread_match(places[0]), rows)
    first_half[...] = total[:, : D // 2].astype(jnp.bfloat16)
    second_half[...] = total[:, D // 2 :].astype(jnp.bfloat16)


def output_pass(order, places, hidden, weights):
    devices, local, row_count = places.shape
    return pl.pallas_call(
        output_kernel,
        grid_spec=pltpu.PrefetchScalarGridSpec(
            num_scalar_prefetch=1,
            grid=(devices,),
            in_specs=[
                pl.BlockSpec((1, local, row_count), lambda j, order: (order[j], 0, 0)),
                pl.BlockSpec((local, CAP, F), lambda j, order: (0, j, 0)),
                pl.BlockSpec((1, D, local * F), lambda j, order: (2, 0, 0)),
            ],
            out_specs=(pl.BlockSpec((row_count, D // 2), lambda j, order: (order[j], 0)),) * 2,
        ),
        out_shape=(jax.ShapeDtypeStruct((devices * row_count, D // 2), jnp.bfloat16),) * 2,
        compiler_params=params(),
        cost_estimate=pl.CostEstimate(
            flops=work(26), bytes_accessed=devices * row_count * D * 3,
            transcendentals=0,
        ),
        name="output_pass",
    )(order, places, hidden, weights)


def weight_grad_kernel(half, slot_rows, slot_grads, d_gate_pre, d_up, hidden, *out):
    out[0][...] = tn(slot_rows[0], d_gate_pre[0]).astype(out[0].dtype)
    out[1][...] = tn(slot_rows[0], d_up[0]).astype(out[1].dtype)
    out[2][...] = tn(slot_grads[0], hidden[0]).astype(out[2].dtype)


def weight_grad(half, slot_rows, slot_grads, d_gate_pre, d_up, hidden, dtype):
    local, count, _ = hidden.shape
    wide_slots = pl.BlockSpec((1, count, D // 2), lambda e, half: (e, 0, half[0]))
    slots = pl.BlockSpec((1, count, F), lambda e, half: (e, 0, 0))
    return pl.pallas_call(
        weight_grad_kernel,
        grid_spec=pltpu.PrefetchScalarGridSpec(
            num_scalar_prefetch=1,
            grid=(local,),
            in_specs=[wide_slots, wide_slots, slots, slots, slots],
            out_specs=(pl.BlockSpec((D // 2, F), lambda e, half: (0, e)),) * 3,
        ),
        out_shape=(jax.ShapeDtypeStruct((D // 2, local * F), dtype),) * 3,
        compiler_params=params(),
        cost_estimate=pl.CostEstimate(
            flops=work(15), bytes_accessed=local * count * D * 8, transcendentals=0
        ),
        name="weight_grad",
    )(half, slot_rows, slot_grads, d_gate_pre, d_up, hidden)


LINE = 4
ROWS = 2
CORES = 2
together = lax.optimization_barrier


def place(z, y, c):
    return (z * ROWS + y) * CORES + c


def move(values, target):
    pairs = []
    for z in range(LINE):
        for y in range(ROWS):
            for c in range(CORES):
                there = target(z, y, c)
                if there is not None and 0 <= there[0] < LINE:
                    pairs.append((place(z, y, c), place(*there)))
    return lax.ppermute(values, "ctx", pairs)


def core_swap(values):
    return move(values, lambda z, y, c: (z, y, 1 - c))


def row_swap(values):
    return move(values, lambda z, y, c: (z, 1 - y, c))


def up_from(values, sources):
    return move(values, lambda z, y, c: (z + 1, y, c) if z in sources else None)


def down_from(values, sources):
    return move(values, lambda z, y, c: (z - 1, y, c) if z in sources else None)


def added(*terms):
    total = terms[0].astype(jnp.float32)
    for term in terms[1:]:
        total = total + term.astype(jnp.float32)
    return total.astype(jnp.bfloat16)


LINE_ORDER = ((0, 1, 2, 3), (1, 2, 3, 0), (2, 1, 0, 3), (3, 2, 1, 0))


def send_on(s, own, up, down):
    sent = []
    if s < LINE:
        sent.append(row_swap(own))
    if s < LINE - 1:
        sent.append(up_from(up, tuple(range(s, LINE - 1))))
        sent.append(down_from(down, tuple(range(1, LINE - s))))
    return sent


def newest(s, ups, downs, z):
    if s < LINE - 1:
        return jnp.where(z >= 2, ups[s], downs[s])
    return jnp.where(
        z == 0, downs[3], jnp.where(z == 1, ups[1], jnp.where(z == 2, downs[1], ups[3]))
    )


def near_order(position):
    z = position // (ROWS * CORES)
    y = position // CORES % ROWS
    c = position % CORES
    line = jnp.asarray(LINE_ORDER, jnp.int32)[z]
    steps = []
    for s in range(LINE + 1):
        for other_core in range(CORES):
            if s < LINE:
                steps.append(place(line[s], y, c ^ other_core))
            if s > 0:
                steps.append(place(line[s - 1], 1 - y, c ^ other_core))
    return jnp.stack(steps).astype(jnp.int32)


def scatter_sum(summed, z, later, beside):
    across_3 = row_swap(summed[4][0])
    across_3, give_2, give_1, give_0, *later = together(
        (across_3, summed[3][1], summed[2][1], summed[1][1], *later)
    )
    part_3 = added(summed[3][0], across_3)
    up_3 = up_from(part_3, (0,))
    down_3 = down_from(part_3, (3,))
    across_2 = row_swap(give_2)
    up_3, down_3, across_2, give_1, give_0, beside = together(
        (up_3, down_3, across_2, give_1, give_0, beside)
    )
    part_2 = added(summed[2][0], across_2)
    up_2 = up_from(added(part_2, up_3), (0, 1))
    down_2 = down_from(added(part_2, down_3), (3, 2))
    across_1 = row_swap(give_1)
    up_2, down_2, across_1, give_0 = together((up_2, down_2, across_1, give_0))
    part_1 = added(summed[1][0], across_1)
    up_1 = up_from(added(jnp.where(z == 2, part_3, part_1), up_2), (0, 1, 2))
    down_1 = down_from(added(jnp.where(z == 1, part_3, part_1), down_2), (1, 2, 3))
    across_0 = row_swap(give_0)
    return [summed[0][0], across_0, up_1, down_1], later, beside


def one_of(values, index, axis):
    return lax.dynamic_index_in_dim(values, index, axis, keepdims=False)


def halves(values, core, axis):
    total = values.shape[axis]
    shape = list(values.shape)
    split = shape[:axis] + [LINE * ROWS * 2, CORES, total // (2 * LINE * ROWS * CORES)]
    values = values.reshape(split + shape[axis + 1 :])
    shape[axis] = total // CORES
    return tuple(
        one_of(values, which, axis + 1).reshape(shape) for which in (core, 1 - core)
    )


def by_side(values):
    spots = LINE * ROWS
    return values.reshape(2, spots, values.shape[0] // (2 * spots), values.shape[1])


def side_sum(values, side):
    return added(one_of(values, side, 0), exchange(one_of(values, 1 - side, 0)))


def owner_last(values):
    groups = [[spot * CORES + core for spot in range(LINE * ROWS)] for core in range(CORES)]
    values = lax.all_to_all(
        values, "ctx", split_axis=0, concat_axis=0, tiled=True, axis_index_groups=groups
    )
    return jnp.sum(values.astype(jnp.float32), axis=0)


def exchange(values):
    return lax.ppermute(values, "dp", [(0, 1), (1, 0)])


def to_heads(values):
    return lax.all_to_all(values, "ctx", split_axis=0, concat_axis=0, tiled=True)


def turn(values, cosine, sine):
    half = HD // 2
    first, second = values[:, :half, :], values[:, half:, :]
    return jnp.concatenate(
        [first * cosine - second * sine, second * cosine + first * sine], axis=1
    )


def per_device(
    tokens, grad_out, w_query, w_key, w_value, w_output, gain_attn, gain_ffn, w_router, w_experts,
    deal_table, routes
):
    row_count = tokens.shape[0]
    devices = lax.axis_size("ctx")
    position = lax.axis_index("ctx")
    side = lax.axis_index("dp")
    both = ("dp", "ctx")
    shard = w_query.shape[0]
    wide = HQ * HD
    narrow = KVH * HD

    extras = jnp.concatenate(
        [w_router, gain_attn[:, None], gain_ffn[:, None], jnp.zeros((shard, 94), jnp.bfloat16)],
        axis=1,
    )
    packed_weights = lax.all_gather(
        jnp.concatenate([w_query, w_key, w_value, extras], axis=1), both, axis=0, tiled=True
    )
    other_experts = exchange(w_experts)
    local = w_experts.shape[2] // F
    line_place = position // (ROWS * CORES)
    order = near_order(position)

    g_ups, g_downs, g_across, g_own = [grad_out], [grad_out], [], [grad_out]
    for s in range(3):
        sent = send_on(s, g_own[s], g_ups[s], g_downs[s])
        if s == 1:
            packed_weights, *sent = together((packed_weights, *sent))
        elif s == 0:
            sent = together(tuple(sent))
        else:
            step_2 = sent
        g_across.append(sent[0])
        g_ups.append(sent[1])
        g_downs.append(sent[2])
        g_own.append(newest(s + 1, g_ups, g_downs, line_place))

    full_qkv = packed_weights[:, : wide + 2 * narrow]
    extra_columns = packed_weights[:, wide + 2 * narrow :]
    full_router = extra_columns[:, :E]
    gain_attn_full = extra_columns[:, E].astype(jnp.float32)
    gain_ffn_full = extra_columns[:, E + 1].astype(jnp.float32)

    expert_ids = jnp.arange(E, dtype=jnp.int32)
    picked = routes[:, :, None] == expert_ids[None, None, :]
    member = jnp.any(picked, axis=1)
    below = (jnp.arange(row_count)[:, None] > jnp.arange(row_count)[None, :]).astype(jnp.bfloat16)
    before = nn(below, member.astype(jnp.bfloat16))
    places = jnp.where(member, before, -1.0)
    slot_places = to_heads(places.T.reshape(devices, local, row_count))

    group_blocks = deal_table[0]
    own_blocks = lax.dynamic_slice_in_dim(group_blocks, 2 * position, 2)
    offsets = jnp.arange(BLK, dtype=jnp.int32)
    positions = ((own_blocks % BLOCKS)[:, None] * BLK + offsets[None, :]).reshape(-1)
    core = position % CORES
    table = jnp.concatenate([jnp.argsort(group_blocks).astype(jnp.int32), core.reshape(1)])
    frequency = 10000.0 ** (-(jnp.arange(HD // 2).astype(jnp.float32) * 2.0 / HD))
    angles = frequency[:, None] * positions.astype(jnp.float32)[None, :]
    cosine, sine = jnp.cos(angles)[None], jnp.sin(angles)[None]
    inputs = tokens.astype(jnp.float32)
    normed = rms_norm(inputs, gain_attn_full).astype(jnp.bfloat16)
    normed_near, normed_far = halves(normed, core, 1)
    raw = tt(full_qkv, normed)
    queries = turn(raw[:wide].reshape(HQ, HD, row_count), cosine, sine).astype(jnp.bfloat16)
    keys = turn(raw[wide : wide + narrow].reshape(KVH, HD, row_count), cosine, sine).astype(
        jnp.bfloat16
    )
    values = raw[wide + narrow :].reshape(KVH, HD, row_count).astype(jnp.bfloat16)
    pairs = jnp.stack([keys, values], axis=1).reshape(HQ, HD, row_count)
    outgoing = jnp.concatenate([queries, pairs], axis=1)
    outgoing, other_experts, slot_places, w_output, *step_2 = together(
        (outgoing, other_experts, slot_places, w_output, *step_2)
    )
    full_output = lax.all_gather(w_output, both, axis=0, tiled=True)
    packed = to_heads(outgoing)
    g_across[2], g_ups[3], g_downs[3] = step_2
    g_own[3] = newest(3, g_ups, g_downs, line_place)
    first_half = jnp.where(side == 0, w_experts, other_experts)
    second_half = jnp.where(side == 0, other_experts, w_experts)
    experts = jnp.concatenate([first_half, second_half], axis=1)
    g_kept, g_first = None, 0
    for s in range(LINE + 1):
        if s == LINE:
            packed, g_own[3], *g_kept = together((packed, g_own[3], *g_kept))
            other_packed = core_swap(packed)
            g_across.append(row_swap(g_own[3]))
            heads, attended_rows, log_sum = attention_forward(table, packed, other_packed)
            heads, g_across[3] = together((heads, g_across[3]))
            attended = to_heads(heads)
        blocks = g_own[s : s + 1] + (g_across[s - 1 : s] if s else [])
        blocks += [core_swap(b) for b in blocks]
        count = len(blocks)
        g_kept = grad_step(
            g_first, order[g_first : g_first + count], slot_places, blocks, experts, g_kept
        )
        g_first += count
    attended, *g_kept = together((attended, *g_kept))
    attended = attended.reshape(wide, row_count)
    slot_grads, d_hidden = g_kept
    residual = inputs + tn(attended, full_output)

    normed_ffn = rms_norm(residual, gain_ffn_full).astype(jnp.bfloat16)
    logits = nn(normed_ffn, full_router)
    masked = jnp.where(member, logits, floor_value)
    powers = jnp.where(member, jnp.exp(masked - jnp.max(masked, axis=1, keepdims=True)), 0.0)
    gates = powers / jnp.sum(powers, axis=1, keepdims=True)
    swapped = core_swap(normed_ffn)
    gates_out, swapped = together((gates.T.reshape(devices, local, row_count), swapped))
    slot_gates = to_heads(gates_out)
    summed, d_gate_parts, kept = [], [], None
    own, across = normed_ffn, None
    ups, downs = [normed_ffn], [normed_ffn]
    first = 0
    for s in range(LINE + 1):
        blocks = [b for b in (own, across) if b is not None]
        sent = send_on(s, own, ups[-1], downs[-1])
        blocks += [core_swap(b) for b in blocks] if s else [swapped]
        count = len(blocks)
        *kept, d_gate_part, near_part, far_part = expert_step(
            first, order[first : first + count], slot_places, slot_gates, blocks, d_hidden,
            experts, kept
        )
        if sent and summed:
            *sent, near_part, summed[-1] = together((*sent, near_part, summed[-1]))
        elif sent:
            *sent, near_part = together((*sent, near_part))
        first += count
        summed.append(added(near_part, core_swap(far_part)))
        d_gate_parts.append(d_gate_part)
        across = sent[0] if s < LINE else None
        if s < LINE - 1:
            ups.append(sent[1])
            downs.append(sent[2])
        own = newest(s + 1, ups, downs, line_place) if s < LINE - 1 else None
    slot_rows, hidden, d_gate_pre, d_up = kept
    out_rows, late_rows = output_pass(order, slot_places, hidden, experts)
    arrived, d_gate_parts, out_rows = scatter_sum(summed, line_place, d_gate_parts, out_rows)
    mixture = lax.psum_scatter(out_rows, "ctx", scatter_dimension=0, tiled=True)
    given = weight_grad(
        (1 - side).reshape(1), slot_rows, slot_grads, d_gate_pre, d_up, hidden, jnp.bfloat16
    )
    taken = [exchange(part) for part in given]
    owned_experts = weight_grad(
        side.reshape(1), slot_rows, slot_grads, d_gate_pre, d_up, hidden, jnp.float32
    )
    back = jnp.argsort(order)
    d_gate = to_heads(jnp.concatenate(d_gate_parts, axis=0)[back])
    *arrived, taken[0], taken[1], owned_experts, d_gate = together(
        (*arrived, taken[0], taken[1], owned_experts, d_gate)
    )
    d_gate = d_gate.reshape(E, row_count).T
    ffn_grad = sum(part.astype(jnp.float32) for part in arrived)

    d_logits = gates * (d_gate - jnp.sum(gates * d_gate, axis=1, keepdims=True))
    ffn_grad = ffn_grad + jnp.einsum(
        "re,de->rd", d_logits, full_router.astype(jnp.float32), precision=highest
    )
    router_grad = jnp.einsum(
        "rd,re->de", normed_ffn.astype(jnp.float32), d_logits, precision=highest
    )
    _, norm_back_ffn = jax.vjp(rms_norm, residual, gain_ffn_full)
    residual_norm_grad, gain_ffn_grad = norm_back_ffn(ffn_grad)
    residual_grad = grad_out.astype(jnp.float32) + residual_norm_grad
    branch_grad = residual_grad.astype(jnp.bfloat16)
    attended_grad = nt(full_output, branch_grad).astype(jnp.bfloat16)
    d_heads = to_heads(attended_grad.reshape(HQ, HD, row_count))
    output_grad = jnp.concatenate(
        [
            nn(attended, branch_grad).astype(jnp.bfloat16),
            router_grad.astype(jnp.bfloat16),
            gain_ffn_grad[:, None].astype(jnp.bfloat16),
            jnp.zeros((D, 95), jnp.bfloat16),
        ],
        axis=1,
    )
    first_near, first_far = halves(output_grad, core, 0)
    first_parts = by_side(added(first_near, core_swap(first_far)))
    d_heads, first_parts, late_rows = together((d_heads, first_parts, late_rows))
    late_mixture = lax.psum_scatter(late_rows, "ctx", scatter_dimension=0, tiled=True)
    first_taken = exchange(one_of(first_parts, 1 - side, 0))

    q_grads, kept_grads, given_grads = attention_backward(
        table, packed, other_packed, d_heads, attended_rows, log_sum
    )
    q_grads, first_taken, taken[2] = together((q_grads, first_taken, taken[2]))
    q_back = to_heads(q_grads)
    pair_grads = added(kept_grads, core_swap(given_grads))
    q_back, pair_grads = together((q_back, pair_grads))
    pair_back = to_heads(pair_grads)
    d_query = (
        turn(q_back.astype(jnp.float32), cosine, -sine)
        .astype(jnp.bfloat16)
        .reshape(wide, row_count)
    )
    far_grad = core_swap(tt(normed_far, d_query).astype(jnp.bfloat16))
    near_grad = tt(normed_near, d_query).astype(jnp.bfloat16)
    query_parts = side_sum(by_side(added(near_grad, far_grad)), side)
    query_parts = jnp.concatenate(
        [query_parts, added(one_of(first_parts, side, 0), first_taken)], axis=2
    )
    pairs = pair_back.astype(jnp.float32).reshape(KVH, 2, HD, row_count)
    d_pairs = jnp.concatenate(
        [
            turn(pairs[:, 0], cosine, -sine).astype(jnp.bfloat16),
            pairs[:, 1].astype(jnp.bfloat16),
        ],
        axis=0,
    ).reshape(2 * narrow, row_count)
    far_grad, query_parts = together((tt(normed_far, d_pairs).astype(jnp.bfloat16), query_parts))
    far_grad = core_swap(far_grad)
    query_owned = owner_last(query_parts)
    near_grad = tt(normed_near, d_pairs).astype(jnp.bfloat16)
    normed_grad = tt(d_query, full_qkv[:, :wide]) + tt(d_pairs, full_qkv[:, wide:])
    _, norm_back_attn = jax.vjp(rms_norm, inputs, gain_attn_full)
    input_norm_grad, gain_attn_grad = norm_back_attn(normed_grad)
    gain_near, gain_far = halves(gain_attn_grad[:, None].astype(jnp.bfloat16), core, 0)
    pair_parts = by_side(added(near_grad, far_grad))
    given_pairs = exchange(one_of(pair_parts, 1 - side, 0))
    gain_parts = by_side(added(gain_near, core_swap(gain_far)))
    given_gain = exchange(one_of(gain_parts, 1 - side, 0))
    tokens_grad = residual_grad + input_norm_grad
    given_pairs, given_gain, tokens_grad = together((given_pairs, given_gain, tokens_grad))
    gain_parts = added(one_of(gain_parts, side, 0), given_gain)
    pair_owned = owner_last(
        jnp.concatenate(
            [
                added(one_of(pair_parts, side, 0), given_pairs),
                gain_parts,
                jnp.zeros((*gain_parts.shape[:2], 127), jnp.bfloat16),
            ],
            axis=2,
        )
    )
    mixture = jnp.concatenate([mixture, late_mixture], axis=1)
    mixed = (residual + mixture.astype(jnp.float32)).astype(jnp.bfloat16)
    expert_grad = jnp.stack(
        [mine + part.astype(jnp.float32) for mine, part in zip(owned_experts, taken)]
    )
    return (
        mixed,
        tokens_grad,
        query_owned[:, :wide],
        pair_owned[:, :narrow],
        pair_owned[:, narrow : 2 * narrow],
        query_owned[:, wide : wide + D],
        pair_owned[:, 2 * narrow],
        query_owned[:, wide + D + E],
        query_owned[:, wide + D : wide + D + E],
        expert_grad,
    )


def solution(mesh):
    in_specs = (
        P(("dp", "ctx"), None),
        P(("dp", "ctx"), None),
        P(("dp", "ctx"), None),
        P(("dp", "ctx"), None),
        P(("dp", "ctx"), None),
        P(("dp", "ctx"), None),
        P(("dp", "ctx")),
        P(("dp", "ctx")),
        P(("dp", "ctx"), None),
        P(None, "dp", "ctx"),
        P("dp", None),
        P(("dp", "ctx"), None),
    )
    out_specs = (
        P(("dp", "ctx"), None),
        P(("dp", "ctx"), None),
        P(("dp", "ctx"), None),
        P(("dp", "ctx"), None),
        P(("dp", "ctx"), None),
        P(("dp", "ctx"), None),
        P(("dp", "ctx")),
        P(("dp", "ctx")),
        P(("dp", "ctx"), None),
        P(None, "dp", "ctx"),
    )
    body = per_device if mesh.shape["ctx"] == HQ else general_device
    return jax.shard_map(
        body, mesh=mesh, in_specs=in_specs, out_specs=out_specs, check_vma=False
    )
```
